256 devices in a mesh: dp: 16 (over x, y_hi, core), blk: 16 (over y_lo, z).
Axes of the slice: x: 4, y: 4 (y_hi: 2, y_lo: 2; y = y_hi * 2 + y_lo), z: 8, core: 2. Of those that a mesh axis runs over, the one named last changes fastest.
Arguments:
- queries: bfloat16 [16, 2048, 4096], P('dp', 'blk'), may hold values from -24 to 24
- response_key_rows: bfloat16 [16, 2048, 512], P('dp', 'blk'), may hold values from -6 to 6
- response_value_rows: bfloat16 [16, 2048, 512], P('dp', 'blk'), may hold values from -6 to 6
- prompt_keys: bfloat16 [16, 1024, 512], P('dp', 'blk'), may hold values from -24 to 24
- prompt_value_rows: bfloat16 [16, 1024, 512], P('dp', 'blk'), may hold values from -6 to 6
- output_gradient: bfloat16 [16, 2048, 4096], P('dp', 'blk'), may hold values from -256 to 256
- prompt_owner: int32 [16], replicated, may hold values from 0 to 15, each once
- response_prompt: int32 [16], replicated, may hold values from 0 to 15
- lengths: int32 [16], replicated, may hold values from 1 to 2048, 17408 in all
- half_blocks: int32 [32], replicated, may hold values from 0 to 31, each once
Outputs:
- attn_out: bfloat16 [16, 2048, 4096], P('dp', 'blk')
- prompt_key_grad: float32 [16, 1024, 512], P('dp', 'blk')
- prompt_value_grad: float32 [16, 1024, 512], P('dp', 'blk')
The draws below stay inside these ranges and needn't reach their ends.
Inputs may be any that keep to these rules, and one draw needn't show every extreme that they name: `prompt_owner`: A permutation of the owner rows. `response_prompt`: several responses may share a prompt; some prompts have none. `lengths`: some response has the full length 2048. `half_blocks`: A permutation of the 2 * 16 position blocks.
All inputs are finite; a program needn't handle non-finite values.
Results may differ from the reference program's by a relative error of at most 0.006.
Values may be sent and summed in bfloat16 or wider, within the bound.
A program may use at most 192 MiB of HBM per device.

```python
import math
import jax
import jax.numpy as jnp
import numpy as np
from jax import lax

QUERY_HEADS = 32
KEY_VALUE_HEADS = 4
HEAD_WIDTH = 128
R_DEV = 128
RESPONSE_LENGTH = 2048
PROMPT_LENGTH = 1024
PROMPT_COUNT = 16
RESPONSE_COUNT = 16
N_BLK = 16


def draw_queries(key, part):
    key = jax.random.fold_in(key, 5)
    value_rows = jnp.clip(jax.random.normal(key, (RESPONSE_COUNT, RESPONSE_LENGTH, QUERY_HEADS * HEAD_WIDTH), jnp.float32), -6.0, 6.0)
    return value_rows.astype(jnp.bfloat16)


def draw_prompt_keys(key, part):
    key = jax.random.fold_in(key, 7)
    first_part = jax.random.fold_in(key, 0)
    value_rows = jnp.clip(jax.random.normal(first_part, (PROMPT_COUNT, PROMPT_LENGTH, KEY_VALUE_HEADS * HEAD_WIDTH), jnp.float32), -6.0, 6.0)
    return value_rows.astype(jnp.bfloat16)


def touch_ends(array, rng, low, high):
    longest = array.shape.index(max(array.shape))
    spots = []
    for shift in (0, 1):
        where = [jax.random.randint(jax.random.fold_in(rng, axis), (), 0, length) for axis, length in enumerate(array.shape)]
        where[longest] = (where[longest] + shift) % array.shape[longest]
        spots.append(tuple(where))
    return array.at[spots[0]].set(low).at[spots[1]].set(high)


def shard_levels(own_key, dims, cuts, low, high):
    def one(position, parts):
        steps = jax.random.uniform(jax.random.fold_in(jax.random.fold_in(own_key, 6), position), (parts,), jnp.float32, low / len(cuts), high / len(cuts))
        return jnp.repeat(jnp.exp(steps), dims[position] // parts).reshape((-1,) + (1,) * (len(dims) - position - 1))

    gain = one(*cuts[0])
    for cut in cuts[1:]:
        gain = gain * one(*cut)
    return gain


def rank_table(number_of, lean):
    portions = [(1 << 20) // math.isqrt(standing ** lean) + 1 for standing in range(1, number_of + 1)]
    scale = 1 + sum(portions) // (1 << 30)
    return np.cumsum(np.array([max(1, weight // scale) for weight in portions]))


def skewed_ids(own_key, extent, count, skew):
    listing = rank_table(count, skew)
    pick = jax.random.randint(jax.random.fold_in(own_key, 1), extent, 0, int(listing[count - 1]))
    standing = jnp.searchsorted(jnp.asarray(listing, jnp.int32), pick, side="right")
    return jax.random.permutation(jax.random.fold_in(own_key, 2), count)[standing].astype(jnp.int32)


def length_profile(amount, total, most, lean):
    weights = [(1 << 20) // math.isqrt(standing ** lean) + 1 for standing in range(2, amount + 1)]
    surplus, holding = total - most - (amount - 1), [1] * (amount - 1)
    while surplus > 0:
        free = [i for i in range(amount - 1) if holding[i] < most]
        pool, left = sum([weights[i] for i in free]), surplus
        for i in free:
            extra = min(most - holding[i], max(1, left * weights[i] // pool), surplus)
            holding[i] = holding[i] + extra
            surplus = surplus - extra
    return np.array([most] + holding)


def uneven_parts(own_key, amount, total, limit, slope):
    if amount == 2:
        one = jax.random.randint(own_key, (), max(1, total - limit), min(limit, total - 1) + 1)
        return jnp.stack([one, total - one])
    sizes = jnp.asarray(length_profile(amount, total, limit, slope), jnp.int32)
    twos = (amount - 1) // 2
    giver, sink = sizes[1:1 + 2 * twos:2], sizes[2:2 + 2 * twos:2]
    slack = jnp.minimum(giver - 1, limit - sink)
    passed = jax.random.randint(jax.random.fold_in(own_key, 1), (twos,), 0, 1 << 20) % (slack + 1)
    sizes = sizes.at[1:1 + 2 * twos:2].set(giver - passed).at[2:2 + 2 * twos:2].set(sink + passed)
    return sizes[jax.random.permutation(jax.random.fold_in(own_key, 2), amount)]


def gaussian(rng, shape, scale, reach, shards=(), kind=jnp.bfloat16):
    result = scale * jax.random.normal(rng, shape, jnp.float32)
    if shards:
        result = result * shard_levels(rng, shape, shards, -0.22, 0.18)
    return jnp.clip(result, -reach, reach).astype(kind)


def setup_inputs(seed: int = 0) -> dict:
    arg_keys = jax.random.split(jax.random.key(seed), 11)
    queries = draw_queries(jax.random.fold_in(arg_keys[10], 71), 0)
    response_key_rows = gaussian(arg_keys[1], (RESPONSE_COUNT, RESPONSE_LENGTH, KEY_VALUE_HEADS * HEAD_WIDTH), 1.0, 6.0, ((0, 16), (1, 16)))
    response_value_rows = gaussian(arg_keys[2], (RESPONSE_COUNT, RESPONSE_LENGTH, KEY_VALUE_HEADS * HEAD_WIDTH), 1.0, 6.0, ((0, 16), (1, 16)))
    prompt_keys = draw_prompt_keys(jax.random.fold_in(arg_keys[10], 71), 0)
    prompt_value_rows = gaussian(arg_keys[4], (PROMPT_COUNT, PROMPT_LENGTH, KEY_VALUE_HEADS * HEAD_WIDTH), 1.0, 6.0, ((0, 16), (1, 16)))
    output_gradient = gaussian(arg_keys[5], (RESPONSE_COUNT, RESPONSE_LENGTH, QUERY_HEADS * HEAD_WIDTH), ((PROMPT_LENGTH + RESPONSE_LENGTH // 2) * RESPONSE_LENGTH ** -0.5), 256.0, ((0, 16), (1, 16)))
    prompt_owner = jax.random.permutation(arg_keys[6], PROMPT_COUNT).astype(jnp.int32)
    response_prompt = touch_ends(skewed_ids(arg_keys[7], (RESPONSE_COUNT,), PROMPT_COUNT, 2), jax.random.fold_in(arg_keys[7], 3), 0, PROMPT_COUNT - 1).astype(jnp.int32)
    lengths = uneven_parts(arg_keys[8], RESPONSE_COUNT, RESPONSE_LENGTH * (RESPONSE_COUNT + 1) // 2, RESPONSE_LENGTH, 2).astype(jnp.int32)
    half_blocks = jax.random.permutation(arg_keys[9], 2 * N_BLK).astype(jnp.int32)
    return dict(queries=queries, response_key_rows=response_key_rows, response_value_rows=response_value_rows, prompt_keys=prompt_keys, prompt_value_rows=prompt_value_rows, output_gradient=output_gradient, prompt_owner=prompt_owner, response_prompt=response_prompt, lengths=lengths, half_blocks=half_blocks)


NEGATIVE_LIMIT = -1.0e30
EXACT = lax.Precision.HIGHEST


def positions(half_blocks, half_rows, total_rows):
    index = jnp.arange(total_rows, dtype=jnp.int32)
    return half_blocks[index // half_rows] * half_rows + index % half_rows


def rounded(input_array):
    narrow = lax.optimization_barrier(input_array.astype(jnp.bfloat16))
    return narrow.astype(jnp.float32)


def head_terms(query_rows, keys_prompt, values_prompt, keys_resp, values_resp, output_cotangent, visible):
    scale = HEAD_WIDTH ** -0.5
    scores_prompt = jnp.einsum('grd,kd->grk', query_rows, keys_prompt, precision=EXACT) * scale
    scores_resp = jnp.einsum('grd,kd->grk', query_rows, keys_resp, precision=EXACT) * scale
    scores_resp = jnp.where(visible[None], scores_resp, NEGATIVE_LIMIT)
    peak = jnp.maximum(jnp.max(scores_prompt, -1), jnp.max(scores_resp, -1))
    weights_prompt = jnp.exp(scores_prompt - peak[..., None])
    weights_resp = jnp.where(visible[None], jnp.exp(scores_resp - peak[..., None]), 0.0)
    total = jnp.sum(weights_prompt, -1) + jnp.sum(weights_resp, -1)
    mixed = jnp.einsum('grk,kd->grd', rounded(weights_prompt), values_prompt, precision=EXACT)
    mixed = mixed + jnp.einsum('grk,kd->grd', rounded(weights_resp), values_resp, precision=EXACT)
    output = mixed / total[..., None]
    log_total = peak + jnp.log(total)
    delta = jnp.sum(output_cotangent * output, -1)
    probs = jnp.exp(scores_prompt - log_total[..., None])
    value_gradient = jnp.einsum('grk,grd->kd', rounded(probs), output_cotangent, precision=EXACT)
    back = jnp.einsum('grd,kd->grk', output_cotangent, values_prompt, precision=EXACT)
    slopes = probs * (back - delta[..., None])
    key_gradient = jnp.einsum('grk,grd->kd', slopes, query_rows, precision=EXACT) * scale
    return output, key_gradient, value_gradient


def reference(queries, response_key_rows, response_value_rows, prompt_keys, prompt_value_rows, output_gradient, prompt_owner, response_prompt, lengths, half_blocks):
    head_group = QUERY_HEADS // KEY_VALUE_HEADS
    where_rows = positions(half_blocks, R_DEV // 2, RESPONSE_LENGTH)

    def by_query_head(input_array):
        return input_array.astype(jnp.float32).reshape(RESPONSE_LENGTH, KEY_VALUE_HEADS, head_group, HEAD_WIDTH).transpose(1, 2, 0, 3)

    def by_key_head(input_array, item_count):
        return input_array.astype(jnp.float32).reshape(item_count, KEY_VALUE_HEADS, HEAD_WIDTH).transpose(1, 0, 2)

    def one_response(carry, index):
        key_gradient_sum, value_gradient_sum = carry
        owned_row_index = prompt_owner[response_prompt[index]]
        visible = (where_rows[None, :] <= where_rows[:, None]) & (where_rows[None, :] < lengths[index])
        inputs = (by_query_head(queries[index]), by_key_head(prompt_keys[owned_row_index], PROMPT_LENGTH),
                  by_key_head(prompt_value_rows[owned_row_index], PROMPT_LENGTH), by_key_head(response_key_rows[index], RESPONSE_LENGTH),
                  by_key_head(response_value_rows[index], RESPONSE_LENGTH), by_query_head(output_gradient[index]))
        output, key_gradient, value_gradient = lax.map(lambda items: head_terms(*items, visible), inputs)
        output = output.transpose(2, 0, 1, 3).reshape(RESPONSE_LENGTH, QUERY_HEADS * HEAD_WIDTH).astype(jnp.bfloat16)
        key_gradient_sum = key_gradient_sum.at[owned_row_index].add(key_gradient.transpose(1, 0, 2).reshape(PROMPT_LENGTH, KEY_VALUE_HEADS * HEAD_WIDTH))
        value_gradient_sum = value_gradient_sum.at[owned_row_index].add(value_gradient.transpose(1, 0, 2).reshape(PROMPT_LENGTH, KEY_VALUE_HEADS * HEAD_WIDTH))
        return (key_gradient_sum, value_gradient_sum), output

    zero_filled = jnp.zeros((PROMPT_COUNT, PROMPT_LENGTH, KEY_VALUE_HEADS * HEAD_WIDTH), jnp.float32)
    totals, outputs = lax.scan(one_response, (zero_filled, zero_filled), jnp.arange(RESPONSE_COUNT, dtype=jnp.int32))
    return outputs, totals[0], totals[1]
```

```python
import jax
import jax.numpy as jnp
from jax import lax
from jax.experimental import pallas as pl
from jax.experimental.pallas import tpu as pltpu
from jax.sharding import PartitionSpec as P

MESH = pl.DeviceIdType.MESH
HEAD_WIDTH = 128
SCALE = HEAD_WIDTH ** (-0.5)
LOG2E = 1.4426950408889634
SCORE_SCALE = SCALE * LOG2E
MASKED = -1e30
LOWEST = -1e20
BF = jnp.bfloat16
F32 = jnp.float32

X, YH, CORES, YL, Z = 4, 2, 2, 2, 8
GROUP = 8
ROWS = 128
PROWS = 64
HALF_KV = 256
HALF_Q = 2048


def nt(a, b):
    return lax.dot_general(a, b, (((1,), (1,)), ((), ())), preferred_element_type=F32)


def nn(a, b):
    return lax.dot_general(a, b, (((1,), (0,)), ((), ())), preferred_element_type=F32)


def tn(a, b):
    return lax.dot_general(a, b, (((0,), (0,)), ((), ())), preferred_element_type=F32)


def kernel(
    q_ref, rk_ref, rv_ref, pk_ref, pv_ref, do_ref, owner_ref, prompt_ref, length_ref, half_ref,
    out_ref, gk_ref, gv_ref,
    q_far, do_far, out_far, resp, xbuf, hp_out, hp_in, prompt,
    m_ref, l_ref, acc_ref, lse_ref, delta_ref, gacc,
    zs_out, zs_in, share, yh_in, core_in, xs_out, xs_in, y_out, y_in, xsum,
    send_sem, recv_sem,
):
    dp = lax.axis_index("dp")
    blk = lax.axis_index("blk")
    x, yh, c = dp // 4, (dp // 2) % 2, dp % 2
    yl, z = blk // Z, blk % Z
    other = 1 - yl
    y_id = (dp, other * Z + z)
    z_right, z_left = (dp, yl * Z + (z + 1) % Z), (dp, yl * Z + (z + Z - 1) % Z)
    x_right = (((x + 1) % X) * 4 + yh * 2 + c, blk)
    x_left = (((x + X - 1) % X) * 4 + yh * 2 + c, blk)
    core_id = (x * 4 + yh * 2 + (1 - c), blk)
    yh_id = (x * 4 + (1 - yh) * 2 + c, blk)

    barrier = pltpu.get_barrier_semaphore()
    peers = (y_id, z_right, z_left, x_right, x_left, core_id, yh_id)
    for peer in peers:
        pl.semaphore_signal(barrier, inc=1, device_id=peer, device_id_type=MESH)
    pl.semaphore_wait(barrier, len(peers))

    started = []

    def send(src, dst, peer):
        index = len(started)
        copy = pltpu.make_async_remote_copy(
            src_ref=src, dst_ref=dst, send_sem=send_sem.at[index], recv_sem=recv_sem.at[index],
            device_id=peer, device_id_type=MESH,
        )
        copy.start()
        started.append(copy)
        return copy

    def arrive(copies):
        for copy in copies:
            copy.wait_recv()

    def lanes(which, width):
        return pl.ds(pl.multiple_of(which * width, width), width)

    mine_kv, far_kv = lanes(yl, HALF_KV), lanes(other, HALF_KV)
    mine_q, far_q = lanes(yl, HALF_Q), lanes(other, HALF_Q)

    y_prompt = [
        send(ref.at[0, :, far_kv], xbuf.at[x, c, kv, yl], y_id)
        for kv, ref in enumerate((pk_ref, pv_ref))
    ]
    y_resp = [
        send(ref.at[0, :, far_kv], resp.at[z, kv, yl], y_id)
        for kv, ref in enumerate((rk_ref, rv_ref))
    ]
    y_q = send(q_ref.at[0, :, far_q], q_far, y_id)
    for kv, ref in enumerate((pk_ref, pv_ref)):
        xbuf[x, c, kv, yl] = ref[0, :, mine_kv]
    for kv, ref in enumerate((rk_ref, rv_ref)):
        resp[z, kv, yl] = ref[0, :, mine_kv]

    def gather_step(slot, pos, n, step, right, left):
        halves_right, halves_left = ((0, 1), (0, 1)) if step < n // 2 - 1 else ((0,), (1,))
        from_slot = (pos + n - step) % n
        copies = [send(slot(from_slot, h), slot(from_slot, h), right) for h in halves_right]
        from_slot = (pos + step) % n
        copies += [send(slot(from_slot, h), slot(from_slot, h), left) for h in halves_left]
        return copies

    def x_slot(i, h):
        return xbuf.at[i, c, h]

    def core_send(i):
        return send(xbuf.at[i, c], xbuf.at[i, c], core_id)

    def resp_slot(i, h):
        return resp.at[i, h]

    def prompt_slot(i, h):
        return prompt.at[i, h]

    lane = lax.broadcasted_iota(jnp.int32, (1, 2 * ROWS), 1)
    last = length_ref[dp] - 1
    limit = jnp.zeros((1, 2 * ROWS), jnp.int32)
    for part, holder in enumerate((blk, other * Z + z)):
        for e in range(2):
            block = part * 2 + e
            inside = (lane >= block * 64) & (lane < block * 64 + 64)
            limit = jnp.where(inside, half_ref[2 * holder + e] * 64 + lane - block * 64, limit)
    limit = jnp.minimum(limit, last)
    down = lax.broadcasted_iota(jnp.int32, (64, 2 * ROWS), 0)

    def head_of(ref, far, h):
        near = ref[0, :, pl.ds(pl.multiple_of(yl * HALF_Q + h * 128, 128), 128)]
        return jnp.concatenate([near, far[:, pl.ds(pl.multiple_of(h * 128, 128), 128)]], axis=0)

    def keys_of(buf, slots, kv, a, rows):
        return jnp.concatenate(
            [buf[i, kv, :, :, a * 128 : (a + 1) * 128].reshape(2 * rows, 128) for i in slots], axis=0
        )

    def absorb(buf, slots, rows, masked):
        bounds = []
        if masked:
            for i in slots:
                for y in range(2):
                    for e in range(2):
                        bounds.append(limit - half_ref[2 * (y * Z + i) + e] * 64)

        def body(g, carry):
            for a in range(2):
                h = a * GROUP + g
                query = head_of(q_ref, q_far, h)
                scores = nt(keys_of(buf, slots, 0, a, rows), query) * SCORE_SCALE
                if masked:
                    scores = jnp.concatenate(
                        [
                            jnp.where(down <= bound, scores[64 * n : 64 * n + 64], MASKED)
                            for n, bound in enumerate(bounds)
                        ],
                        axis=0,
                    )
                old = m_ref[h]
                peak = jnp.maximum(old, jnp.max(scores, axis=0, keepdims=True))
                weights = jnp.exp2(scores - peak)
                factor = jnp.exp2(old - peak)
                m_ref[h] = peak
                l_ref[h] = l_ref[h] * factor + jnp.sum(weights, axis=0, keepdims=True)
                acc_ref[h] = acc_ref[h] * factor + tn(
                    keys_of(buf, slots, 1, a, rows), weights.astype(BF)
                )
            return carry

        lax.fori_loop(0, GROUP, body, 0)

    m_ref[...] = jnp.full(m_ref.shape, LOWEST, F32)
    l_ref[...] = jnp.zeros(l_ref.shape, F32)
    acc_ref[...] = jnp.zeros(acc_ref.shape, F32)

    arrive(y_prompt)
    x0 = gather_step(x_slot, x, X, 0, x_right, x_left)
    cores = [core_send(x)]
    arrive(y_resp)
    r0 = gather_step(resp_slot, z, Z, 0, z_right, z_left)
    arrive(x0)
    x1 = gather_step(x_slot, x, X, 1, x_right, x_left)
    cores += [core_send((x + 1) % X), core_send((x + X - 1) % X)]
    arrive(x1)
    cores += [core_send((x + 2) % X)]
    arrive(cores)
    theirs = owner_ref[prompt_ref[x * 4 + (1 - yh) * 2 + c]]
    mine = owner_ref[prompt_ref[dp]]
    hp_out[...] = xbuf[theirs // 4, theirs % 2]
    yh_copy = send(hp_out, hp_in, yh_id)
    arrive(r0)
    r1 = gather_step(resp_slot, z, Z, 1, z_right, z_left)
    arrive([yh_copy])
    prompt[z] = jnp.where((mine // 2) % 2 == yh, xbuf[mine // 4, mine % 2], hp_in[...])
    p0 = gather_step(prompt_slot, z, Z, 0, z_right, z_left)
    y_do = send(do_ref.at[0, :, far_q], do_far, y_id)
    arrive([y_q])

    def pair(step):
        return [(z + step) % Z, (z + Z - step) % Z]

    absorb(resp, [z], ROWS, True)
    arrive(r1)
    r2 = gather_step(resp_slot, z, Z, 2, z_right, z_left)
    absorb(resp, pair(1), ROWS, True)
    arrive(p0)
    p1 = gather_step(prompt_slot, z, Z, 1, z_right, z_left)
    arrive(r2)
    r3 = gather_step(resp_slot, z, Z, 3, z_right, z_left)
    absorb(resp, pair(2), ROWS, True)
    arrive(p1)
    p2 = gather_step(prompt_slot, z, Z, 2, z_right, z_left)
    absorb(resp, pair(3), ROWS, True)
    arrive(r3)
    arrive(p2)
    p3 = gather_step(prompt_slot, z, Z, 3, z_right, z_left)
    absorb(resp, [(z + 4) % Z], ROWS, True)
    absorb(prompt, [z] + pair(1), PROWS, False)
    absorb(prompt, pair(2) + pair(3), PROWS, False)
    arrive(p3)
    absorb(prompt, [(z + 4) % Z], PROWS, False)

    arrive([y_do])

    def finish(h, carry):
        total = l_ref[h]
        mixed = acc_ref[h] / total
        lse_ref[h] = m_ref[h] + jnp.log(total) * LOG2E
        cotangent = head_of(do_ref, do_far, h).astype(F32)
        delta_ref[h] = jnp.sum(cotangent.T * mixed, axis=0, keepdims=True)
        rows = mixed.T.astype(BF)
        out_ref[0, :, pl.ds(pl.multiple_of(yl * HALF_Q + h * 128, 128), 128)] = rows[:ROWS]
        out_far[:, pl.ds(pl.multiple_of(h * 128, 128), 128)] = rows[ROWS:]
        return carry

    lax.fori_loop(0, 2 * GROUP, finish, 0)
    y_result = send(out_far, out_ref.at[0, :, mine_q], y_id)

    def gradients(slots):
        count = len(slots)
        gacc[...] = jnp.zeros(gacc.shape, F32)

        def body(g, carry):
            for a in range(2):
                h = a * GROUP + g
                query = head_of(q_ref, q_far, h)
                cotangent = head_of(do_ref, do_far, h)
                probs = jnp.exp2(
                    nt(keys_of(prompt, slots, 0, a, PROWS), query) * SCORE_SCALE - lse_ref[h]
                )
                back = nt(keys_of(prompt, slots, 1, a, PROWS), cotangent)
                slopes = probs * (back - delta_ref[h])
                key_part = nn(slopes.astype(BF), query)
                value_part = nn(probs.astype(BF), cotangent)
                for n in range(count):
                    rows = slice(n * 128, n * 128 + 128)
                    columns = slice(a * 128, a * 128 + 128)
                    gacc[n, 0, :, columns] += key_part[rows]
                    gacc[n, 1, :, columns] += value_part[rows]
            return carry

        lax.fori_loop(0, GROUP, body, 0)

    def own_part(n, h):
        part = gacc[n, h].reshape(2, PROWS, HALF_KV)
        return part * SCALE if h == 0 else part

    def scatter_step(own, outgoing, incoming, step, n, right, left):
        halves = ((0,), (1,)) if step == 0 else ((0, 1), (0, 1))
        before = ((0,), (1,)) if step == 1 else ((0, 1), (0, 1))
        copies = []
        for way, peer in enumerate((right, left)):
            for h in halves[way]:
                part = own(way, h)
                if step > 0 and h in before[way]:
                    part = part + incoming[way, step - 1, h].astype(F32)
                outgoing[way, step, h] = part.astype(BF)
                copies.append(send(outgoing.at[way, step, h], incoming.at[way, step, h], peer))
        return copies

    gradients([(z + 4) % Z])
    s0 = scatter_step(lambda way, h: own_part(0, h), zs_out, zs_in, 0, Z, z_right, z_left)
    previous = s0
    for step in range(1, 4):
        gradients(pair(4 - step))
        arrive(previous)
        previous = scatter_step(own_part, zs_out, zs_in, step, Z, z_right, z_left)
    gradients([z])
    arrive(previous)
    for h in range(2):
        share[0, h] = (
            own_part(0, h) + zs_in[0, 3, h].astype(F32) + zs_in[1, 3, h].astype(F32)
        ).astype(BF)

    arrive([send(share.at[0], share.at[1], yh_id)])
    arrive([send(share, core_in, core_id)])
    owners = []
    for source_core in (c, 1 - c):
        for source_half in (yh, 1 - yh):
            owners.append(owner_ref[prompt_ref[x * 4 + source_half * 2 + source_core]])

    def destined(target, h):
        total = jnp.zeros((2, PROWS, HALF_KV), F32)
        for n, owner in enumerate(owners):
            part = (share if n < 2 else core_in)[n % 2, h].astype(F32)
            total = total + jnp.where(owner == target * 4 + yh * 2 + c, part, 0.0)
        return total

    def toward(distance):
        return lambda way, h: destined((x + distance) % X if way == 0 else (x + X - distance) % X, h)

    previous = scatter_step(toward(2), xs_out, xs_in, 0, X, x_right, x_left)
    arrive(previous)
    previous = scatter_step(toward(1), xs_out, xs_in, 1, X, x_right, x_left)
    arrive(previous)
    for h, ref in enumerate((gk_ref, gv_ref)):
        xsum[h] = destined(x, h) + xs_in[0, 1, h].astype(F32) + xs_in[1, 1, h].astype(F32)
        y_out[h] = xsum[h, other].astype(BF)
    last_copy = send(y_out, y_in, y_id)
    for h, ref in enumerate((gk_ref, gv_ref)):
        ref[0, :, mine_kv] = xsum[h, yl]
    arrive([last_copy])
    for h, ref in enumerate((gk_ref, gv_ref)):
        ref[0, :, far_kv] = y_in[h].astype(F32)
    arrive([y_result])
    for copy in started:
        copy.wait_send()


COPIES = 96


def on_device(*arguments):
    block = (2, 2, PROWS, HALF_KV)
    vmem = pl.BlockSpec(memory_space=pltpu.VMEM)
    smem = pl.BlockSpec(memory_space=pltpu.SMEM)
    return pl.pallas_call(
        kernel,
        out_shape=(
            jax.ShapeDtypeStruct((1, ROWS, 4096), BF),
            jax.ShapeDtypeStruct((1, PROWS, 512), F32),
            jax.ShapeDtypeStruct((1, PROWS, 512), F32),
        ),
        in_specs=[vmem] * 6 + [smem] * 4,
        out_specs=(vmem, vmem, vmem),
        scratch_shapes=[
            pltpu.VMEM((ROWS, HALF_Q), BF),
            pltpu.VMEM((ROWS, HALF_Q), BF),
            pltpu.VMEM((ROWS, HALF_Q), BF),
            pltpu.VMEM((Z, 2, 2, ROWS, HALF_KV), BF),
            pltpu.VMEM((X, 2) + block, BF),
            pltpu.VMEM(block, BF),
            pltpu.VMEM(block, BF),
            pltpu.VMEM((Z,) + block, BF),
            pltpu.VMEM((16, 1, 256), F32),
            pltpu.VMEM((16, 1, 256), F32),
            pltpu.VMEM((16, 128, 256), F32),
            pltpu.VMEM((16, 1, 256), F32),
            pltpu.VMEM((16, 1, 256), F32),
            pltpu.VMEM((2, 2, 128, HALF_KV), F32),
            pltpu.VMEM((2, 4) + block, BF),
            pltpu.VMEM((2, 4) + block, BF),
            pltpu.VMEM((2,) + block, BF),
            pltpu.VMEM(block, BF),
            pltpu.VMEM((2,) + block, BF),
            pltpu.VMEM((2, 2) + block, BF),
            pltpu.VMEM((2, 2) + block, BF),
            pltpu.VMEM((2, PROWS, HALF_KV), BF),
            pltpu.VMEM((2, PROWS, HALF_KV), BF),
            pltpu.VMEM(block, F32),
            pltpu.SemaphoreType.DMA((COPIES,)),
            pltpu.SemaphoreType.DMA((COPIES,)),
        ],
        compiler_params=pltpu.CompilerParams(
            collective_id=0, has_side_effects=True, vmem_limit_bytes=48 * 1024 * 1024
        ),
        cost_estimate=pl.CostEstimate(
            flops=10_000_000_000, bytes_accessed=8 * 1024 * 1024, transcendentals=17_000_000
        ),
    )(*arguments)


def solution(mesh):
    split = P("dp", "blk", None)
    return jax.shard_map(
        on_device,
        mesh=mesh,
        in_specs=(split,) * 6 + (P(),) * 4,
        out_specs=(split, split, split),
        check_vma=False,
    )
```

```python
import jax
import jax.numpy as jnp
from jax import lax
from jax.experimental import pallas as pl
from jax.experimental.pallas import tpu as pltpu
from jax.sharding import PartitionSpec as P

MESH = pl.DeviceIdType.MESH
HEAD_WIDTH = 128
SCALE = HEAD_WIDTH ** (-0.5)
LOG2E = 1.4426950408889634
SCORE_SCALE = SCALE * LOG2E
MASKED = -1e30
LOWEST = -1e20
BF = jnp.bfloat16
F32 = jnp.float32

X, YH, CORES, YL, Z = 4, 2, 2, 2, 8
GROUP = 8
ROWS = 128
PROWS = 64
HALF_KV = 256
HALF_Q = 2048


def nt(a, b):
    return lax.dot_general(a, b, (((1,), (1,)), ((), ())), preferred_element_type=F32)


def nn(a, b):
    return lax.dot_general(a, b, (((1,), (0,)), ((), ())), preferred_element_type=F32)


def tn(a, b):
    return lax.dot_general(a, b, (((0,), (0,)), ((), ())), preferred_element_type=F32)


def kernel(
    q_ref, rk_ref, rv_ref, pk_ref, pv_ref, do_ref, owner_hbm, prompt_hbm, length_hbm, half_hbm,
    out_ref, gk_ref, gv_ref,
    q_near, q_far, do_near, do_far, out_near, out_far, q_rows, q_turned, do_rows, do_turned,
    resp, xbuf, hp_out, hp_in, prompt, v_turned,
    m_ref, l_ref, acc_ref, lse_ref, delta_ref, gacc,
    zs_out, zs_in, share, core_in, xs_out, xs_in, y_out, y_in, xsum,
    owner_ref, prompt_ref, length_ref, half_ref,
    send_sem, recv_sem, local_sem,
):
    dp = lax.axis_index("dp")
    blk = lax.axis_index("blk")
    x, yh, c = dp // 4, (dp // 2) % 2, dp % 2
    yl, z = blk // Z, blk % Z
    other = 1 - yl
    y_id = (dp, other * Z + z)
    z_right, z_left = (dp, yl * Z + (z + 1) % Z), (dp, yl * Z + (z + Z - 1) % Z)
    x_right = (((x + 1) % X) * 4 + yh * 2 + c, blk)
    x_left = (((x + X - 1) % X) * 4 + yh * 2 + c, blk)
    core_id = (x * 4 + yh * 2 + (1 - c), blk)
    yh_id = (x * 4 + (1 - yh) * 2 + c, blk)

    def lanes(which, width):
        return pl.ds(pl.multiple_of(which * width, width), width)

    mine_kv, far_kv = lanes(yl, HALF_KV), lanes(other, HALF_KV)
    mine_q, far_q = lanes(yl, HALF_Q), lanes(other, HALF_Q)

    fetched = []

    def fetch(src, dst):
        copy = pltpu.make_async_copy(src, dst, local_sem.at[len(fetched)])
        copy.start()
        fetched.append(copy)
        return copy

    def present(copies):
        for copy in copies:
            copy.wait()

    own_prompt = [
        fetch(ref.at[0, :, mine_kv], xbuf.at[x, c, kv, yl])
        for kv, ref in enumerate((pk_ref, pv_ref))
    ]
    own_resp = [
        fetch(ref.at[0, :, mine_kv], resp.at[z, kv, yl])
        for kv, ref in enumerate((rk_ref, rv_ref))
    ]
    tables = [
        fetch(owner_hbm, owner_ref), fetch(prompt_hbm, prompt_ref),
        fetch(length_hbm, length_ref), fetch(half_hbm, half_ref),
    ]
    own_q = fetch(q_ref.at[0, :, mine_q], q_near)
    own_do = fetch(do_ref.at[0, :, mine_q], do_near)

    barrier = pltpu.get_barrier_semaphore()
    peers = (y_id, z_right, z_left, x_right, x_left, core_id, yh_id)
    for peer in peers:
        pl.semaphore_signal(barrier, inc=1, device_id=peer, device_id_type=MESH)
    pl.semaphore_wait(barrier, len(peers))

    started = []

    def send(src, dst, peer):
        index = len(started)
        copy = pltpu.make_async_remote_copy(
            src_ref=src, dst_ref=dst, send_sem=send_sem.at[index], recv_sem=recv_sem.at[index],
            device_id=peer, device_id_type=MESH,
        )
        copy.start()
        started.append(copy)
        return copy

    def arrive(copies):
        for copy in copies:
            copy.wait_recv()

    y_prompt = [
        send(ref.at[0, :, far_kv], xbuf.at[x, c, kv, yl], y_id)
        for kv, ref in enumerate((pk_ref, pv_ref))
    ]
    y_resp = [
        send(ref.at[0, :, far_kv], resp.at[z, kv, yl], y_id)
        for kv, ref in enumerate((rk_ref, rv_ref))
    ]
    y_q = send(q_ref.at[0, :, far_q], q_far, y_id)
    def gather_step(slot, pos, n, step, right, left):
        halves_right, halves_left = ((0, 1), (0, 1)) if step < n // 2 - 1 else ((0,), (1,))
        from_slot = (pos + n - step) % n
        copies = [send(slot(from_slot, h), slot(from_slot, h), right) for h in halves_right]
        from_slot = (pos + step) % n
        copies += [send(slot(from_slot, h), slot(from_slot, h), left) for h in halves_left]
        return copies

    def x_slot(i, h):
        return xbuf.at[i, c, h]

    def core_send(i):
        return send(xbuf.at[i, c], xbuf.at[i, c], core_id)

    def resp_slot(i, h):
        return resp.at[i, h]

    def prompt_slot(i, h):
        return prompt.at[i, h]

    def prepare(source, part, rows, turned):
        def body(h, carry):
            tile = source[:, pl.ds(pl.multiple_of(h * 128, 128), 128)]
            rows[h, part * ROWS : (part + 1) * ROWS] = tile
            turned[h, :, part * ROWS : (part + 1) * ROWS] = tile.T
            return carry

        lax.fori_loop(0, 2 * GROUP, body, 0, unroll=4)

    present(tables)
    lane = lax.broadcasted_iota(jnp.int32, (1, 2 * ROWS), 1)
    last = length_ref[dp] - 1
    limit = jnp.zeros((1, 2 * ROWS), jnp.int32)
    for part, holder in enumerate((blk, other * Z + z)):
        for e in range(2):
            block = part * 2 + e
            inside = (lane >= block * 64) & (lane < block * 64 + 64)
            limit = jnp.where(inside, half_ref[2 * holder + e] * 64 + lane - block * 64, limit)
    limit = jnp.minimum(limit, last)
    down = lax.broadcasted_iota(jnp.int32, (64, 2 * ROWS), 0)

    def keys_of(buf, slots, kv, a, rows):
        columns = pl.ds(pl.multiple_of(a * 128, 128), 128)
        return [buf[i, kv, :, :, columns].reshape(2 * rows, 128) for i in slots]

    def absorb(*chunks):
        bounds = []
        for buf, slots, rows, masked in chunks:
            for i in slots:
                for n in range(2 * rows // 64):
                    if masked:
                        bounds.append(limit - half_ref[2 * ((n // 2) * Z + i) + n % 2] * 64)
                    else:
                        bounds.append(None)
        count = 64 * len(bounds)

        def all_keys(kv, a):
            parts = []
            for buf, slots, rows, masked in chunks:
                parts += keys_of(buf, slots, kv, a, rows)
            return jnp.concatenate(parts, axis=0) if len(parts) > 1 else parts[0]

        for a in range(2):
            v_turned[a, :, :count] = all_keys(1, a).T

        def hide(scores):
            pieces = []
            for n, bound in enumerate(bounds):
                piece = scores[64 * n : 64 * n + 64]
                pieces.append(piece if bound is None else jnp.where(down <= bound, piece, MASKED))
            return jnp.concatenate(pieces, axis=0)

        def body(t, carry):
            a = t // 2
            heads = pl.ds(t * 4, 4)
            keys, values = all_keys(0, a), v_turned[a, :, :count]
            old, old_total, old_mixed = m_ref[heads], l_ref[heads], acc_ref[heads]
            scores = [hide(nn(keys, q_turned[t * 4 + j]) * SCORE_SCALE) for j in range(4)]
            peaks, totals, mixes = [], [], []
            for j in range(4):
                peak = jnp.maximum(old[j], jnp.max(scores[j], axis=0, keepdims=True))
                weights = jnp.exp2(scores[j] - peak)
                factor = jnp.exp2(old[j] - peak)
                peaks.append(peak)
                totals.append(old_total[j] * factor + jnp.sum(weights, axis=0, keepdims=True))
                mixes.append(old_mixed[j] * factor + nn(values, weights.astype(BF)))
            for j in range(4):
                m_ref[t * 4 + j] = peaks[j]
                l_ref[t * 4 + j] = totals[j]
                acc_ref[t * 4 + j] = mixes[j]
            return carry

        lax.fori_loop(0, 4, body, 0)

    m_ref[...] = jnp.full(m_ref.shape, LOWEST, F32)
    l_ref[...] = jnp.zeros(l_ref.shape, F32)
    acc_ref[...] = jnp.zeros(acc_ref.shape, F32)

    present(own_prompt)
    arrive(y_prompt)
    x0 = gather_step(x_slot, x, X, 0, x_right, x_left)
    cores = [core_send(x)]
    present(own_resp)
    arrive(y_resp)
    r0 = gather_step(resp_slot, z, Z, 0, z_right, z_left)
    present([own_q, own_do])
    prepare(q_near, 0, q_rows, q_turned)
    prepare(do_near, 0, do_rows, do_turned)
    arrive(x0)
    x1 = gather_step(x_slot, x, X, 1, x_right, x_left)
    cores += [core_send((x + 1) % X), core_send((x + X - 1) % X)]
    arrive(x1)
    cores += [core_send((x + 2) % X)]
    arrive(cores)
    theirs = owner_ref[prompt_ref[x * 4 + (1 - yh) * 2 + c]]
    mine = owner_ref[prompt_ref[dp]]
    hp_out[...] = xbuf[theirs // 4, theirs % 2]
    yh_copy = send(hp_out, hp_in, yh_id)
    arrive(r0)
    r1 = gather_step(resp_slot, z, Z, 1, z_right, z_left)
    arrive([yh_copy])
    prompt[z] = jnp.where((mine // 2) % 2 == yh, xbuf[mine // 4, mine % 2], hp_in[...])
    p0 = gather_step(prompt_slot, z, Z, 0, z_right, z_left)
    y_do = send(do_ref.at[0, :, far_q], do_far, y_id)
    arrive([y_q])
    prepare(q_far, 1, q_rows, q_turned)

    def pair(step):
        return [(z + step) % Z, (z + Z - step) % Z]

    absorb((resp, [z] + pair(1), ROWS, True))
    arrive(r1)
    r2 = gather_step(resp_slot, z, Z, 2, z_right, z_left)
    arrive(p0)
    p1 = gather_step(prompt_slot, z, Z, 1, z_right, z_left)
    absorb((resp, pair(2), ROWS, True))
    arrive(r2)
    r3 = gather_step(resp_slot, z, Z, 3, z_right, z_left)
    arrive(p1)
    p2 = gather_step(prompt_slot, z, Z, 2, z_right, z_left)
    absorb((resp, pair(3), ROWS, True))
    arrive([y_do])
    prepare(do_far, 1, do_rows, do_turned)
    arrive(p2)
    p3 = gather_step(prompt_slot, z, Z, 3, z_right, z_left)
    arrive(r3)
    absorb((resp, [(z + 4) % Z], ROWS, True), (prompt, [z] + pair(1) + pair(2), PROWS, False))
    arrive(p3)
    absorb((prompt, pair(3) + [(z + 4) % Z], PROWS, False))

    def finish(t, carry):
        heads = pl.ds(t * 4, 4)
        peak, total, mixed = m_ref[heads], l_ref[heads], acc_ref[heads]
        turned = do_turned[heads]
        outs, sums, deltas = [], [], []
        for j in range(4):
            result = mixed[j] / total[j]
            sums.append(peak[j] + jnp.log(total[j]) * LOG2E)
            deltas.append(jnp.sum(turned[j].astype(F32) * result, axis=0, keepdims=True))
            outs.append(result.T.astype(BF))
        for j in range(4):
            h = t * 4 + j
            lse_ref[h] = sums[j]
            delta_ref[h] = deltas[j]
            columns = pl.ds(pl.multiple_of(h * 128, 128), 128)
            out_near[:, columns] = outs[j][:ROWS]
            out_far[:, columns] = outs[j][ROWS:]
        return carry

    lax.fori_loop(0, 4, finish, 0)
    y_result = send(out_far, out_ref.at[0, :, mine_q], y_id)
    own_result = fetch(out_near, out_ref.at[0, :, mine_q])

    def gradients(slots):
        def body(a, carry):
            keys = jnp.concatenate(keys_of(prompt, slots, 0, a, PROWS), axis=0)
            values = jnp.concatenate(keys_of(prompt, slots, 1, a, PROWS), axis=0)
            all_probs, all_slopes = [], []
            for j in range(GROUP):
                h = a * GROUP + j
                probs = jnp.exp2(nn(keys, q_turned[h]) * SCORE_SCALE - lse_ref[h])
                slopes = probs * (nn(values, do_turned[h]) - delta_ref[h])
                all_probs.append(probs.astype(BF))
                all_slopes.append(slopes.astype(BF))
            heads = pl.ds(a * GROUP, GROUP)
            queries = q_rows[heads].reshape(GROUP * 2 * ROWS, 128)
            cotangents = do_rows[heads].reshape(GROUP * 2 * ROWS, 128)
            key_part = nn(jnp.concatenate(all_slopes, axis=1), queries)
            value_part = nn(jnp.concatenate(all_probs, axis=1), cotangents)
            columns = pl.ds(pl.multiple_of(a * 128, 128), 128)
            for n in range(len(slots)):
                gacc[n, 0, :, columns] = key_part[n * 128 : n * 128 + 128]
                gacc[n, 1, :, columns] = value_part[n * 128 : n * 128 + 128]
            return carry

        lax.fori_loop(0, 2, body, 0)

    def own_part(n, h):
        part = gacc[n, h].reshape(2, PROWS, HALF_KV)
        return part * SCALE if h == 0 else part

    def scatter_step(own, outgoing, incoming, step, n, right, left):
        halves = ((0,), (1,)) if step == 0 else ((0, 1), (0, 1))
        before = ((0,), (1,)) if step == 1 else ((0, 1), (0, 1))
        copies = []
        for way, peer in enumerate((right, left)):
            for h in halves[way]:
                part = own(way, h)
                if step > 0 and h in before[way]:
                    part = part + incoming[way, step - 1, h].astype(F32)
                outgoing[way, step, h] = part.astype(BF)
                copies.append(send(outgoing.at[way, step, h], incoming.at[way, step, h], peer))
        return copies

    gradients([(z + 4) % Z])
    s0 = scatter_step(lambda way, h: own_part(0, h), zs_out, zs_in, 0, Z, z_right, z_left)
    previous = s0
    for step in range(1, 4):
        gradients(pair(4 - step))
        arrive(previous)
        previous = scatter_step(own_part, zs_out, zs_in, step, Z, z_right, z_left)
    gradients([z])
    arrive(previous)
    for h in range(2):
        share[0, h] = (
            own_part(0, h) + zs_in[0, 3, h].astype(F32) + zs_in[1, 3, h].astype(F32)
        ).astype(BF)

    arrive([send(share.at[0], share.at[1], yh_id)])
    arrive([send(share, core_in, core_id)])
    owners = []
    for source_core in (c, 1 - c):
        for source_half in (yh, 1 - yh):
            owners.append(owner_ref[prompt_ref[x * 4 + source_half * 2 + source_core]])

    def destined(target, h):
        total = jnp.zeros((2, PROWS, HALF_KV), F32)
        for n, owner in enumerate(owners):
            part = (share if n < 2 else core_in)[n % 2, h].astype(F32)
            total = total + jnp.where(owner == target * 4 + yh * 2 + c, part, 0.0)
        return total

    def toward(distance):
        return lambda way, h: destined((x + distance) % X if way == 0 else (x + X - distance) % X, h)

    previous = scatter_step(toward(2), xs_out, xs_in, 0, X, x_right, x_left)
    arrive(previous)
    previous = scatter_step(toward(1), xs_out, xs_in, 1, X, x_right, x_left)
    arrive(previous)
    for h, ref in enumerate((gk_ref, gv_ref)):
        xsum[h] = destined(x, h) + xs_in[0, 1, h].astype(F32) + xs_in[1, 1, h].astype(F32)
        y_out[h] = xsum[h, other].astype(BF)
    last_copy = send(y_out, y_in, y_id)
    for h, ref in enumerate((gk_ref, gv_ref)):
        ref[0, :, mine_kv] = xsum[h, yl]
    arrive([last_copy])
    for h, ref in enumerate((gk_ref, gv_ref)):
        ref[0, :, far_kv] = y_in[h].astype(F32)
    arrive([y_result])
    present([own_result])
    for copy in started:
        copy.wait_send()


COPIES = 96


def on_device(*arguments):
    block = (2, 2, PROWS, HALF_KV)
    vmem = pl.BlockSpec(memory_space=pltpu.VMEM)
    hbm = pl.BlockSpec(memory_space=pltpu.HBM)
    return pl.pallas_call(
        kernel,
        out_shape=(
            jax.ShapeDtypeStruct((1, ROWS, 4096), BF),
            jax.ShapeDtypeStruct((1, PROWS, 512), F32),
            jax.ShapeDtypeStruct((1, PROWS, 512), F32),
        ),
        in_specs=[hbm] * 10,
        out_specs=(hbm, vmem, vmem),
        scratch_shapes=[
            pltpu.VMEM((ROWS, HALF_Q), BF),
            pltpu.VMEM((ROWS, HALF_Q), BF),
            pltpu.VMEM((ROWS, HALF_Q), BF),
            pltpu.VMEM((ROWS, HALF_Q), BF),
            pltpu.VMEM((ROWS, HALF_Q), BF),
            pltpu.VMEM((ROWS, HALF_Q), BF),
            pltpu.VMEM((16, 256, 128), BF),
            pltpu.VMEM((16, 128, 256), BF),
            pltpu.VMEM((16, 256, 128), BF),
            pltpu.VMEM((16, 128, 256), BF),
            pltpu.VMEM((Z, 2, 2, ROWS, HALF_KV), BF),
            pltpu.VMEM((X, 2) + block, BF),
            pltpu.VMEM(block, BF),
            pltpu.VMEM(block, BF),
            pltpu.VMEM((Z,) + block, BF),
            pltpu.VMEM((2, 128, 1024), BF),
            pltpu.VMEM((16, 1, 256), F32),
            pltpu.VMEM((16, 1, 256), F32),
            pltpu.VMEM((16, 128, 256), F32),
            pltpu.VMEM((16, 1, 256), F32),
            pltpu.VMEM((16, 1, 256), F32),
            pltpu.VMEM((2, 2, 128, HALF_KV), F32),
            pltpu.VMEM((2, 4) + block, BF),
            pltpu.VMEM((2, 4) + block, BF),
            pltpu.VMEM((2,) + block, BF),
            pltpu.VMEM((2,) + block, BF),
            pltpu.VMEM((2, 2) + block, BF),
            pltpu.VMEM((2, 2) + block, BF),
            pltpu.VMEM((2, PROWS, HALF_KV), BF),
            pltpu.VMEM((2, PROWS, HALF_KV), BF),
            pltpu.VMEM(block, F32),
            pltpu.SMEM((16,), jnp.int32),
            pltpu.SMEM((16,), jnp.int32),
            pltpu.SMEM((16,), jnp.int32),
            pltpu.SMEM((32,), jnp.int32),
            pltpu.SemaphoreType.DMA((COPIES,)),
            pltpu.SemaphoreType.DMA((COPIES,)),
            pltpu.SemaphoreType.DMA((16,)),
        ],
        compiler_params=pltpu.CompilerParams(
            collective_id=0, has_side_effects=True, vmem_limit_bytes=60 * 1024 * 1024
        ),
        cost_estimate=pl.CostEstimate(
            flops=10_000_000_000, bytes_accessed=8 * 1024 * 1024, transcendentals=17_000_000
        ),
    )(*arguments)


def solution(mesh):
    split = P("dp", "blk", None)
    return jax.shard_map(
        on_device,
        mesh=mesh,
        in_specs=(split,) * 6 + (P(),) * 4,
        out_specs=(split, split, split),
        check_vma=False,
    )
```

```python
import jax
import jax.numpy as jnp
from jax import lax
from jax.experimental import pallas as pl
from jax.experimental.pallas import tpu as pltpu
from jax.sharding import PartitionSpec as P

MESH = pl.DeviceIdType.MESH
HEAD_WIDTH = 128
SCALE = HEAD_WIDTH ** (-0.5)
LOG2E = 1.4426950408889634
SCORE_SCALE = SCALE * LOG2E
MASKED = -1e30
LOWEST = -1e20
BF = jnp.bfloat16
F32 = jnp.float32

X, YH, CORES, YL, Z = 4, 2, 2, 2, 8
GROUP = 8
ROWS = 128
PROWS = 64
HALF_KV = 256
HALF_Q = 2048


def nt(a, b):
    return lax.dot_general(a, b, (((1,), (1,)), ((), ())), preferred_element_type=F32)


def nn(a, b):
    return lax.dot_general(a, b, (((1,), (0,)), ((), ())), preferred_element_type=F32)


def tn(a, b):
    return lax.dot_general(a, b, (((0,), (0,)), ((), ())), preferred_element_type=F32)


def kernel(
    q_ref, rk_ref, rv_ref, pk_ref, pv_ref, do_ref, owner_hbm, prompt_hbm, length_hbm, half_hbm,
    out_ref, gk_ref, gv_ref,
    q_near, q_far, do_near, do_far, out_near, out_far, q_rows, q_turned, do_rows, do_turned,
    resp, xbuf, chosen_out, chosen_in, prompt, v_turned,
    m_ref, acc_ref, lse_ref, delta_ref, gacc,
    zs_out, zs_in, share_out, share, core_in, xs_out, xs_in,
    owner_ref, prompt_ref, length_ref, half_ref,
    send_sem, recv_sem, local_sem,
):
    dp = lax.axis_index("dp")
    blk = lax.axis_index("blk")
    x, yh, c = dp // 4, (dp // 2) % 2, dp % 2
    yl, z = blk // Z, blk % Z
    other = 1 - yl
    y_id = (dp, other * Z + z)
    z_right, z_left = (dp, yl * Z + (z + 1) % Z), (dp, yl * Z + (z + Z - 1) % Z)
    x_right = (((x + 1) % X) * 4 + yh * 2 + c, blk)
    x_left = (((x + X - 1) % X) * 4 + yh * 2 + c, blk)
    core_id = (x * 4 + yh * 2 + (1 - c), blk)
    yh_id = (x * 4 + (1 - yh) * 2 + c, blk)
    diagonal_id = (x * 4 + (1 - yh) * 2 + c, other * Z + z)

    def lanes(which, width):
        return pl.ds(pl.multiple_of(which * width, width), width)

    def head_lanes(half, a):
        return pl.ds(pl.multiple_of(half * HALF_KV + a * 128, 128), 128)

    def group_lanes(half, a):
        return pl.ds(pl.multiple_of(half * HALF_Q + a * 1024, 1024), 1024)

    mine_kv, far_kv = lanes(yl, HALF_KV), lanes(other, HALF_KV)
    mine_q = lanes(yl, HALF_Q)

    fetched = []

    def fetch(src, dst):
        copy = pltpu.make_async_copy(src, dst, local_sem.at[len(fetched)])
        copy.start()
        fetched.append(copy)
        return copy

    def present(copies):
        for copy in copies:
            copy.wait()

    own_prompt = [
        fetch(ref.at[0], xbuf.at[x, c, kv]) for kv, ref in enumerate((pk_ref, pv_ref))
    ]
    own_resp = [
        fetch(ref.at[0, :, mine_kv], resp.at[z, kv, yl])
        for kv, ref in enumerate((rk_ref, rv_ref))
    ]
    tables = [
        fetch(owner_hbm, owner_ref), fetch(prompt_hbm, prompt_ref),
        fetch(length_hbm, length_ref), fetch(half_hbm, half_ref),
    ]
    own_q = fetch(q_ref.at[0, :, mine_q], q_near)
    own_do = fetch(do_ref.at[0, :, mine_q], do_near)

    barrier = pltpu.get_barrier_semaphore()
    peers = (y_id, z_right, z_left, x_right, x_left, core_id, yh_id, diagonal_id)
    for peer in peers:
        pl.semaphore_signal(barrier, inc=1, device_id=peer, device_id_type=MESH)
    pl.semaphore_wait(barrier, len(peers))

    started = []

    def send(src, dst, peer):
        index = len(started)
        copy = pltpu.make_async_remote_copy(
            src_ref=src, dst_ref=dst, send_sem=send_sem.at[index], recv_sem=recv_sem.at[index],
            device_id=peer, device_id_type=MESH,
        )
        copy.start()
        started.append(copy)
        return copy

    def arrive(copies):
        for copy in copies:
            copy.wait_recv()

    x0 = [
        send(ref.at[0], xbuf.at[x, c, kv], peer)
        for peer in (x_right, x_left)
        for kv, ref in enumerate((pk_ref, pv_ref))
    ]
    y_resp = [
        send(ref.at[0, :, far_kv], resp.at[z, kv, yl], y_id)
        for kv, ref in enumerate((rk_ref, rv_ref))
    ]
    cores = [
        send(ref.at[0], xbuf.at[x, c, kv], core_id) for kv, ref in enumerate((pk_ref, pv_ref))
    ]
    y_q = [
        send(q_ref.at[0, :, group_lanes(other, a)], q_far.at[:, a * 1024 : a * 1024 + 1024], y_id)
        for a in range(2)
    ]

    def gather_step(slot, pos, n, step, right, left, halves=(0, 1)):
        final = step == n // 2 - 1
        copies = []
        for h in halves:
            for way, peer in enumerate((right, left)):
                if not final or h == way:
                    at = slot((pos + n - step) % n if way == 0 else (pos + step) % n, h)
                    copies.append(send(at, at, peer))
        return copies

    def resp_gather(step, h):
        return gather_step(lambda i, h: resp.at[i, h], z, Z, step, z_right, z_left, (h,))

    def prompt_gather(a, step):
        return gather_step(lambda i, h: prompt.at[a, i, h], z, Z, step, z_right, z_left)

    def core_send(i):
        return send(xbuf.at[i, c], xbuf.at[i, c], core_id)

    def prepare(source, part, a, rows, turned):
        def body(g, carry):
            h = a * GROUP + g
            tile = source[:, pl.ds(pl.multiple_of(h * 128, 128), 128)]
            rows[h, part * ROWS : (part + 1) * ROWS] = tile
            turned[h, :, part * ROWS : (part + 1) * ROWS] = tile.T
            return carry

        lax.fori_loop(0, GROUP, body, 0, unroll=4)

    present(tables)
    lane = lax.broadcasted_iota(jnp.int32, (1, 2 * ROWS), 1)
    last = length_ref[dp] - 1
    limit = jnp.zeros((1, 2 * ROWS), jnp.int32)
    for part, holder in enumerate((blk, other * Z + z)):
        for e in range(2):
            block = part * 2 + e
            inside = (lane >= block * 64) & (lane < block * 64 + 64)
            limit = jnp.where(inside, half_ref[2 * holder + e] * 64 + lane - block * 64, limit)
    limit = jnp.minimum(limit, last)
    down = lax.broadcasted_iota(jnp.int32, (64, 2 * ROWS), 0)

    def resp_rows(slots, kv, a):
        return [
            resp[i, kv, :, :, a * 128 : (a + 1) * 128].reshape(2 * ROWS, 128) for i in slots
        ]

    def prompt_rows(slots, kv, a):
        return [prompt[a, i, kv].reshape(2 * PROWS, 128) for i in slots]

    def absorb(a, resp_slots, prompt_slots):
        bounds = []
        for i in resp_slots:
            for n in range(4):
                bounds.append(limit - half_ref[2 * ((n // 2) * Z + i) + n % 2] * 64)
        bounds += [None] * (2 * len(prompt_slots))
        count = 64 * len(bounds)

        def all_rows(kv):
            parts = resp_rows(resp_slots, kv, a) + prompt_rows(prompt_slots, kv, a)
            return jnp.concatenate(parts, axis=0) if len(parts) > 1 else parts[0]

        v_turned[:128, :count] = all_rows(1).T

        def hide(scores):
            pieces = []
            for n, bound in enumerate(bounds):
                piece = scores[64 * n : 64 * n + 64]
                pieces.append(piece if bound is None else jnp.where(down <= bound, piece, MASKED))
            return jnp.concatenate(pieces, axis=0)

        def body(t, carry):
            first = a * GROUP + t * 4
            heads = pl.ds(first, 4)
            keys, values = all_rows(0), v_turned[:, :count]
            old, old_mixed = m_ref[heads], acc_ref[heads]
            scores = [hide(nn(keys, q_turned[first + j]) * SCORE_SCALE) for j in range(4)]
            peaks, mixes = [], []
            for j in range(4):
                peak = jnp.maximum(old[j], jnp.max(scores[j], axis=0, keepdims=True))
                weights = jnp.exp2(scores[j] - peak).astype(BF)
                peaks.append(peak)
                mixes.append(old_mixed[j] * jnp.exp2(old[j] - peak) + nn(values, weights))
            for j in range(4):
                m_ref[first + j] = peaks[j]
                acc_ref[first + j] = mixes[j]
            return carry

        lax.fori_loop(0, 2, body, 0)

    def finish(a):
        def body(t, carry):
            first = a * GROUP + t * 4
            heads = pl.ds(first, 4)
            peak, mixed, turned = m_ref[heads], acc_ref[heads], do_turned[heads]
            outs, sums, deltas = [], [], []
            for j in range(4):
                total = mixed[j, 128:129]
                result = mixed[j, :128] / total
                sums.append(peak[j] + jnp.log(total) * LOG2E)
                deltas.append(jnp.sum(turned[j].astype(F32) * result, axis=0, keepdims=True))
                outs.append(result.T.astype(BF))
            for j in range(4):
                h = first + j
                lse_ref[h] = sums[j]
                delta_ref[h] = deltas[j]
                columns = pl.ds(pl.multiple_of(h * 128, 128), 128)
                out_near[:, columns] = outs[j][:ROWS]
                out_far[:, columns] = outs[j][ROWS:]
            return carry

        lax.fori_loop(0, 2, body, 0)
        return send(
            out_far.at[:, a * 1024 : a * 1024 + 1024], out_ref.at[0, :, group_lanes(yl, a)], y_id
        )

    def gradients(a, slots):
        keys = jnp.concatenate(prompt_rows(slots, 0, a), axis=0)
        values = jnp.concatenate(prompt_rows(slots, 1, a), axis=0)
        all_probs, all_slopes = [], []
        for h in range(a * GROUP, a * GROUP + GROUP):
            probs = jnp.exp2(nn(keys, q_turned[h]) * SCORE_SCALE - lse_ref[h])
            slopes = probs * (nn(values, do_turned[h]) - delta_ref[h])
            all_probs.append(probs.astype(BF))
            all_slopes.append(slopes.astype(BF))
        heads = slice(a * GROUP, a * GROUP + GROUP)
        queries = q_rows[heads].reshape(GROUP * 2 * ROWS, 128)
        cotangents = do_rows[heads].reshape(GROUP * 2 * ROWS, 128)
        key_part = nn(jnp.concatenate(all_slopes, axis=1), queries) * SCALE
        value_part = nn(jnp.concatenate(all_probs, axis=1), cotangents)
        for n in range(len(slots)):
            gacc[n, 0] = key_part[n * 128 : n * 128 + 128].reshape(2, PROWS, 128)
            gacc[n, 1] = value_part[n * 128 : n * 128 + 128].reshape(2, PROWS, 128)

    def scatter_step(own, outgoing, incoming, step, right, left):
        halves = ((0,), (1,)) if step == 0 else ((0, 1), (0, 1))
        before = ((0,), (1,)) if step == 1 else ((0, 1), (0, 1))
        copies = []
        for way, peer in enumerate((right, left)):
            for h in halves[way]:
                part = own(way, h)
                if step > 0 and h in before[way]:
                    part = part + incoming[way, step - 1, h].astype(F32)
                outgoing[way, step, h] = part.astype(BF)
                copies.append(send(outgoing.at[way, step, h], incoming.at[way, step, h], peer))
        return copies

    def z_scatter(a, step):
        own = (lambda way, h: gacc[0, h]) if step == 0 else (lambda way, h: gacc[way, h])
        return scatter_step(own, zs_out.at[a], zs_in.at[a], step, z_right, z_left)

    def to_y_ring(a):
        for h in range(2):
            for n, where in enumerate((yl, other)):
                total = gacc[0, h, where]
                for way in range(2):
                    total = total + zs_in[a, way, 3, h, where].astype(F32)
                (share.at[a, 0, 0] if n == 0 else share_out.at[a])[h] = total.astype(BF)
        return [
            send(share_out.at[a], share.at[a, 0, 1], y_id),
            send(share.at[a, 0, 0], share.at[a, 1, 0], yh_id),
            send(share_out.at[a], share.at[a, 1, 1], diagonal_id),
        ]

    def to_core(a):
        return [send(share.at[a], core_in.at[a], core_id)]

    owners = []
    for source_core in (c, 1 - c):
        for source_half in (yh, 1 - yh):
            owners.append(owner_ref[prompt_ref[x * 4 + source_half * 2 + source_core]])

    def destined(a, target, h):
        total = jnp.zeros((2, PROWS, 128), F32)
        for n, owner in enumerate(owners):
            part = (share if n < 2 else core_in)[a, n % 2, :, h].astype(F32)
            total = total + jnp.where(owner == target * 4 + yh * 2 + c, part, 0.0)
        return total

    def x_scatter(a, step):
        distance = 2 - step
        targets = ((x + distance) % X, (x + X - distance) % X)
        return scatter_step(
            lambda way, h: destined(a, targets[way], h),
            xs_out.at[a], xs_in.at[a], step, x_right, x_left,
        )

    def store(a):
        for h, ref in enumerate((gk_ref, gv_ref)):
            total = destined(a, x, h)
            for way in range(2):
                total = total + xs_in[a, way, 1, h].astype(F32)
            ref[0, :, head_lanes(yl, a)] = total[0]
            ref[0, :, head_lanes(other, a)] = total[1]

    drained = []

    def drain():
        for copy in started[len(drained) :]:
            copy.wait_send()
            drained.append(copy)

    m_ref[...] = jnp.full(m_ref.shape, LOWEST, F32)
    acc_ref[...] = jnp.zeros(acc_ref.shape, F32)
    v_turned[128:] = jnp.ones((16, v_turned.shape[1]), BF)

    def pair(step):
        return [(z + step) % Z, (z + Z - step) % Z]

    opposite = [(z + 4) % Z]
    p, r = [None, None], [None, None]

    def pass_on(step):
        for a in range(2):
            arrive(p[a])
            p[a] = prompt_gather(a, step)

    def pass_on_resp(step):
        for h in range(2):
            arrive(r[h])
            r[h] = resp_gather(step, h)

    present([own_q])
    for a in range(2):
        prepare(q_near, 0, a, q_rows, q_turned)
    arrive(x0)
    x1 = gather_step(lambda i, h: xbuf.at[i, c, h], x, X, 1, x_right, x_left)
    cores += [core_send((x + 1) % X), core_send((x + X - 1) % X)]
    present(own_resp)
    for h in range(2):
        arrive([y_resp[h]])
        r[h] = resp_gather(0, h)
    arrive(x1)
    cores += [core_send((x + 2) % X)]
    present([own_do])
    for a in range(2):
        prepare(do_near, 0, a, do_rows, do_turned)
    present(own_prompt)
    arrive(cores)
    theirs = owner_ref[prompt_ref[x * 4 + (1 - yh) * 2 + c]]
    mine = owner_ref[prompt_ref[dp]]

    def piece(owner, half, a):
        return xbuf[owner // 4, owner % 2, :, :, head_lanes(half, a)]

    ring = []
    for n, (owner, half, peer) in enumerate(
        ((mine, other, y_id), (theirs, yl, yh_id), (theirs, other, diagonal_id))
    ):
        for a in range(2):
            chosen_out[n, a] = piece(owner, half, a)
        ring.append(send(chosen_out.at[n], chosen_in.at[n], peer))
    arrive([y_q[0]])
    prepare(q_far, 1, 0, q_rows, q_turned)
    absorb(0, [z], [])
    pass_on_resp(1)
    arrive(ring)
    here = (mine // 2) % 2 == yh
    for a in range(2):
        for kv in range(2):
            prompt[a, z, kv, yl] = jnp.where(here, piece(mine, yl, a)[kv], chosen_in[1, a, kv])
            prompt[a, z, kv, other] = jnp.where(here, chosen_in[0, a, kv], chosen_in[2, a, kv])
        p[a] = prompt_gather(a, 0)
    y_do = [
        send(do_ref.at[0, :, group_lanes(other, a)], do_far.at[:, a * 1024 : a * 1024 + 1024], y_id)
        for a in range(2)
    ]
    absorb(0, pair(1), [])
    arrive([y_q[1]])
    prepare(q_far, 1, 1, q_rows, q_turned)
    absorb(1, [z] + pair(1), [])
    pass_on(1)
    pass_on_resp(2)
    absorb(0, pair(2), [])
    pass_on(2)
    absorb(1, pair(2), [])
    pass_on_resp(3)
    pass_on(3)
    absorb(0, pair(3), [])
    absorb(1, pair(3), [])
    drain()
    for h in range(2):
        arrive(r[h])
    absorb(0, opposite, [z] + pair(1) + pair(2))
    arrive([y_do[0]])
    prepare(do_far, 1, 0, do_rows, do_turned)
    arrive(p[0])
    absorb(0, [], pair(3) + opposite)
    results = [finish(0)]
    gradients(0, opposite)
    s0 = z_scatter(0, 0)
    absorb(1, opposite, [z] + pair(1) + pair(2))
    gradients(0, pair(3))
    arrive(s0)
    s0 = z_scatter(0, 1)
    arrive([y_do[1]])
    prepare(do_far, 1, 1, do_rows, do_turned)
    arrive(p[1])
    absorb(1, [], pair(3) + opposite)
    results += [finish(1)]
    own_result = fetch(out_near, out_ref.at[0, :, mine_q])
    gradients(1, opposite)
    s1 = z_scatter(1, 0)
    gradients(0, pair(2))
    arrive(s0)
    s0 = z_scatter(0, 2)
    gradients(1, pair(3))
    arrive(s1)
    s1 = z_scatter(1, 1)
    gradients(0, pair(1))
    arrive(s0)
    s0 = z_scatter(0, 3)
    gradients(1, pair(2))
    arrive(s1)
    s1 = z_scatter(1, 2)
    gradients(0, [z])
    arrive(s0)

    t0 = to_y_ring(0)
    gradients(1, pair(1))
    arrive(s1)
    s1 = z_scatter(1, 3)
    arrive(t0)
    t0 = to_core(0)
    gradients(1, [z])
    arrive(t0)
    t0 = x_scatter(0, 0)
    arrive(s1)
    t1 = to_y_ring(1)
    arrive(t0)
    t0 = x_scatter(0, 1)
    arrive(t1)
    t1 = to_core(1)
    drain()
    arrive(t1)
    t1 = x_scatter(1, 0)
    arrive(t0)
    store(0)
    arrive(t1)
    t1 = x_scatter(1, 1)
    arrive(results)
    present([own_result])
    drain()
    arrive(t1)
    store(1)


COPIES = 128


PIECES = 4


def copy_out(*refs):
    ins, outs, held = refs[:3], refs[3:6], refs[6:9]
    in_sem, out_sem = refs[9:]
    parts = [(0, slice(n * 1024, n * 1024 + 1024)) for n in range(PIECES)]
    parts += [(1, slice(0, 512)), (2, slice(0, 512))]

    def move(sources, targets, sem):
        return [
            pltpu.make_async_copy(sources[n].at[0, :, columns], targets[n].at[0, :, columns], sem.at[i])
            for i, (n, columns) in enumerate(parts)
        ]

    loads, stores = move(ins, held, in_sem), move(held, outs, out_sem)
    for copy in loads:
        copy.start()
    for load, save in zip(loads, stores):
        load.wait()
        save.start()
    for copy in stores:
        copy.wait()


def on_device(*arguments):
    block = (2, 2, PROWS, 128)
    vmem = pl.BlockSpec(memory_space=pltpu.VMEM)
    hbm = pl.BlockSpec(memory_space=pltpu.HBM)
    results = pl.pallas_call(
        kernel,
        out_shape=(
            jax.ShapeDtypeStruct((1, ROWS, 4096), BF),
            jax.ShapeDtypeStruct((1, PROWS, 512), F32),
            jax.ShapeDtypeStruct((1, PROWS, 512), F32),
        ),
        in_specs=[hbm] * 10,
        out_specs=(hbm, vmem, vmem),
        scratch_shapes=[
            pltpu.VMEM((ROWS, HALF_Q), BF),
            pltpu.VMEM((ROWS, HALF_Q), BF),
            pltpu.VMEM((ROWS, HALF_Q), BF),
            pltpu.VMEM((ROWS, HALF_Q), BF),
            pltpu.VMEM((ROWS, HALF_Q), BF),
            pltpu.VMEM((ROWS, HALF_Q), BF),
            pltpu.VMEM((16, 256, 128), BF),
            pltpu.VMEM((16, 128, 256), BF),
            pltpu.VMEM((16, 256, 128), BF),
            pltpu.VMEM((16, 128, 256), BF),
            pltpu.VMEM((Z, 2, 2, ROWS, HALF_KV), BF),
            pltpu.VMEM((X, 2, 2, PROWS, 512), BF),
            pltpu.VMEM((3, 2, 2, PROWS, 128), BF),
            pltpu.VMEM((3, 2, 2, PROWS, 128), BF),
            pltpu.VMEM((2, Z) + block, BF),
            pltpu.VMEM((144, 1024), BF),
            pltpu.VMEM((16, 1, 256), F32),
            pltpu.VMEM((16, 144, 256), F32),
            pltpu.VMEM((16, 1, 256), F32),
            pltpu.VMEM((16, 1, 256), F32),
            pltpu.VMEM((2,) + block, F32),
            pltpu.VMEM((2, 2, 4) + block, BF),
            pltpu.VMEM((2, 2, 4) + block, BF),
            pltpu.VMEM((2, 2, PROWS, 128), BF),
            pltpu.VMEM((2, 2) + block, BF),
            pltpu.VMEM((2, 2) + block, BF),
            pltpu.VMEM((2, 2, 2) + block, BF),
            pltpu.VMEM((2, 2, 2) + block, BF),
            pltpu.SMEM((16,), jnp.int32),
            pltpu.SMEM((16,), jnp.int32),
            pltpu.SMEM((16,), jnp.int32),
            pltpu.SMEM((32,), jnp.int32),
            pltpu.SemaphoreType.DMA((COPIES,)),
            pltpu.SemaphoreType.DMA((COPIES,)),
            pltpu.SemaphoreType.DMA((16,)),
        ],
        compiler_params=pltpu.CompilerParams(
            collective_id=0, has_side_effects=True, vmem_limit_bytes=60 * 1024 * 1024
        ),
        cost_estimate=pl.CostEstimate(
            flops=10_000_000_000, bytes_accessed=8 * 1024 * 1024, transcendentals=17_000_000
        ),
    )(*arguments)
    return pl.pallas_call(
        copy_out,
        out_shape=tuple(jax.ShapeDtypeStruct(r.shape, r.dtype) for r in results),
        in_specs=[pl.BlockSpec(memory_space=pl.ANY)] * 3,
        out_specs=(hbm,) * 3,
        scratch_shapes=[pltpu.VMEM(r.shape, r.dtype) for r in results]
        + [pltpu.SemaphoreType.DMA((PIECES + 2,))] * 2,
        compiler_params=pltpu.CompilerParams(vmem_limit_bytes=60 * 1024 * 1024),
    )(*results)


def solution(mesh):
    split = P("dp", "blk", None)
    return jax.shard_map(
        on_device,
        mesh=mesh,
        in_specs=(split,) * 6 + (P(),) * 4,
        out_specs=(split, split, split),
        check_vma=False,
    )
```

```python
import jax
import jax.numpy as jnp
from jax import lax
from jax.experimental import pallas as pl
from jax.experimental.pallas import tpu as pltpu
from jax.sharding import PartitionSpec as P

MESH = pl.DeviceIdType.MESH
HEAD_WIDTH = 128
SCALE = HEAD_WIDTH ** (-0.5)
LOG2E = 1.4426950408889634
SCORE_SCALE = SCALE * LOG2E
MASKED = -1e30
LOWEST = -1e20
BF = jnp.bfloat16
F32 = jnp.float32

X, YH, CORES, YL, Z = 4, 2, 2, 2, 8
GROUP = 8
ROWS = 128
PROWS = 64
HALF_KV = 256
HALF_Q = 2048


def nt(a, b):
    return lax.dot_general(a, b, (((1,), (1,)), ((), ())), preferred_element_type=F32)


def nn(a, b):
    return lax.dot_general(a, b, (((1,), (0,)), ((), ())), preferred_element_type=F32)


def tn(a, b):
    return lax.dot_general(a, b, (((0,), (0,)), ((), ())), preferred_element_type=F32)


def kernel(
    q_ref, rk_ref, rv_ref, pk_ref, pv_ref, do_ref, owner_hbm, prompt_hbm, length_hbm, half_hbm,
    out_ref, gk_ref, gv_ref,
    q_near, q_far, do_near, do_far, out_near, out_far,
    resp_keys, resp_values, values_in, xbuf, chosen_out, chosen_in, prompt, v_turned,
    m_ref, acc_ref, lse_ref, delta_ref, gacc,
    zs_out, zs_in, share_out, share, core_in, xs_out, xs_in,
    owner_ref, prompt_ref, length_ref, half_ref,
    send_sem, recv_sem, local_sem,
):
    dp = lax.axis_index("dp")
    blk = lax.axis_index("blk")
    x, yh, c = dp // 4, (dp // 2) % 2, dp % 2
    yl, z = blk // Z, blk % Z
    other = 1 - yl
    y_id = (dp, other * Z + z)
    z_right, z_left = (dp, yl * Z + (z + 1) % Z), (dp, yl * Z + (z + Z - 1) % Z)
    x_right = (((x + 1) % X) * 4 + yh * 2 + c, blk)
    x_left = (((x + X - 1) % X) * 4 + yh * 2 + c, blk)
    core_id = (x * 4 + yh * 2 + (1 - c), blk)
    yh_id = (x * 4 + (1 - yh) * 2 + c, blk)
    diagonal_id = (x * 4 + (1 - yh) * 2 + c, other * Z + z)

    def lanes(which, width):
        return pl.ds(pl.multiple_of(which * width, width), width)

    def head_lanes(half, a):
        return pl.ds(pl.multiple_of(half * HALF_KV + a * 128, 128), 128)

    def group_lanes(half, a):
        return pl.ds(pl.multiple_of(half * HALF_Q + a * 1024, 1024), 1024)

    mine_kv, far_kv = lanes(yl, HALF_KV), lanes(other, HALF_KV)
    mine_q = lanes(yl, HALF_Q)

    fetched = []

    def fetch(src, dst):
        copy = pltpu.make_async_copy(src, dst, local_sem.at[len(fetched)])
        copy.start()
        fetched.append(copy)
        return copy

    def present(copies):
        for copy in copies:
            copy.wait()

    own_prompt = [
        fetch(ref.at[0], xbuf.at[x, c, kv]) for kv, ref in enumerate((pk_ref, pv_ref))
    ]
    own_resp = [
        fetch(rk_ref.at[0, :, mine_kv], resp_keys.at[z, yl]),
        fetch(rv_ref.at[0, :, mine_kv], values_in.at[yl]),
    ]
    tables = [
        fetch(owner_hbm, owner_ref), fetch(prompt_hbm, prompt_ref),
        fetch(length_hbm, length_ref), fetch(half_hbm, half_ref),
    ]
    own_q = fetch(q_ref.at[0, :, mine_q], q_near)
    own_do = fetch(do_ref.at[0, :, mine_q], do_near)

    barrier = pltpu.get_barrier_semaphore()
    peers = (y_id, z_right, z_left, x_right, x_left, core_id, yh_id, diagonal_id)
    for peer in peers:
        pl.semaphore_signal(barrier, inc=1, device_id=peer, device_id_type=MESH)
    pl.semaphore_wait(barrier, len(peers))

    started = []

    def send(src, dst, peer):
        index = len(started)
        copy = pltpu.make_async_remote_copy(
            src_ref=src, dst_ref=dst, send_sem=send_sem.at[index], recv_sem=recv_sem.at[index],
            device_id=peer, device_id_type=MESH,
        )
        copy.start()
        started.append(copy)
        return copy

    def arrive(copies):
        for copy in copies:
            copy.wait_recv()

    x0 = [
        send(ref.at[0], xbuf.at[x, c, kv], peer)
        for peer in (x_right, x_left)
        for kv, ref in enumerate((pk_ref, pv_ref))
    ]
    y_resp = [
        send(rk_ref.at[0, :, far_kv], resp_keys.at[z, yl], y_id),
        send(rv_ref.at[0, :, far_kv], values_in.at[yl], y_id),
    ]
    cores = [
        send(ref.at[0], xbuf.at[x, c, kv], core_id) for kv, ref in enumerate((pk_ref, pv_ref))
    ]
    y_q = [
        send(q_ref.at[0, :, group_lanes(other, a)], q_far.at[:, a * 1024 : a * 1024 + 1024], y_id)
        for a in range(2)
    ]

    def gather_step(slot, pos, n, step, right, left, halves=(0, 1)):
        final = step == n // 2 - 1
        copies = []
        for h in halves:
            for way, peer in enumerate((right, left)):
                if not final or h == way:
                    at = slot((pos + n - step) % n if way == 0 else (pos + step) % n, h)
                    copies.append(send(at, at, peer))
        return copies

    def resp_gather(step, h):
        return gather_step(lambda i, h: (resp_values if h else resp_keys).at[i], z, Z, step, z_right, z_left, (h,))

    def prompt_gather(a, step):
        return gather_step(lambda i, h: prompt.at[a, i, h], z, Z, step, z_right, z_left)

    def core_send(i):
        return send(xbuf.at[i, c], xbuf.at[i, c], core_id)

    def head_of(near, far, h):
        columns = pl.ds(pl.multiple_of(h * 128, 128), 128)
        return jnp.concatenate([near[:, columns], far[:, columns]], axis=0)

    def turn_values():
        for a in range(2):
            for y in range(2):
                resp_values[z, a, :, y * ROWS : (y + 1) * ROWS] = values_in[
                    y, :, a * 128 : (a + 1) * 128
                ].T

    present(tables)
    lane = lax.broadcasted_iota(jnp.int32, (1, 2 * ROWS), 1)
    last = length_ref[dp] - 1
    limit = jnp.zeros((1, 2 * ROWS), jnp.int32)
    for part, holder in enumerate((blk, other * Z + z)):
        for e in range(2):
            block = part * 2 + e
            inside = (lane >= block * 64) & (lane < block * 64 + 64)
            limit = jnp.where(inside, half_ref[2 * holder + e] * 64 + lane - block * 64, limit)
    limit = jnp.minimum(limit, last)
    down = lax.broadcasted_iota(jnp.int32, (64, 2 * ROWS), 0)

    def prompt_rows(slots, kv, a):
        return [prompt[a, i, kv].reshape(2 * PROWS, 128) for i in slots]

    def absorb(a, resp_slots, prompt_slots):
        bounds = []
        for i in resp_slots:
            for n in range(4):
                bounds.append(limit - half_ref[2 * ((n // 2) * Z + i) + n % 2] * 64)
        bounds += [None] * (2 * len(prompt_slots))
        count = 64 * len(bounds)

        keys = [
            resp_keys[i, :, :, a * 128 : (a + 1) * 128].reshape(2 * ROWS, 128) for i in resp_slots
        ] + prompt_rows(prompt_slots, 0, a)
        for n, part in enumerate(prompt_rows(prompt_slots, 1, a)):
            v_turned[:, n * 128 : n * 128 + 128] = part.T

        def score(query):
            pieces, tops, n = [], [], 0
            for part in keys:
                scores = nt(part, query) * SCORE_SCALE
                for m in range(part.shape[0] // 64):
                    piece = scores[64 * m : 64 * m + 64]
                    if bounds[n] is not None:
                        piece = jnp.where(down <= bounds[n], piece, MASKED)
                    tops.append(jnp.max(piece.reshape(8, 8, 2 * ROWS), axis=0))
                    pieces.append(piece)
                    n += 1
            while len(tops) > 1:
                tops = [
                    jnp.maximum(tops[i], tops[i + 1]) if i + 1 < len(tops) else tops[i]
                    for i in range(0, len(tops), 2)
                ]
            return jnp.concatenate(pieces, axis=0), jnp.max(tops[0], axis=0, keepdims=True)

        def body(t, carry):
            first = a * GROUP + t * 4
            heads = pl.ds(first, 4)
            values = [resp_values[i, a] for i in resp_slots]
            if prompt_slots:
                values.append(v_turned[:, : 128 * len(prompt_slots)])
            values = jnp.concatenate(values, axis=1) if len(values) > 1 else values[0]
            values = jnp.concatenate([values, jnp.ones((16, count), BF)], axis=0)
            old, old_mixed = m_ref[heads], acc_ref[heads]
            peaks, mixes = [], []

            def weigh(j, scores, top):
                peak = jnp.maximum(old[j], top)
                weights = jnp.exp2(scores - peak).astype(BF)
                peaks.append(peak)
                mixes.append(old_mixed[j] * jnp.exp2(old[j] - peak) + nn(values, weights))

            ready = score(head_of(q_near, q_far, first))
            for j in range(4):
                following = score(head_of(q_near, q_far, first + j + 1)) if j < 3 else None
                weigh(j, *ready)
                ready = following
            for j in range(4):
                m_ref[first + j] = peaks[j]
                acc_ref[first + j] = mixes[j]
            return carry

        lax.fori_loop(0, 2, body, 0)

    def finish(a):
        def body(t, carry):
            first = a * GROUP + t * 4
            heads = pl.ds(first, 4)
            peak, mixed = m_ref[heads], acc_ref[heads]
            outs, sums, deltas = [], [], []
            for j in range(4):
                total = mixed[j, 128:129]
                result = (mixed[j, :128] / total).T
                sums.append(peak[j] + jnp.log(total) * LOG2E)
                product = result * head_of(do_near, do_far, first + j).astype(F32)
                high = product.astype(BF)
                low = (product - high.astype(F32)).astype(BF)
                halves = jnp.concatenate([high, low], axis=1)
                deltas.append(nt(jnp.ones((16, 256), BF), halves)[:1])
                outs.append(result.astype(BF))
            for j in range(4):
                h = first + j
                lse_ref[h] = sums[j]
                delta_ref[h] = deltas[j]
                columns = pl.ds(pl.multiple_of(h * 128, 128), 128)
                out_near[:, columns] = outs[j][:ROWS]
                out_far[:, columns] = outs[j][ROWS:]
            return carry

        lax.fori_loop(0, 2, body, 0)
        return send(
            out_far.at[:, a * 1024 : a * 1024 + 1024], out_ref.at[0, :, group_lanes(yl, a)], y_id
        )

    def gradients(a, slots):
        keys = jnp.concatenate(prompt_rows(slots, 0, a), axis=0)
        values = jnp.concatenate(prompt_rows(slots, 1, a), axis=0)
        heads = range(a * GROUP, a * GROUP + GROUP)
        queries = [head_of(q_near, q_far, h) for h in heads]
        cotangents = [head_of(do_near, do_far, h) for h in heads]
        all_probs, all_slopes = [], []
        for h, query, cotangent in zip(heads, queries, cotangents):
            probs = jnp.exp2(nt(keys, query) * SCORE_SCALE - lse_ref[h])
            slopes = probs * (nt(values, cotangent) - delta_ref[h])
            all_probs.append(probs.astype(BF))
            all_slopes.append(slopes.astype(BF))
        queries = jnp.concatenate(queries, axis=0)
        cotangents = jnp.concatenate(cotangents, axis=0)
        key_part = nn(jnp.concatenate(all_slopes, axis=1), queries) * SCALE
        value_part = nn(jnp.concatenate(all_probs, axis=1), cotangents)
        for n in range(len(slots)):
            gacc[n, 0] = key_part[n * 128 : n * 128 + 128].reshape(2, PROWS, 128)
            gacc[n, 1] = value_part[n * 128 : n * 128 + 128].reshape(2, PROWS, 128)

    def scatter_step(own, outgoing, incoming, step, right, left):
        halves = ((0,), (1,)) if step == 0 else ((0, 1), (0, 1))
        before = ((0,), (1,)) if step == 1 else ((0, 1), (0, 1))
        copies = []
        for way, peer in enumerate((right, left)):
            for h in halves[way]:
                part = own(way, h)
                if step > 0 and h in before[way]:
                    part = part + incoming[way, step - 1, h].astype(F32)
                outgoing[way, step, h] = part.astype(BF)
                copies.append(send(outgoing.at[way, step, h], incoming.at[way, step, h], peer))
        return copies

    def z_scatter(a, step):
        own = (lambda way, h: gacc[0, h]) if step == 0 else (lambda way, h: gacc[way, h])
        return scatter_step(own, zs_out.at[a], zs_in.at[a], step, z_right, z_left)

    def to_y_ring(a):
        for h in range(2):
            for n, where in enumerate((yl, other)):
                total = gacc[0, h, where]
                for way in range(2):
                    total = total + zs_in[a, way, 3, h, where].astype(F32)
                (share.at[a, 0, 0] if n == 0 else share_out.at[a])[h] = total.astype(BF)
        return [
            send(share_out.at[a], share.at[a, 0, 1], y_id),
            send(share.at[a, 0, 0], share.at[a, 1, 0], yh_id),
            send(share_out.at[a], share.at[a, 1, 1], diagonal_id),
        ]

    def to_core(a):
        return [send(share.at[a], core_in.at[a], core_id)]

    owners = []
    for source_core in (c, 1 - c):
        for source_half in (yh, 1 - yh):
            owners.append(owner_ref[prompt_ref[x * 4 + source_half * 2 + source_core]])

    def destined(a, target, h):
        total = jnp.zeros((2, PROWS, 128), F32)
        for n, owner in enumerate(owners):
            part = (share if n < 2 else core_in)[a, n % 2, :, h].astype(F32)
            total = total + jnp.where(owner == target * 4 + yh * 2 + c, part, 0.0)
        return total

    def x_scatter(a, step):
        distance = 2 - step
        targets = ((x + distance) % X, (x + X - distance) % X)
        return scatter_step(
            lambda way, h: destined(a, targets[way], h),
            xs_out.at[a], xs_in.at[a], step, x_right, x_left,
        )

    def store(a):
        for h, ref in enumerate((gk_ref, gv_ref)):
            total = destined(a, x, h)
            for way in range(2):
                total = total + xs_in[a, way, 1, h].astype(F32)
            ref[0, :, head_lanes(yl, a)] = total[0]
            ref[0, :, head_lanes(other, a)] = total[1]

    drained = []

    def drain():
        for copy in started[len(drained) :]:
            copy.wait_send()
            drained.append(copy)

    m_ref[...] = jnp.full(m_ref.shape, LOWEST, F32)
    acc_ref[...] = jnp.zeros(acc_ref.shape, F32)

    def pair(step):
        return [(z + step) % Z, (z + Z - step) % Z]

    opposite = [(z + 4) % Z]
    p, r = [None, None], [None, None]

    def pass_on(step):
        for a in range(2):
            arrive(p[a])
            p[a] = prompt_gather(a, step)

    def pass_on_resp(step):
        for h in range(2):
            arrive(r[h])
            r[h] = resp_gather(step, h)

    arrive(x0)
    x1 = gather_step(lambda i, h: xbuf.at[i, c, h], x, X, 1, x_right, x_left)
    cores += [core_send((x + 1) % X), core_send((x + X - 1) % X)]
    present(own_resp)
    arrive([y_resp[0]])
    r[0] = resp_gather(0, 0)
    arrive([y_resp[1]])
    turn_values()
    r[1] = resp_gather(0, 1)
    arrive(x1)
    cores += [core_send((x + 2) % X)]
    present(own_prompt + [own_q, own_do])
    arrive(cores)
    theirs = owner_ref[prompt_ref[x * 4 + (1 - yh) * 2 + c]]
    mine = owner_ref[prompt_ref[dp]]

    def piece(owner, half, a):
        return xbuf[owner // 4, owner % 2, :, :, head_lanes(half, a)]

    ring = []
    for n, (owner, half, peer) in enumerate(
        ((mine, other, y_id), (theirs, yl, yh_id), (theirs, other, diagonal_id))
    ):
        for a in range(2):
            chosen_out[n, a] = piece(owner, half, a)
        ring.append(send(chosen_out.at[n], chosen_in.at[n], peer))
    arrive([y_q[0]])
    absorb(0, [z], [])
    pass_on_resp(1)
    arrive(ring)
    here = (mine // 2) % 2 == yh
    for a in range(2):
        for kv in range(2):
            prompt[a, z, kv, yl] = jnp.where(here, piece(mine, yl, a)[kv], chosen_in[1, a, kv])
            prompt[a, z, kv, other] = jnp.where(here, chosen_in[0, a, kv], chosen_in[2, a, kv])
        p[a] = prompt_gather(a, 0)
    y_do = [
        send(do_ref.at[0, :, group_lanes(other, a)], do_far.at[:, a * 1024 : a * 1024 + 1024], y_id)
        for a in range(2)
    ]
    absorb(0, pair(1), [])
    arrive([y_q[1]])
    absorb(1, [z] + pair(1), [])
    pass_on(1)
    pass_on_resp(2)
    absorb(0, pair(2), [])
    pass_on(2)
    absorb(1, pair(2), [])
    pass_on_resp(3)
    pass_on(3)
    absorb(0, pair(3), [])
    absorb(1, pair(3), [])
    drain()
    for h in range(2):
        arrive(r[h])
    absorb(0, opposite, [z] + pair(1) + pair(2))
    arrive([y_do[0]])
    arrive(p[0])
    absorb(0, [], pair(3) + opposite)
    results = [finish(0)]
    gradients(0, opposite)
    s0 = z_scatter(0, 0)
    absorb(1, opposite, [z] + pair(1) + pair(2))
    gradients(0, pair(3))
    arrive(s0)
    s0 = z_scatter(0, 1)
    arrive([y_do[1]])
    arrive(p[1])
    absorb(1, [], pair(3) + opposite)
    results += [finish(1)]
    own_result = fetch(out_near, out_ref.at[0, :, mine_q])
    gradients(1, opposite)
    s1 = z_scatter(1, 0)
    gradients(0, pair(2))
    arrive(s0)
    s0 = z_scatter(0, 2)
    gradients(1, pair(3))
    arrive(s1)
    s1 = z_scatter(1, 1)
    gradients(0, pair(1))
    arrive(s0)
    s0 = z_scatter(0, 3)
    gradients(1, pair(2))
    arrive(s1)
    s1 = z_scatter(1, 2)
    gradients(0, [z])
    arrive(s0)

    t0 = to_y_ring(0)
    gradients(1, pair(1))
    arrive(s1)
    s1 = z_scatter(1, 3)
    arrive(t0)
    t0 = to_core(0)
    gradients(1, [z])
    arrive(t0)
    t0 = x_scatter(0, 0)
    arrive(s1)
    t1 = to_y_ring(1)
    arrive(t0)
    t0 = x_scatter(0, 1)
    arrive(t1)
    t1 = to_core(1)
    drain()
    arrive(t1)
    t1 = x_scatter(1, 0)
    arrive(t0)
    store(0)
    arrive(t1)
    t1 = x_scatter(1, 1)
    arrive(results)
    present([own_result])
    drain()
    arrive(t1)
    store(1)


COPIES = 128


PIECES = 4


def copy_out(*refs):
    ins, outs, held = refs[:3], refs[3:6], refs[6:9]
    in_sem, out_sem = refs[9:]
    parts = [(0, slice(n * 1024, n * 1024 + 1024)) for n in range(PIECES)]
    parts += [(1, slice(0, 512)), (2, slice(0, 512))]

    def move(sources, targets, sem):
        return [
            pltpu.make_async_copy(sources[n].at[0, :, columns], targets[n].at[0, :, columns], sem.at[i])
            for i, (n, columns) in enumerate(parts)
        ]

    loads, stores = move(ins, held, in_sem), move(held, outs, out_sem)
    for copy in loads:
        copy.start()
    for load, save in zip(loads, stores):
        load.wait()
        save.start()
    for copy in stores:
        copy.wait()


def on_device(*arguments):
    block = (2, 2, PROWS, 128)
    vmem = pl.BlockSpec(memory_space=pltpu.VMEM)
    hbm = pl.BlockSpec(memory_space=pltpu.HBM)
    results = pl.pallas_call(
        kernel,
        out_shape=(
            jax.ShapeDtypeStruct((1, ROWS, 4096), BF),
            jax.ShapeDtypeStruct((1, PROWS, 512), F32),
            jax.ShapeDtypeStruct((1, PROWS, 512), F32),
        ),
        in_specs=[hbm] * 10,
        out_specs=(hbm, vmem, vmem),
        scratch_shapes=[
            pltpu.VMEM((ROWS, HALF_Q), BF),
            pltpu.VMEM((ROWS, HALF_Q), BF),
            pltpu.VMEM((ROWS, HALF_Q), BF),
            pltpu.VMEM((ROWS, HALF_Q), BF),
            pltpu.VMEM((ROWS, HALF_Q), BF),
            pltpu.VMEM((ROWS, HALF_Q), BF),
            pltpu.VMEM((Z, 2, ROWS, HALF_KV), BF),
            pltpu.VMEM((Z, 2, 128, 2 * ROWS), BF),
            pltpu.VMEM((2, ROWS, HALF_KV), BF),
            pltpu.VMEM((X, 2, 2, PROWS, 512), BF),
            pltpu.VMEM((3, 2, 2, PROWS, 128), BF),
            pltpu.VMEM((3, 2, 2, PROWS, 128), BF),
            pltpu.VMEM((2, Z) + block, BF),
            pltpu.VMEM((128, 1024), BF),
            pltpu.VMEM((16, 1, 256), F32),
            pltpu.VMEM((16, 144, 256), F32),
            pltpu.VMEM((16, 1, 256), F32),
            pltpu.VMEM((16, 1, 256), F32),
            pltpu.VMEM((2,) + block, F32),
            pltpu.VMEM((2, 2, 4) + block, BF),
            pltpu.VMEM((2, 2, 4) + block, BF),
            pltpu.VMEM((2, 2, PROWS, 128), BF),
            pltpu.VMEM((2, 2) + block, BF),
            pltpu.VMEM((2, 2) + block, BF),
            pltpu.VMEM((2, 2, 2) + block, BF),
            pltpu.VMEM((2, 2, 2) + block, BF),
            pltpu.SMEM((16,), jnp.int32),
            pltpu.SMEM((16,), jnp.int32),
            pltpu.SMEM((16,), jnp.int32),
            pltpu.SMEM((32,), jnp.int32),
            pltpu.SemaphoreType.DMA((COPIES,)),
            pltpu.SemaphoreType.DMA((COPIES,)),
            pltpu.SemaphoreType.DMA((16,)),
        ],
        compiler_params=pltpu.CompilerParams(
            collective_id=0, has_side_effects=True, vmem_limit_bytes=60 * 1024 * 1024
        ),
        cost_estimate=pl.CostEstimate(
            flops=10_000_000_000, bytes_accessed=8 * 1024 * 1024, transcendentals=17_000_000
        ),
    )(*arguments)
    return pl.pallas_call(
        copy_out,
        out_shape=tuple(jax.ShapeDtypeStruct(r.shape, r.dtype) for r in results),
        in_specs=[pl.BlockSpec(memory_space=pl.ANY)] * 3,
        out_specs=(hbm,) * 3,
        scratch_shapes=[pltpu.VMEM(r.shape, r.dtype) for r in results]
        + [pltpu.SemaphoreType.DMA((PIECES + 2,))] * 2,
        compiler_params=pltpu.CompilerParams(vmem_limit_bytes=60 * 1024 * 1024),
    )(*results)


def solution(mesh):
    split = P("dp", "blk", None)
    return jax.shard_map(
        on_device,
        mesh=mesh,
        in_specs=(split,) * 6 + (P(),) * 4,
        out_specs=(split, split, split),
        check_vma=False,
    )
```

```python
import jax
import jax.numpy as jnp
from jax import lax
from jax.experimental import pallas as pl
from jax.experimental.pallas import tpu as pltpu
from jax.sharding import PartitionSpec as P

MESH = pl.DeviceIdType.MESH
HEAD_WIDTH = 128
SCALE = HEAD_WIDTH ** (-0.5)
LOG2E = 1.4426950408889634
SCORE_SCALE = SCALE * LOG2E
MASKED = -1e30
LOWEST = -1e20
BF = jnp.bfloat16
F32 = jnp.float32

X, YH, CORES, YL, Z = 4, 2, 2, 2, 8
GROUP = 8
ROWS = 128
PROWS = 64
HALF_KV = 256
HALF_Q = 2048


def nt(a, b):
    return lax.dot_general(a, b, (((1,), (1,)), ((), ())), preferred_element_type=F32)


def nn(a, b):
    return lax.dot_general(a, b, (((1,), (0,)), ((), ())), preferred_element_type=F32)


def tn(a, b):
    return lax.dot_general(a, b, (((0,), (0,)), ((), ())), preferred_element_type=F32)


def kernel(
    q_ref, rk_ref, rv_ref, pk_ref, pv_ref, do_ref, owner_hbm, prompt_hbm, length_hbm, half_hbm,
    out_ref, gk_ref, gv_ref,
    q_near, q_far, do_near, do_far, out_near, out_far,
    resp_keys, resp_values, values_in, xbuf, chosen_out, chosen_in, prompt, limit_ref,
    m_ref, acc_ref, lse_ref, delta_ref, gacc,
    zs_out, zs_in, share_out, share, core_in, xs_out, xs_in,
    owner_ref, prompt_ref, length_ref, half_ref,
    send_sem, recv_sem, local_sem,
):
    dp = lax.axis_index("dp")
    blk = lax.axis_index("blk")
    x, yh, c = dp // 4, (dp // 2) % 2, dp % 2
    yl, z = blk // Z, blk % Z
    other = 1 - yl
    y_id = (dp, other * Z + z)
    z_right, z_left = (dp, yl * Z + (z + 1) % Z), (dp, yl * Z + (z + Z - 1) % Z)
    x_right = (((x + 1) % X) * 4 + yh * 2 + c, blk)
    x_left = (((x + X - 1) % X) * 4 + yh * 2 + c, blk)
    core_id = (x * 4 + yh * 2 + (1 - c), blk)
    yh_id = (x * 4 + (1 - yh) * 2 + c, blk)
    diagonal_id = (x * 4 + (1 - yh) * 2 + c, other * Z + z)

    def lanes(which, width):
        return pl.ds(pl.multiple_of(which * width, width), width)

    def head_lanes(half, a):
        return pl.ds(pl.multiple_of(half * HALF_KV + a * 128, 128), 128)

    def group_lanes(half, a):
        return pl.ds(pl.multiple_of(half * HALF_Q + a * 1024, 1024), 1024)

    mine_kv, far_kv = lanes(yl, HALF_KV), lanes(other, HALF_KV)
    mine_q = lanes(yl, HALF_Q)

    fetched = []

    def fetch(src, dst):
        copy = pltpu.make_async_copy(src, dst, local_sem.at[len(fetched)])
        copy.start()
        fetched.append(copy)
        return copy

    def present(copies):
        for copy in copies:
            copy.wait()

    own_prompt = [
        fetch(ref.at[0], xbuf.at[x, c, kv]) for kv, ref in enumerate((pk_ref, pv_ref))
    ]
    own_resp = [
        fetch(rk_ref.at[0, :, mine_kv], resp_keys.at[z, yl]),
        fetch(rv_ref.at[0, :, mine_kv], values_in.at[yl]),
    ]
    tables = [
        fetch(owner_hbm, owner_ref), fetch(prompt_hbm, prompt_ref),
        fetch(length_hbm, length_ref), fetch(half_hbm, half_ref),
    ]
    own_q = fetch(q_ref.at[0, :, mine_q], q_near)
    own_do = fetch(do_ref.at[0, :, mine_q], do_near)

    barrier = pltpu.get_barrier_semaphore()
    peers = (y_id, z_right, z_left, x_right, x_left, core_id, yh_id, diagonal_id)
    for peer in peers:
        pl.semaphore_signal(barrier, inc=1, device_id=peer, device_id_type=MESH)
    pl.semaphore_wait(barrier, len(peers))

    total = [0]

    def room(n):
        total[0] += n
        return total[0] - n

    def copy(index, src, dst, peer):
        return pltpu.make_async_remote_copy(
            src_ref=src, dst_ref=dst, send_sem=send_sem.at[index], recv_sem=recv_sem.at[index],
            device_id=peer, device_id_type=MESH,
        )

    def start(copies):
        for one in copies:
            one.start()

    def arrive(copies):
        for one in copies:
            one.wait_recv()

    def drain(copies):
        for one in copies:
            one.wait_send()

    def gather(base, slot, pos, n, step, right, left, halves):
        copies = []
        for h in halves:
            for way, peer in enumerate((right, left)):
                if step < n // 2 - 1 or h == way:
                    at = slot((pos + n - step) % n if way == 0 else (pos + step) % n, h)
                    copies.append(copy(base + h * 2 + way, at, at, peer))
        return copies

    x_base, core_base, ys_base, yq_base, yd_base = room(8), room(5), room(2), room(2), room(2)
    ring_base, r_base, p_base, result_base = room(3), room(16), room(32), room(2)
    zs_base, yr_base, cs_base, xs_base = room(32), room(6), room(2), room(16)

    def x_copies(step):
        if step == 0:
            return [
                copy(x_base + kv * 2 + way, ref.at[0], xbuf.at[x, c, kv], peer)
                for way, peer in enumerate((x_right, x_left))
                for kv, ref in enumerate((pk_ref, pv_ref))
            ]
        return gather(
            x_base + 4, lambda i, h: xbuf.at[i, c, h], x, X, 1, x_right, x_left, (0, 1)
        )

    def core_copies(which):
        if which == 0:
            return [
                copy(core_base + kv, ref.at[0], xbuf.at[x, c, kv], core_id)
                for kv, ref in enumerate((pk_ref, pv_ref))
            ]
        slots = ((x + 1) % X, (x + X - 1) % X) if which == 1 else ((x + 2) % X,)
        return [
            copy(core_base + which * 2 + n, xbuf.at[i, c], xbuf.at[i, c], core_id)
            for n, i in enumerate(slots)
        ]

    y_resp = [
        copy(ys_base, rk_ref.at[0, :, far_kv], resp_keys.at[z, yl], y_id),
        copy(ys_base + 1, rv_ref.at[0, :, far_kv], values_in.at[yl], y_id),
    ]

    def y_group(base, ref, far):
        return [
            copy(base + a, ref.at[0, :, group_lanes(other, a)], far.at[:, a * 1024 : a * 1024 + 1024], y_id)
            for a in range(2)
        ]

    y_q, y_do = y_group(yq_base, q_ref, q_far), y_group(yd_base, do_ref, do_far)
    ring = [
        copy(ring_base + n, chosen_out.at[n], chosen_in.at[n], peer)
        for n, peer in enumerate((y_id, yh_id, diagonal_id))
    ]

    def r_copies(step, h):
        return gather(
            r_base + step * 4, lambda i, h: (resp_values if h else resp_keys).at[i],
            z, Z, step, z_right, z_left, (h,),
        )

    def p_copies(a, step):
        return gather(
            p_base + a * 16 + step * 4, lambda i, h: prompt.at[a, i, h],
            z, Z, step, z_right, z_left, (0, 1),
        )

    def result_copies(a):
        columns = pl.ds(pl.multiple_of(a * 1024, 1024), 1024)
        return [copy(result_base + a, out_far.at[:, columns], out_ref.at[0, :, group_lanes(yl, a)], y_id)]

    def sums(base, outgoing, incoming, a, step, right, left):
        return [
            copy(
                base + step * 4 + way * 2 + h,
                outgoing.at[a, way, step, h], incoming.at[a, way, step, h], peer,
            )
            for way, peer in enumerate((right, left))
            for h in range(2)
            if step > 0 or h == way
        ]

    def zs_copies(a, step):
        return sums(zs_base + a * 16, zs_out, zs_in, a, step, z_right, z_left)

    def xs_copies(a, step):
        return sums(xs_base + a * 8, xs_out, xs_in, a, step, x_right, x_left)

    def yr_copies(a):
        return [
            copy(yr_base + a * 3, share_out.at[a], share.at[a, 0, 1], y_id),
            copy(yr_base + a * 3 + 1, share.at[a, 0, 0], share.at[a, 1, 0], yh_id),
            copy(yr_base + a * 3 + 2, share_out.at[a], share.at[a, 1, 1], diagonal_id),
        ]

    def cs_copies(a):
        return [copy(cs_base + a, share.at[a], core_in.at[a], core_id)]

    def head_of(near, far, h):
        columns = pl.ds(pl.multiple_of(h * 128, 128), 128)
        return jnp.concatenate([near[:, columns], far[:, columns]], axis=0)

    def loop(count, body):
        def step(i, carry):
            body(i)
            return carry

        lax.fori_loop(0, count, step, 0)

    start(x_copies(0))
    start(y_resp)
    start(core_copies(0))
    start(y_q)

    present(tables)
    lane = lax.broadcasted_iota(jnp.int32, (1, 2 * ROWS), 1)
    last = length_ref[dp] - 1
    limit = jnp.zeros((1, 2 * ROWS), jnp.int32)
    for part, holder in enumerate((blk, other * Z + z)):
        for e in range(2):
            block = part * 2 + e
            inside = (lane >= block * 64) & (lane < block * 64 + 64)
            limit = jnp.where(inside, half_ref[2 * holder + e] * 64 + lane - block * 64, limit)
    limit_ref[...] = jnp.minimum(limit, last)
    m_ref[...] = jnp.full(m_ref.shape, LOWEST, F32)
    acc_ref[...] = jnp.zeros(acc_ref.shape, F32)

    def absorb(a, keys, values, bounds):
        def score(query):
            pieces, tops = [], []
            down = lax.broadcasted_iota(jnp.int32, (64, 2 * ROWS), 0)
            for part, offset in zip(keys, range(0, 64 * len(bounds), keys[0].shape[0])):
                scores = nt(part, query) * SCORE_SCALE
                for m in range(part.shape[0] // 64):
                    piece, bound = scores[64 * m : 64 * m + 64], bounds[offset // 64 + m]
                    if bound is not None:
                        piece = jnp.where(down <= bound, piece, MASKED)
                    tops.append(jnp.max(piece.reshape(8, 8, 2 * ROWS), axis=0))
                    pieces.append(piece)
            while len(tops) > 1:
                tops = [jnp.maximum(tops[i], tops[i + 1]) for i in range(0, len(tops), 2)]
            return jnp.concatenate(pieces, axis=0), jnp.max(tops[0], axis=0, keepdims=True)

        values = jnp.concatenate([values, jnp.ones((16, 64 * len(bounds)), BF)], axis=0)

        def body(t):
            first = a * GROUP + t * UNROLL
            heads = pl.ds(first, UNROLL)
            old, old_mixed = m_ref[heads], acc_ref[heads]
            peaks, mixes = [], []

            def weigh(j, scores, top):
                peak = jnp.maximum(old[j], top)
                weights = jnp.exp2(scores - peak).astype(BF)
                peaks.append(peak)
                mixes.append(old_mixed[j] * jnp.exp2(old[j] - peak) + nn(values, weights))

            ready = score(head_of(q_near, q_far, first))
            for j in range(UNROLL):
                following = score(head_of(q_near, q_far, first + j + 1)) if j < UNROLL - 1 else None
                weigh(j, *ready)
                ready = following
            for j in range(UNROLL):
                m_ref[first + j] = peaks[j]
                acc_ref[first + j] = mixes[j]

        loop(GROUP // UNROLL, body)

    def absorb_resp(a, slots):
        columns = pl.ds(pl.multiple_of(a * 128, 128), 128)
        keys = [resp_keys[i, :, :, columns].reshape(2 * ROWS, 128) for i in slots]
        values = jnp.concatenate([resp_values[i, a] for i in slots], axis=1)
        limit = limit_ref[...]
        bounds = [
            limit - half_ref[2 * ((n // 2) * Z + i) + n % 2] * 64 for i in slots for n in range(4)
        ]
        absorb(a, keys, values, bounds)

    def absorb_prompt(a, slots):
        keys = jnp.concatenate([prompt[a, i, 0].reshape(2 * PROWS, 128) for i in slots], axis=0)
        values = [prompt[a, i, 1].reshape(2 * PROWS, 128).T for i in slots]
        absorb(a, [keys], jnp.concatenate(values, axis=1), [None] * (2 * len(slots)))

    def finish(a):
        def body(t):
            first = a * GROUP + t * UNROLL
            heads = pl.ds(first, UNROLL)
            peak, mixed = m_ref[heads], acc_ref[heads]
            outs, logs, deltas = [], [], []
            for j in range(UNROLL):
                total = mixed[j, 128:129]
                result = (mixed[j, :128] / total).T
                logs.append(peak[j] + jnp.log(total) * LOG2E)
                product = result * head_of(do_near, do_far, first + j).astype(F32)
                high = product.astype(BF)
                low = (product - high.astype(F32)).astype(BF)
                halves = jnp.concatenate([high, low], axis=1)
                deltas.append(nt(jnp.ones((16, 256), BF), halves)[:1])
                outs.append(result.astype(BF))
            for j in range(UNROLL):
                h = first + j
                lse_ref[h] = logs[j]
                delta_ref[h] = deltas[j]
                columns = pl.ds(pl.multiple_of(h * 128, 128), 128)
                out_near[:, columns] = outs[j][:ROWS]
                out_far[:, columns] = outs[j][ROWS:]

        loop(GROUP // UNROLL, body)

    def gradients(a, k, slots):
        keys = jnp.concatenate([prompt[a, i, 0].reshape(2 * PROWS, 128) for i in slots], axis=0)
        values = jnp.concatenate([prompt[a, i, 1].reshape(2 * PROWS, 128) for i in slots], axis=0)
        heads = [a * GROUP + j for j in range(GROUP)]
        queries = [head_of(q_near, q_far, h) for h in heads]
        cotangents = [head_of(do_near, do_far, h) for h in heads]
        all_probs, all_slopes = [], []
        for h, query, cotangent in zip(heads, queries, cotangents):
            probs = jnp.exp2(nt(keys, query) * SCORE_SCALE - lse_ref[h])
            slopes = probs * (nt(values, cotangent) - delta_ref[h])
            all_probs.append(probs.astype(BF))
            all_slopes.append(slopes.astype(BF))
        queries = jnp.concatenate(queries, axis=0)
        cotangents = jnp.concatenate(cotangents, axis=0)
        key_part = nn(jnp.concatenate(all_slopes, axis=1), queries) * SCALE
        value_part = nn(jnp.concatenate(all_probs, axis=1), cotangents)
        for n in range(2):
            gacc[a, k, n, 0] = key_part[n * 128 : n * 128 + 128].reshape(2, PROWS, 128)
            gacc[a, k, n, 1] = value_part[n * 128 : n * 128 + 128].reshape(2, PROWS, 128)

    def z_messages(a, step):
        for way in range(2):
            for h in range(2):
                if step > 0 or h == way:
                    if way == 0 and step > 0:
                        part = gacc[a, step - 1, 1, h]
                    else:
                        part = gacc[a, step, 0, h]
                    if step > 1 or (step == 1 and h == way):
                        part = part + zs_in[a, way, step - 1, h].astype(F32)
                    zs_out[a, way, step, h] = part.astype(BF)
        start(zs_copies(a, step))

    def to_y_ring(a):
        for h in range(2):
            for n, where in enumerate((yl, other)):
                part = gacc[a, 3, 1, h, where]
                for way in range(2):
                    part = part + zs_in[a, way, 3, h, where].astype(F32)
                (share.at[a, 0, 0] if n == 0 else share_out.at[a])[h] = part.astype(BF)
        start(yr_copies(a))

    def destined(a, target, h):
        result = jnp.zeros((2, PROWS, 128), F32)
        for n in range(4):
            source = x * 4 + (yh if n % 2 == 0 else 1 - yh) * 2 + (c if n < 2 else 1 - c)
            owner = owner_ref[prompt_ref[source]]
            part = (share if n < 2 else core_in)[a, n % 2, :, h].astype(F32)
            result = result + jnp.where(owner == target * 4 + yh * 2 + c, part, 0.0)
        return result

    def x_messages(a, step):
        for way in range(2):
            distance = 2 - step
            target = (x + distance) % X if way == 0 else (x + X - distance) % X
            for h in range(2):
                if step > 0 or h == way:
                    part = destined(a, target, h)
                    if step == 1 and h == way:
                        part = part + xs_in[a, way, 0, h].astype(F32)
                    xs_out[a, way, step, h] = part.astype(BF)
        start(xs_copies(a, step))

    def store(a):
        for h, ref in enumerate((gk_ref, gv_ref)):
            part = destined(a, x, h)
            for way in range(2):
                part = part + xs_in[a, way, 1, h].astype(F32)
            ref[0, :, head_lanes(yl, a)] = part[0]
            ref[0, :, head_lanes(other, a)] = part[1]

    arrive(x_copies(0))
    start(x_copies(1))
    start(core_copies(1))
    present(own_resp)
    arrive(y_resp[:1])
    start(r_copies(0, 0))
    arrive(y_resp[1:])
    for a in range(2):
        for y in range(2):
            resp_values[z, a, :, y * ROWS : (y + 1) * ROWS] = values_in[
                y, :, a * 128 : (a + 1) * 128
            ].T
    start(r_copies(0, 1))
    arrive(x_copies(1))
    start(core_copies(2))
    present(own_prompt + [own_q, own_do])
    for which in range(3):
        arrive(core_copies(which))
    theirs = owner_ref[prompt_ref[x * 4 + (1 - yh) * 2 + c]]
    mine = owner_ref[prompt_ref[dp]]

    def piece(owner, half, a):
        return xbuf[owner // 4, owner % 2, :, :, head_lanes(half, a)]

    for n, (owner, half) in enumerate(((mine, other), (theirs, yl), (theirs, other))):
        for a in range(2):
            chosen_out[n, a] = piece(owner, half, a)
        start(ring[n : n + 1])

    def pass_on(step):
        for a in range(2):
            arrive(p_copies(a, step - 1))
            start(p_copies(a, step))

    def resp_unit(u):
        a, s = u % 2, u // 2

        @pl.when(u == 0)
        def _():
            arrive(y_q[:1])

        @pl.when(u == 1)
        def _():
            arrive(y_q[1:])
            arrive(ring)
            here = (mine // 2) % 2 == yh
            for a in range(2):
                for kv in range(2):
                    prompt[a, z, kv, yl] = jnp.where(
                        here, piece(mine, yl, a)[kv], chosen_in[1, a, kv]
                    )
                    prompt[a, z, kv, other] = jnp.where(
                        here, chosen_in[0, a, kv], chosen_in[2, a, kv]
                    )
                start(p_copies(a, 0))
            start(y_do)

        for step in range(1, 5):

            @pl.when(u == 2 * step - 2)
            def _():
                for h in range(2):
                    arrive(r_copies(step - 1, h))
                    if step < 4:
                        start(r_copies(step, h))

            if step < 4:

                @pl.when(u == 2 * step + 1)
                def _():
                    pass_on(step)

        absorb_resp(a, [(z + Z - s) % Z, (z + s + 1) % Z])

    loop(8, resp_unit)
    arrive(y_do)

    def key_head(a):
        def prompt_unit(w):
            @pl.when(w == 1)
            def _():
                arrive(p_copies(a, 3))

            sign = 1 - 2 * w
            absorb_prompt(
                a,
                [(z + 4 * w) % Z, (z + Z + 4 * w + sign) % Z, (z + Z - 4 * w - sign) % Z, (z + 2 + 4 * w) % Z],
            )

        loop(2, prompt_unit)

        @pl.when(a == 1)
        def _():
            arrive(zs_copies(0, 3))
            to_y_ring(0)

        finish(a)
        start(result_copies(a))

        @pl.when(a == 1)
        def _():
            arrive(yr_copies(0))
            start(cs_copies(0))

        def gradient_unit(k):
            gradients(a, k, [(z + 4 + k) % Z, (z + 3 + Z - k) % Z])
            for step in range(4):

                @pl.when(k == step)
                def _():
                    if step > 0:
                        arrive(zs_copies(a, step - 1))
                    z_messages(a, step)

            for step in range(3):

                @pl.when((a == 1) & (k == step))
                def _():
                    if step == 0:
                        arrive(cs_copies(0))
                        x_messages(0, 0)
                    elif step == 1:
                        arrive(xs_copies(0, 0))
                        x_messages(0, 1)
                    else:
                        arrive(xs_copies(0, 1))
                        store(0)

        loop(4, gradient_unit)

    loop(2, key_head)
    own_result = fetch(out_near, out_ref.at[0, :, mine_q])

    early = [x_copies(0), x_copies(1), core_copies(0), core_copies(1), core_copies(2)]
    early += [y_resp, y_q, y_do, ring, zs_copies(0, 3), yr_copies(0), cs_copies(0)]
    for step in range(4):
        early += [r_copies(step, h) for h in range(2)] + [p_copies(a, step) for a in range(2)]
    for step in range(3):
        early += [zs_copies(a, step) for a in range(2)]
    early += [xs_copies(0, 0), xs_copies(0, 1)]
    for copies in early[: len(early) // 2]:
        drain(copies)
    arrive(zs_copies(1, 3))
    to_y_ring(1)
    for copies in early[len(early) // 2 :]:
        drain(copies)
    arrive(yr_copies(1))
    start(cs_copies(1))
    drain(zs_copies(1, 3))
    for a in range(2):
        arrive(result_copies(a))
        drain(result_copies(a))
    present([own_result])
    arrive(cs_copies(1))
    x_messages(1, 0)
    drain(yr_copies(1) + cs_copies(1))
    arrive(xs_copies(1, 0))
    x_messages(1, 1)
    drain(xs_copies(1, 0))
    arrive(xs_copies(1, 1))
    store(1)
    drain(xs_copies(1, 1))


COPIES = 128
UNROLL = 4
PIECES = 4


def copy_out(*refs):
    ins, outs, held = refs[:3], refs[3:6], refs[6:9]
    in_sem, out_sem = refs[9:]
    parts = [(0, slice(n * 1024, n * 1024 + 1024)) for n in range(PIECES)]
    parts += [(1, slice(0, 512)), (2, slice(0, 512))]

    def move(sources, targets, sem):
        return [
            pltpu.make_async_copy(sources[n].at[0, :, columns], targets[n].at[0, :, columns], sem.at[i])
            for i, (n, columns) in enumerate(parts)
        ]

    loads, stores = move(ins, held, in_sem), move(held, outs, out_sem)
    for copy in loads:
        copy.start()
    for load, save in zip(loads, stores):
        load.wait()
        save.start()
    for copy in stores:
        copy.wait()


def on_device(*arguments):
    block = (2, 2, PROWS, 128)
    vmem = pl.BlockSpec(memory_space=pltpu.VMEM)
    hbm = pl.BlockSpec(memory_space=pltpu.HBM)
    results = pl.pallas_call(
        kernel,
        out_shape=(
            jax.ShapeDtypeStruct((1, ROWS, 4096), BF),
            jax.ShapeDtypeStruct((1, PROWS, 512), F32),
            jax.ShapeDtypeStruct((1, PROWS, 512), F32),
        ),
        in_specs=[hbm] * 10,
        out_specs=(hbm, vmem, vmem),
        scratch_shapes=[
            pltpu.VMEM((ROWS, HALF_Q), BF),
            pltpu.VMEM((ROWS, HALF_Q), BF),
            pltpu.VMEM((ROWS, HALF_Q), BF),
            pltpu.VMEM((ROWS, HALF_Q), BF),
            pltpu.VMEM((ROWS, HALF_Q), BF),
            pltpu.VMEM((ROWS, HALF_Q), BF),
            pltpu.VMEM((Z, 2, ROWS, HALF_KV), BF),
            pltpu.VMEM((Z, 2, 128, 2 * ROWS), BF),
            pltpu.VMEM((2, ROWS, HALF_KV), BF),
            pltpu.VMEM((X, 2, 2, PROWS, 512), BF),
            pltpu.VMEM((3, 2, 2, PROWS, 128), BF),
            pltpu.VMEM((3, 2, 2, PROWS, 128), BF),
            pltpu.VMEM((2, Z) + block, BF),
            pltpu.VMEM((1, 2 * ROWS), jnp.int32),
            pltpu.VMEM((16, 1, 256), F32),
            pltpu.VMEM((16, 144, 256), F32),
            pltpu.VMEM((16, 1, 256), F32),
            pltpu.VMEM((16, 1, 256), F32),
            pltpu.VMEM((2, 4, 2) + block, F32),
            pltpu.VMEM((2, 2, 4) + block, BF),
            pltpu.VMEM((2, 2, 4) + block, BF),
            pltpu.VMEM((2, 2, PROWS, 128), BF),
            pltpu.VMEM((2, 2) + block, BF),
            pltpu.VMEM((2, 2) + block, BF),
            pltpu.VMEM((2, 2, 2) + block, BF),
            pltpu.VMEM((2, 2, 2) + block, BF),
            pltpu.SMEM((16,), jnp.int32),
            pltpu.SMEM((16,), jnp.int32),
            pltpu.SMEM((16,), jnp.int32),
            pltpu.SMEM((32,), jnp.int32),
            pltpu.SemaphoreType.DMA((COPIES,)),
            pltpu.SemaphoreType.DMA((COPIES,)),
            pltpu.SemaphoreType.DMA((16,)),
        ],
        compiler_params=pltpu.CompilerParams(
            collective_id=0, has_side_effects=True, vmem_limit_bytes=60 * 1024 * 1024
        ),
        cost_estimate=pl.CostEstimate(
            flops=10_000_000_000, bytes_accessed=8 * 1024 * 1024, transcendentals=17_000_000
        ),
    )(*arguments)
    return pl.pallas_call(
        copy_out,
        out_shape=tuple(jax.ShapeDtypeStruct(r.shape, r.dtype) for r in results),
        in_specs=[pl.BlockSpec(memory_space=pl.ANY)] * 3,
        out_specs=(hbm,) * 3,
        scratch_shapes=[pltpu.VMEM(r.shape, r.dtype) for r in results]
        + [pltpu.SemaphoreType.DMA((PIECES + 2,))] * 2,
        compiler_params=pltpu.CompilerParams(vmem_limit_bytes=60 * 1024 * 1024),
    )(*results)


def solution(mesh):
    split = P("dp", "blk", None)
    return jax.shard_map(
        on_device,
        mesh=mesh,
        in_specs=(split,) * 6 + (P(),) * 4,
        out_specs=(split, split, split),
        check_vma=False,
    )
```

```python
import jax
import jax.numpy as jnp
from jax import lax
from jax.experimental import pallas as pl
from jax.experimental.pallas import tpu as pltpu
from jax.sharding import PartitionSpec as P

MESH = pl.DeviceIdType.MESH
HEAD_WIDTH = 128
SCALE = HEAD_WIDTH ** (-0.5)
LOG2E = 1.4426950408889634
SCORE_SCALE = SCALE * LOG2E
MASKED = -1e30
LOWEST = -1e20
BF = jnp.bfloat16
F32 = jnp.float32

X, YH, CORES, YL, Z = 4, 2, 2, 2, 8
GROUP = 8
ROWS = 128
PROWS = 64
HALF_KV = 256
HALF_Q = 2048


def nt(a, b):
    return lax.dot_general(a, b, (((1,), (1,)), ((), ())), preferred_element_type=F32)


def nn(a, b):
    return lax.dot_general(a, b, (((1,), (0,)), ((), ())), preferred_element_type=F32)


def tn(a, b):
    return lax.dot_general(a, b, (((0,), (0,)), ((), ())), preferred_element_type=F32)


def gather_kernel(
    q_ref, rk_ref, rv_ref, pk_ref, pv_ref, do_ref, owner_hbm, prompt_hbm,
    q_far, do_far, resp_keys, resp_values, prompt,
    values_in, xbuf, chosen_out, chosen_in, owner_ref, prompt_ref,
    send_sem, recv_sem, local_sem,
):
    dp = lax.axis_index("dp")
    blk = lax.axis_index("blk")
    x, yh, c = dp // 4, (dp // 2) % 2, dp % 2
    yl, z = blk // Z, blk % Z
    other = 1 - yl
    y_id = (dp, other * Z + z)
    z_right, z_left = (dp, yl * Z + (z + 1) % Z), (dp, yl * Z + (z + Z - 1) % Z)
    x_right = (((x + 1) % X) * 4 + yh * 2 + c, blk)
    x_left = (((x + X - 1) % X) * 4 + yh * 2 + c, blk)
    core_id = (x * 4 + yh * 2 + (1 - c), blk)
    yh_id = (x * 4 + (1 - yh) * 2 + c, blk)
    diagonal_id = (x * 4 + (1 - yh) * 2 + c, other * Z + z)

    def lanes(which, width):
        return pl.ds(pl.multiple_of(which * width, width), width)

    def head_lanes(half, a):
        return pl.ds(pl.multiple_of(half * HALF_KV + a * 128, 128), 128)

    def group_lanes(half, a):
        return pl.ds(pl.multiple_of(half * HALF_Q + a * 1024, 1024), 1024)

    mine_kv, far_kv = lanes(yl, HALF_KV), lanes(other, HALF_KV)
    mine_q = lanes(yl, HALF_Q)

    fetched = []

    def fetch(src, dst):
        copy = pltpu.make_async_copy(src, dst, local_sem.at[len(fetched)])
        copy.start()
        fetched.append(copy)
        return copy

    def present(copies):
        for copy in copies:
            copy.wait()

    own_prompt = [
        fetch(ref.at[0], xbuf.at[x, c, kv]) for kv, ref in enumerate((pk_ref, pv_ref))
    ]
    own_resp = [
        fetch(rk_ref.at[0, :, mine_kv], resp_keys.at[z, yl]),
        fetch(rv_ref.at[0, :, mine_kv], values_in.at[yl]),
    ]
    tables = [fetch(owner_hbm, owner_ref), fetch(prompt_hbm, prompt_ref)]

    barrier = pltpu.get_barrier_semaphore()
    peers = (y_id, z_right, z_left, x_right, x_left, core_id, yh_id, diagonal_id)
    for peer in peers:
        pl.semaphore_signal(barrier, inc=1, device_id=peer, device_id_type=MESH)
    pl.semaphore_wait(barrier, len(peers))

    total = [0]

    def room(n):
        total[0] += n
        return total[0] - n

    def copy(index, src, dst, peer):
        return pltpu.make_async_remote_copy(
            src_ref=src, dst_ref=dst, send_sem=send_sem.at[index], recv_sem=recv_sem.at[index],
            device_id=peer, device_id_type=MESH,
        )

    def start(copies):
        for one in copies:
            one.start()

    def arrive(copies):
        for one in copies:
            one.wait_recv()

    def drain(copies):
        for one in copies:
            one.wait_send()

    def gather(base, slot, pos, n, step, right, left, halves):
        copies = []
        for h in halves:
            for way, peer in enumerate((right, left)):
                if step < n // 2 - 1 or h == way:
                    at = slot((pos + n - step) % n if way == 0 else (pos + step) % n, h)
                    copies.append(copy(base + h * 2 + way, at, at, peer))
        return copies

    x_base, core_base, ys_base, yq_base, yd_base = room(8), room(5), room(2), room(2), room(2)
    ring_base, r_base, p_base = room(3), room(16), room(32)

    def x_copies(step):
        if step == 0:
            return [
                copy(x_base + kv * 2 + way, ref.at[0], xbuf.at[x, c, kv], peer)
                for way, peer in enumerate((x_right, x_left))
                for kv, ref in enumerate((pk_ref, pv_ref))
            ]
        return gather(
            x_base + 4, lambda i, h: xbuf.at[i, c, h], x, X, 1, x_right, x_left, (0, 1)
        )

    def core_copies(which):
        if which == 0:
            return [
                copy(core_base + kv, ref.at[0], xbuf.at[x, c, kv], core_id)
                for kv, ref in enumerate((pk_ref, pv_ref))
            ]
        slots = ((x + 1) % X, (x + X - 1) % X) if which == 1 else ((x + 2) % X,)
        return [
            copy(core_base + which * 2 + n, xbuf.at[i, c], xbuf.at[i, c], core_id)
            for n, i in enumerate(slots)
        ]

    y_resp = [
        copy(ys_base, rk_ref.at[0, :, far_kv], resp_keys.at[z, yl], y_id),
        copy(ys_base + 1, rv_ref.at[0, :, far_kv], values_in.at[yl], y_id),
    ]

    def y_group(base, ref, far):
        return [
            copy(base + a, ref.at[0, :, group_lanes(other, a)], far.at[:, a * 1024 : a * 1024 + 1024], y_id)
            for a in range(2)
        ]

    y_q, y_do = y_group(yq_base, q_ref, q_far), y_group(yd_base, do_ref, do_far)
    ring = [
        copy(ring_base + n, chosen_out.at[n], chosen_in.at[n], peer)
        for n, peer in enumerate((y_id, yh_id, diagonal_id))
    ]

    def r_copies(step, h):
        return gather(
            r_base + step * 4, lambda i, h: (resp_values if h else resp_keys).at[i],
            z, Z, step, z_right, z_left, (h,),
        )

    def p_copies(a, step):
        return gather(
            p_base + a * 16 + step * 4, lambda i, h: prompt.at[a, i, h],
            z, Z, step, z_right, z_left, (0, 1),
        )

    start(x_copies(0))
    start(y_resp)
    start(core_copies(0))
    start(y_q)
    present(tables)
    arrive(x_copies(0))
    start(x_copies(1))
    start(core_copies(1))
    present(own_resp)
    arrive(y_resp[:1])
    start(r_copies(0, 0))
    arrive(y_resp[1:])
    for a in range(2):
        for y in range(2):
            resp_values[z, a, :, y * ROWS : (y + 1) * ROWS] = values_in[
                y, :, a * 128 : (a + 1) * 128
            ].T
    start(r_copies(0, 1))
    arrive(x_copies(1))
    start(core_copies(2))
    present(own_prompt)
    for which in range(3):
        arrive(core_copies(which))
    theirs = owner_ref[prompt_ref[x * 4 + (1 - yh) * 2 + c]]
    mine = owner_ref[prompt_ref[dp]]

    def piece(owner, half, a):
        return xbuf[owner // 4, owner % 2, :, :, head_lanes(half, a)]

    for n, (owner, half) in enumerate(((mine, other), (theirs, yl), (theirs, other))):
        for a in range(2):
            chosen_out[n, a] = piece(owner, half, a)
        start(ring[n : n + 1])
    start(y_do)

    def pass_resp(step):
        for h in range(2):
            arrive(r_copies(step - 1, h))
            start(r_copies(step, h))

    pass_resp(1)
    arrive(ring)
    here = (mine // 2) % 2 == yh
    for a in range(2):
        for kv in range(2):
            prompt[a, z, kv, yl] = jnp.where(here, piece(mine, yl, a)[kv], chosen_in[1, a, kv])
            prompt[a, z, kv, other] = jnp.where(here, chosen_in[0, a, kv], chosen_in[2, a, kv])
        start(p_copies(a, 0))
    for step in range(1, 4):
        for a in range(2):
            arrive(p_copies(a, step - 1))
            start(p_copies(a, step))
        if step < 3:
            pass_resp(step + 1)
    every = [x_copies(0), x_copies(1), core_copies(0), core_copies(1), core_copies(2)]
    every += [y_resp, y_q, y_do, ring]
    for step in range(4):
        every += [r_copies(step, h) for h in range(2)] + [p_copies(a, step) for a in range(2)]
    for copies in every:
        drain(copies)
    arrive(y_q + y_do)
    for h in range(2):
        arrive(r_copies(3, h))
        arrive(p_copies(h, 3))


def compute_kernel(
    q_ref, do_ref, q_far, do_far, resp_keys, resp_values, prompt, length_ref, half_ref,
    out_near, out_far, gacc,
    q_near, do_near, limit_ref, m_ref, acc_ref, lse_ref, delta_ref, local_sem,
):
    dp = lax.axis_index("dp")
    blk = lax.axis_index("blk")
    yl, z = blk // Z, blk % Z
    other = 1 - yl
    mine_q = pl.ds(pl.multiple_of(yl * HALF_Q, HALF_Q), HALF_Q)
    loads = [
        pltpu.make_async_copy(q_ref.at[0, :, mine_q], q_near, local_sem.at[0]),
        pltpu.make_async_copy(do_ref.at[0, :, mine_q], do_near, local_sem.at[1]),
    ]
    for load in loads:
        load.start()
    for load in loads:
        load.wait()

    def head_of(near, far, h):
        columns = pl.ds(pl.multiple_of(h * 128, 128), 128)
        return jnp.concatenate([near[:, columns], far[:, columns]], axis=0)

    def loop(count, body):
        def step(i, carry):
            body(i)
            return carry

        lax.fori_loop(0, count, step, 0)

    lane = lax.broadcasted_iota(jnp.int32, (1, 2 * ROWS), 1)
    last = length_ref[dp] - 1
    limit = jnp.zeros((1, 2 * ROWS), jnp.int32)
    for part, holder in enumerate((blk, other * Z + z)):
        for e in range(2):
            block = part * 2 + e
            inside = (lane >= block * 64) & (lane < block * 64 + 64)
            limit = jnp.where(inside, half_ref[2 * holder + e] * 64 + lane - block * 64, limit)
    limit_ref[...] = jnp.minimum(limit, last)
    m_ref[...] = jnp.full(m_ref.shape, LOWEST, F32)
    acc_ref[...] = jnp.zeros(acc_ref.shape, F32)

    def absorb(a, keys, values, bounds):
        def score(query):
            pieces, tops = [], []
            down = lax.broadcasted_iota(jnp.int32, (64, 2 * ROWS), 0)
            for part, offset in zip(keys, range(0, 64 * len(bounds), keys[0].shape[0])):
                scores = nt(part, query) * SCORE_SCALE
                for m in range(part.shape[0] // 64):
                    piece, bound = scores[64 * m : 64 * m + 64], bounds[offset // 64 + m]
                    if bound is not None:
                        piece = jnp.where(down <= bound, piece, MASKED)
                    tops.append(jnp.max(piece.reshape(8, 8, 2 * ROWS), axis=0))
                    pieces.append(piece)
            while len(tops) > 1:
                tops = [jnp.maximum(tops[i], tops[i + 1]) for i in range(0, len(tops), 2)]
            return jnp.concatenate(pieces, axis=0), jnp.max(tops[0], axis=0, keepdims=True)

        values = jnp.concatenate([values, jnp.ones((16, 64 * len(bounds)), BF)], axis=0)

        def body(t):
            first = a * GROUP + t * UNROLL
            heads = pl.ds(first, UNROLL)
            old, old_mixed = m_ref[heads], acc_ref[heads]
            peaks, mixes = [], []

            def weigh(j, scores, top):
                peak = jnp.maximum(old[j], top)
                weights = jnp.exp2(scores - peak).astype(BF)
                peaks.append(peak)
                mixes.append(old_mixed[j] * jnp.exp2(old[j] - peak) + nn(values, weights))

            ready = score(head_of(q_near, q_far, first))
            for j in range(UNROLL):
                following = score(head_of(q_near, q_far, first + j + 1)) if j < UNROLL - 1 else None
                weigh(j, *ready)
                ready = following
            for j in range(UNROLL):
                m_ref[first + j] = peaks[j]
                acc_ref[first + j] = mixes[j]

        loop(GROUP // UNROLL, body)

    def absorb_resp(a, slots):
        columns = pl.ds(pl.multiple_of(a * 128, 128), 128)
        keys = [resp_keys[i, :, :, columns].reshape(2 * ROWS, 128) for i in slots]
        values = jnp.concatenate([resp_values[i, a] for i in slots], axis=1)
        limit = limit_ref[...]
        bounds = [
            limit - half_ref[2 * ((n // 2) * Z + i) + n % 2] * 64 for i in slots for n in range(4)
        ]
        absorb(a, keys, values, bounds)

    def absorb_prompt(a, slots):
        keys = jnp.concatenate([prompt[a, i, 0].reshape(2 * PROWS, 128) for i in slots], axis=0)
        values = [prompt[a, i, 1].reshape(2 * PROWS, 128).T for i in slots]
        absorb(a, [keys], jnp.concatenate(values, axis=1), [None] * (2 * len(slots)))

    def finish(a):
        def body(t):
            first = a * GROUP + t * UNROLL
            heads = pl.ds(first, UNROLL)
            peak, mixed = m_ref[heads], acc_ref[heads]
            outs, logs, deltas = [], [], []
            for j in range(UNROLL):
                total = mixed[j, 128:129]
                result = (mixed[j, :128] / total).T
                logs.append(peak[j] + jnp.log(total) * LOG2E)
                product = result * head_of(do_near, do_far, first + j).astype(F32)
                high = product.astype(BF)
                low = (product - high.astype(F32)).astype(BF)
                halves = jnp.concatenate([high, low], axis=1)
                deltas.append(nt(jnp.ones((16, 256), BF), halves)[:1])
                outs.append(result.astype(BF))
            for j in range(UNROLL):
                h = first + j
                lse_ref[h] = logs[j]
                delta_ref[h] = deltas[j]
                columns = pl.ds(pl.multiple_of(h * 128, 128), 128)
                out_near[:, columns] = outs[j][:ROWS]
                out_far[:, columns] = outs[j][ROWS:]

        loop(GROUP // UNROLL, body)

    def gradients(a, k, slots):
        keys = jnp.concatenate([prompt[a, i, 0].reshape(2 * PROWS, 128) for i in slots], axis=0)
        values = jnp.concatenate([prompt[a, i, 1].reshape(2 * PROWS, 128) for i in slots], axis=0)
        heads = [a * GROUP + j for j in range(GROUP)]
        queries = [head_of(q_near, q_far, h) for h in heads]
        cotangents = [head_of(do_near, do_far, h) for h in heads]
        all_probs, all_slopes = [], []
        for h, query, cotangent in zip(heads, queries, cotangents):
            probs = jnp.exp2(nt(keys, query) * SCORE_SCALE - lse_ref[h])
            slopes = probs * (nt(values, cotangent) - delta_ref[h])
            all_probs.append(probs.astype(BF))
            all_slopes.append(slopes.astype(BF))
        queries = jnp.concatenate(queries, axis=0)
        cotangents = jnp.concatenate(cotangents, axis=0)
        key_part = nn(jnp.concatenate(all_slopes, axis=1), queries) * SCALE
        value_part = nn(jnp.concatenate(all_probs, axis=1), cotangents)
        for n in range(2):
            gacc[a, k, n, 0] = key_part[n * 128 : n * 128 + 128].reshape(2, PROWS, 128)
            gacc[a, k, n, 1] = value_part[n * 128 : n * 128 + 128].reshape(2, PROWS, 128)

    def resp_unit(u):
        s = u // 2
        absorb_resp(u % 2, [(z + Z - s) % Z, (z + s + 1) % Z])

    def prompt_unit(u):
        absorb_prompt(u % 2, [(u // 2) * 4 + n for n in range(4)])

    def gradient_unit(u):
        a, k = u % 2, u // 2
        gradients(a, k, [(z + 4 + k) % Z, (z + 3 + Z - k) % Z])

    loop(8, resp_unit)
    loop(4, prompt_unit)
    loop(2, finish)
    loop(8, gradient_unit)


def reduce_kernel(
    out_near, out_far, gacc, owner_hbm, prompt_hbm,
    out_ref, gk_ref, gv_ref,
    zs_out, zs_in, share_out, share, core_in, xs_out, xs_in, owner_ref, prompt_ref,
    send_sem, recv_sem, local_sem,
):
    dp = lax.axis_index("dp")
    blk = lax.axis_index("blk")
    x, yh, c = dp // 4, (dp // 2) % 2, dp % 2
    yl, z = blk // Z, blk % Z
    other = 1 - yl
    y_id = (dp, other * Z + z)
    z_right, z_left = (dp, yl * Z + (z + 1) % Z), (dp, yl * Z + (z + Z - 1) % Z)
    x_right = (((x + 1) % X) * 4 + yh * 2 + c, blk)
    x_left = (((x + X - 1) % X) * 4 + yh * 2 + c, blk)
    core_id = (x * 4 + yh * 2 + (1 - c), blk)
    yh_id = (x * 4 + (1 - yh) * 2 + c, blk)
    diagonal_id = (x * 4 + (1 - yh) * 2 + c, other * Z + z)

    def lanes(which, width):
        return pl.ds(pl.multiple_of(which * width, width), width)

    def head_lanes(half, a):
        return pl.ds(pl.multiple_of(half * HALF_KV + a * 128, 128), 128)

    def group_lanes(half, a):
        return pl.ds(pl.multiple_of(half * HALF_Q + a * 1024, 1024), 1024)

    mine_kv, far_kv = lanes(yl, HALF_KV), lanes(other, HALF_KV)
    mine_q = lanes(yl, HALF_Q)

    fetched = []

    def fetch(src, dst):
        copy = pltpu.make_async_copy(src, dst, local_sem.at[len(fetched)])
        copy.start()
        fetched.append(copy)
        return copy

    def present(copies):
        for copy in copies:
            copy.wait()

    tables = [fetch(owner_hbm, owner_ref), fetch(prompt_hbm, prompt_ref)]
    own_result = fetch(out_near, out_ref.at[0, :, mine_q])
    barrier = pltpu.get_barrier_semaphore()
    peers = (y_id, z_right, z_left, x_right, x_left, core_id, yh_id, diagonal_id)
    for peer in peers:
        pl.semaphore_signal(barrier, inc=1, device_id=peer, device_id_type=MESH)
    pl.semaphore_wait(barrier, len(peers))

    total = [0]

    def room(n):
        total[0] += n
        return total[0] - n

    def copy(index, src, dst, peer):
        return pltpu.make_async_remote_copy(
            src_ref=src, dst_ref=dst, send_sem=send_sem.at[index], recv_sem=recv_sem.at[index],
            device_id=peer, device_id_type=MESH,
        )

    def start(copies):
        for one in copies:
            one.start()

    def arrive(copies):
        for one in copies:
            one.wait_recv()

    def drain(copies):
        for one in copies:
            one.wait_send()

    result_base, zs_base, yr_base, cs_base, xs_base = room(2), room(32), room(6), room(2), room(16)

    def result_copies(a):
        columns = pl.ds(pl.multiple_of(a * 1024, 1024), 1024)
        return [copy(result_base + a, out_far.at[:, columns], out_ref.at[0, :, group_lanes(yl, a)], y_id)]

    def sums(base, outgoing, incoming, a, step, right, left):
        return [
            copy(
                base + step * 4 + way * 2 + h,
                outgoing.at[a, way, step, h], incoming.at[a, way, step, h], peer,
            )
            for way, peer in enumerate((right, left))
            for h in range(2)
            if step > 0 or h == way
        ]

    def zs_copies(a, step):
        return sums(zs_base + a * 16, zs_out, zs_in, a, step, z_right, z_left)

    def xs_copies(a, step):
        return sums(xs_base + a * 8, xs_out, xs_in, a, step, x_right, x_left)

    def yr_copies(a):
        return [
            copy(yr_base + a * 3, share_out.at[a], share.at[a, 0, 1], y_id),
            copy(yr_base + a * 3 + 1, share.at[a, 0, 0], share.at[a, 1, 0], yh_id),
            copy(yr_base + a * 3 + 2, share_out.at[a], share.at[a, 1, 1], diagonal_id),
        ]

    def cs_copies(a):
        return [copy(cs_base + a, share.at[a], core_in.at[a], core_id)]

    def z_messages(a, step):
        for way in range(2):
            for h in range(2):
                if step > 0 or h == way:
                    if way == 0 and step > 0:
                        part = gacc[a, step - 1, 1, h]
                    else:
                        part = gacc[a, step, 0, h]
                    if step > 1 or (step == 1 and h == way):
                        part = part + zs_in[a, way, step - 1, h].astype(F32)
                    zs_out[a, way, step, h] = part.astype(BF)
        start(zs_copies(a, step))

    def to_y_ring(a):
        for h in range(2):
            for n, where in enumerate((yl, other)):
                part = gacc[a, 3, 1, h, where]
                for way in range(2):
                    part = part + zs_in[a, way, 3, h, where].astype(F32)
                (share.at[a, 0, 0] if n == 0 else share_out.at[a])[h] = part.astype(BF)
        start(yr_copies(a))

    def destined(a, target, h):
        result = jnp.zeros((2, PROWS, 128), F32)
        for n in range(4):
            source = x * 4 + (yh if n % 2 == 0 else 1 - yh) * 2 + (c if n < 2 else 1 - c)
            owner = owner_ref[prompt_ref[source]]
            part = (share if n < 2 else core_in)[a, n % 2, :, h].astype(F32)
            result = result + jnp.where(owner == target * 4 + yh * 2 + c, part, 0.0)
        return result

    def x_messages(a, step):
        for way in range(2):
            distance = 2 - step
            target = (x + distance) % X if way == 0 else (x + X - distance) % X
            for h in range(2):
                if step > 0 or h == way:
                    part = destined(a, target, h)
                    if step == 1 and h == way:
                        part = part + xs_in[a, way, 0, h].astype(F32)
                    xs_out[a, way, step, h] = part.astype(BF)
        start(xs_copies(a, step))

    def store(a):
        for h, ref in enumerate((gk_ref, gv_ref)):
            part = destined(a, x, h)
            for way in range(2):
                part = part + xs_in[a, way, 1, h].astype(F32)
            ref[0, :, head_lanes(yl, a)] = part[0]
            ref[0, :, head_lanes(other, a)] = part[1]

    for a in range(2):
        z_messages(a, 0)
        start(result_copies(a))
    present(tables)
    for step in range(1, 4):
        for a in range(2):
            arrive(zs_copies(a, step - 1))
            z_messages(a, step)
    for a in range(2):
        arrive(zs_copies(a, 3))
        to_y_ring(a)
    for a in range(2):
        arrive(yr_copies(a))
        start(cs_copies(a))
    for a in range(2):
        arrive(cs_copies(a))
        x_messages(a, 0)
    for a in range(2):
        arrive(xs_copies(a, 0))
        x_messages(a, 1)
    for step in range(4):
        for a in range(2):
            drain(zs_copies(a, step))
    for a in range(2):
        drain(result_copies(a) + yr_copies(a) + cs_copies(a) + xs_copies(a, 0))
        arrive(result_copies(a))
        arrive(xs_copies(a, 1))
        store(a)
        drain(xs_copies(a, 1))
    present([own_result])


UNROLL = 4
PIECES = 4


def copy_out(*refs):
    ins, outs, held = refs[:3], refs[3:6], refs[6:9]
    in_sem, out_sem = refs[9:]
    parts = [(0, slice(n * 1024, n * 1024 + 1024)) for n in range(PIECES)]
    parts += [(1, slice(0, 512)), (2, slice(0, 512))]

    def move(sources, targets, sem):
        return [
            pltpu.make_async_copy(sources[n].at[0, :, columns], targets[n].at[0, :, columns], sem.at[i])
            for i, (n, columns) in enumerate(parts)
        ]

    loads, stores = move(ins, held, in_sem), move(held, outs, out_sem)
    for copy in loads:
        copy.start()
    for load, save in zip(loads, stores):
        load.wait()
        save.start()
    for copy in stores:
        copy.wait()


def on_device(q, rk, rv, pk, pv, do, owner, prompt_index, length, half):
    block = (2, 2, PROWS, 128)
    hbm = pl.BlockSpec(memory_space=pltpu.HBM)
    vmem = pl.BlockSpec(memory_space=pltpu.VMEM)
    smem = pl.BlockSpec(memory_space=pltpu.SMEM)

    def parameters(number=None):
        extra = {} if number is None else dict(collective_id=number, has_side_effects=True)
        return pltpu.CompilerParams(vmem_limit_bytes=60 * 1024 * 1024, **extra)

    def sems(*counts):
        return [pltpu.SemaphoreType.DMA((n,)) for n in counts]

    tables = [pltpu.SMEM((16,), jnp.int32)] * 2
    half_shape = jax.ShapeDtypeStruct((ROWS, HALF_Q), BF)
    q_far, do_far, keys, values, prompt = pl.pallas_call(
        gather_kernel,
        out_shape=(
            half_shape,
            half_shape,
            jax.ShapeDtypeStruct((Z, 2, ROWS, HALF_KV), BF),
            jax.ShapeDtypeStruct((Z, 2, 128, 2 * ROWS), BF),
            jax.ShapeDtypeStruct((2, Z) + block, BF),
        ),
        in_specs=[hbm] * 8,
        out_specs=(vmem,) * 5,
        scratch_shapes=[
            pltpu.VMEM((2, ROWS, HALF_KV), BF),
            pltpu.VMEM((X, 2, 2, PROWS, 512), BF),
            pltpu.VMEM((3, 2, 2, PROWS, 128), BF),
            pltpu.VMEM((3, 2, 2, PROWS, 128), BF),
        ]
        + tables
        + sems(80, 80, 16),
        compiler_params=parameters(0),
    )(q, rk, rv, pk, pv, do, owner, prompt_index)
    out_near, out_far, partial = pl.pallas_call(
        compute_kernel,
        out_shape=(
            half_shape,
            half_shape,
            jax.ShapeDtypeStruct((2, 4, 2) + block, F32),
        ),
        in_specs=[hbm] * 2 + [vmem] * 5 + [smem] * 2,
        out_specs=(vmem,) * 3,
        scratch_shapes=[
            pltpu.VMEM((ROWS, HALF_Q), BF),
            pltpu.VMEM((ROWS, HALF_Q), BF),
            pltpu.VMEM((1, 2 * ROWS), jnp.int32),
            pltpu.VMEM((16, 1, 256), F32),
            pltpu.VMEM((16, 144, 256), F32),
            pltpu.VMEM((16, 1, 256), F32),
            pltpu.VMEM((16, 1, 256), F32),
        ]
        + sems(2),
        compiler_params=parameters(),
    )(q, do, q_far, do_far, keys, values, prompt, length, half)
    results = pl.pallas_call(
        reduce_kernel,
        out_shape=(
            jax.ShapeDtypeStruct((1, ROWS, 4096), BF),
            jax.ShapeDtypeStruct((1, PROWS, 512), F32),
            jax.ShapeDtypeStruct((1, PROWS, 512), F32),
        ),
        in_specs=[vmem] * 3 + [hbm] * 2,
        out_specs=(hbm, vmem, vmem),
        scratch_shapes=[
            pltpu.VMEM((2, 2, 4) + block, BF),
            pltpu.VMEM((2, 2, 4) + block, BF),
            pltpu.VMEM((2, 2, PROWS, 128), BF),
            pltpu.VMEM((2, 2) + block, BF),
            pltpu.VMEM((2, 2) + block, BF),
            pltpu.VMEM((2, 2, 2) + block, BF),
            pltpu.VMEM((2, 2, 2) + block, BF),
        ]
        + tables
        + sems(64, 64, 4),
        compiler_params=parameters(1),
    )(out_near, out_far, partial, owner, prompt_index)
    return pl.pallas_call(
        copy_out,
        out_shape=tuple(jax.ShapeDtypeStruct(r.shape, r.dtype) for r in results),
        in_specs=[pl.BlockSpec(memory_space=pl.ANY)] * 3,
        out_specs=(hbm,) * 3,
        scratch_shapes=[pltpu.VMEM(r.shape, r.dtype) for r in results]
        + [pltpu.SemaphoreType.DMA((PIECES + 2,))] * 2,
        compiler_params=pltpu.CompilerParams(vmem_limit_bytes=60 * 1024 * 1024),
    )(*results)


def solution(mesh):
    split = P("dp", "blk", None)
    return jax.shard_map(
        on_device,
        mesh=mesh,
        in_specs=(split,) * 6 + (P(),) * 4,
        out_specs=(split, split, split),
        check_vma=False,
    )
```

```python
import jax
import jax.numpy as jnp
from jax import lax
from jax.experimental import pallas as pl
from jax.experimental.pallas import tpu as pltpu
from jax.sharding import PartitionSpec as P

MESH = pl.DeviceIdType.MESH
HEAD_WIDTH = 128
SCALE = HEAD_WIDTH ** (-0.5)
LOG2E = 1.4426950408889634
SCORE_SCALE = SCALE * LOG2E
MASKED = -1e30
LOWEST = -1e20
BF = jnp.bfloat16
F32 = jnp.float32

X, YH, CORES, YL, Z = 4, 2, 2, 2, 8
GROUP = 8
ROWS = 128
PROWS = 64
HALF_KV = 256
HALF_Q = 2048


def nt(a, b):
    return lax.dot_general(a, b, (((1,), (1,)), ((), ())), preferred_element_type=F32)


def nn(a, b):
    return lax.dot_general(a, b, (((1,), (0,)), ((), ())), preferred_element_type=F32)


def tn(a, b):
    return lax.dot_general(a, b, (((0,), (0,)), ((), ())), preferred_element_type=F32)


def kernel(
    q_ref, rk_ref, rv_ref, pk_ref, pv_ref, do_ref, owner_hbm, prompt_hbm, length_hbm, half_hbm,
    out_ref, gk_ref, gv_ref,
    q_near, q_far, do_near, do_far, out_near, out_far,
    resp, far_block, values_in, xbuf, chosen_out, chosen_in, prompt, v_turned,
    m_ref, acc_ref, lse_ref, delta_ref, gacc,
    zs_out, zs_in, share_out, share, core_in, xs_out, xs_in,
    owner_ref, prompt_ref, length_ref, half_ref,
    send_sem, recv_sem, local_sem,
):
    dp = lax.axis_index("dp")
    blk = lax.axis_index("blk")
    x, yh, c = dp // 4, (dp // 2) % 2, dp % 2
    yl, z = blk // Z, blk % Z
    other = 1 - yl
    y_id = (dp, other * Z + z)
    z_right, z_left = (dp, yl * Z + (z + 1) % Z), (dp, yl * Z + (z + Z - 1) % Z)
    x_right = (((x + 1) % X) * 4 + yh * 2 + c, blk)
    x_left = (((x + X - 1) % X) * 4 + yh * 2 + c, blk)
    core_id = (x * 4 + yh * 2 + (1 - c), blk)
    yh_id = (x * 4 + (1 - yh) * 2 + c, blk)
    far_x_id = (((x + 2) % X) * 4 + yh * 2 + c, blk)
    diagonal_id = (x * 4 + (1 - yh) * 2 + c, other * Z + z)

    def lanes(which, width):
        return pl.ds(pl.multiple_of(which * width, width), width)

    def head_lanes(half, a):
        return pl.ds(pl.multiple_of(half * HALF_KV + a * 128, 128), 128)

    def group_lanes(half, a):
        return pl.ds(pl.multiple_of(half * HALF_Q + a * 1024, 1024), 1024)

    mine_kv, far_kv = lanes(yl, HALF_KV), lanes(other, HALF_KV)
    mine_q = lanes(yl, HALF_Q)

    fetched = []

    def fetch(src, dst):
        copy = pltpu.make_async_copy(src, dst, local_sem.at[len(fetched)])
        copy.start()
        fetched.append(copy)
        return copy

    def present(copies):
        for copy in copies:
            copy.wait()

    own_prompt = [
        fetch(ref.at[0], xbuf.at[x, c, kv]) for kv, ref in enumerate((pk_ref, pv_ref))
    ]
    own_resp = [fetch(rv_ref.at[0], values_in)]
    own_resp += [
        fetch(rk_ref.at[0, :, head_lanes(half, a)], to.at[0, a])
        for half, to in ((yl, resp.at[z, yl]), (other, far_block))
        for a in range(2)
    ]
    tables = [
        fetch(owner_hbm, owner_ref), fetch(prompt_hbm, prompt_ref),
        fetch(length_hbm, length_ref), fetch(half_hbm, half_ref),
    ]
    own_q = fetch(q_ref.at[0, :, mine_q], q_near)
    own_do = fetch(do_ref.at[0, :, mine_q], do_near)

    barrier = pltpu.get_barrier_semaphore()
    peers = (y_id, z_right, z_left, x_right, x_left, core_id, yh_id, diagonal_id, far_x_id)
    for peer in peers:
        pl.semaphore_signal(barrier, inc=1, device_id=peer, device_id_type=MESH)
    pl.semaphore_wait(barrier, len(peers))

    started = []

    def send(src, dst, peer):
        index = len(started)
        copy = pltpu.make_async_remote_copy(
            src_ref=src, dst_ref=dst, send_sem=send_sem.at[index], recv_sem=recv_sem.at[index],
            device_id=peer, device_id_type=MESH,
        )
        copy.start()
        started.append(copy)
        return copy

    def arrive(copies):
        for copy in copies:
            copy.wait_recv()

    x0 = [
        send(ref.at[0], xbuf.at[x, c, kv], peer)
        for peer in (x_right, x_left)
        for kv, ref in enumerate((pk_ref, pv_ref))
    ]
    y_q = [None, None]

    def send_queries(a):
        near, far = q_ref.at[0, :, group_lanes(other, a)], q_far.at[:, a * 1024 : a * 1024 + 1024]
        y_q[a] = send(near, far, y_id)

    send_queries(0)
    cores = [
        send(ref.at[0], xbuf.at[x, c, kv], core_id) for kv, ref in enumerate((pk_ref, pv_ref))
    ]

    def gather_step(slot, pos, n, step, right, left):
        copies = []
        for way, peer in enumerate((right, left)):
            at = slot((pos + n - step) % n if way == 0 else (pos + step) % n)
            at = at.at[way] if step == n // 2 - 1 else at
            copies.append(send(at, at, peer))
        return copies

    def resp_gather(y, step):
        return gather_step(lambda i: resp.at[i, y], z, Z, step, z_right, z_left)

    def prompt_gather(a, step):
        return gather_step(lambda i: prompt.at[a, i], z, Z, step, z_right, z_left)

    def core_send(i):
        return send(xbuf.at[i, c], xbuf.at[i, c], core_id)

    def head_of(near, far, h):
        columns = pl.ds(pl.multiple_of(h * 128, 128), 128)
        return jnp.concatenate([near[:, columns], far[:, columns]], axis=0)

    def turn_values():
        for half, to in ((yl, resp.at[z, yl]), (other, far_block)):
            for a in range(2):
                to[1, a] = values_in[:, head_lanes(half, a)].T

    present(tables)
    lane = lax.broadcasted_iota(jnp.int32, (1, 2 * ROWS), 1)
    last = length_ref[dp] - 1
    limit = jnp.zeros((1, 2 * ROWS), jnp.int32)
    for part, holder in enumerate((blk, other * Z + z)):
        for e in range(2):
            block = part * 2 + e
            inside = (lane >= block * 64) & (lane < block * 64 + 64)
            limit = jnp.where(inside, half_ref[2 * holder + e] * 64 + lane - block * 64, limit)
    limit = jnp.minimum(limit, last)
    down = lax.broadcasted_iota(jnp.int32, (64, 2 * ROWS), 0)

    def prompt_rows(slots, kv, a):
        return [prompt[a, i, kv].reshape(2 * PROWS, 128) for i in slots]

    def absorb(a, resp_slots, prompt_slots):
        bounds = []
        for i, y in resp_slots:
            bounds += [limit - half_ref[2 * (y * Z + i) + e] * 64 for e in range(2)]
        bounds += [None] * (2 * len(prompt_slots))
        count = 64 * len(bounds)

        keys = [resp[i, y, 0, a] for i, y in resp_slots] + prompt_rows(prompt_slots, 0, a)
        keys = jnp.concatenate(keys, axis=0)
        for n, part in enumerate(prompt_rows(prompt_slots, 1, a)):
            v_turned[:, n * 128 : n * 128 + 128] = part.T

        def score(query):
            pieces, tops = [], []
            scores = nt(keys, query) * SCORE_SCALE
            for n, bound in enumerate(bounds):
                piece = scores[64 * n : 64 * n + 64]
                if bound is not None:
                    piece = jnp.where(down <= bound, piece, MASKED)
                tops.append(jnp.max(piece.reshape(8, 8, 2 * ROWS), axis=0))
                pieces.append(piece)
            while len(tops) > 1:
                tops = [
                    jnp.maximum(tops[i], tops[i + 1]) if i + 1 < len(tops) else tops[i]
                    for i in range(0, len(tops), 2)
                ]
            return jnp.concatenate(pieces, axis=0), jnp.max(tops[0], axis=0, keepdims=True)

        def body(t, carry):
            first = a * GROUP + t * 4
            heads = pl.ds(first, 4)
            values = [resp[i, y, 1, a] for i, y in resp_slots]
            if prompt_slots:
                values.append(v_turned[:, : 128 * len(prompt_slots)])
            values = jnp.concatenate(values, axis=1) if len(values) > 1 else values[0]
            values = jnp.concatenate([values, jnp.ones((16, count), BF)], axis=0)
            old, old_mixed = m_ref[heads], acc_ref[heads]
            peaks, mixes = [], []

            def weigh(j, scores, top):
                peak = jnp.maximum(old[j], top)
                weights = jnp.exp2(scores - peak).astype(BF)
                peaks.append(peak)
                mixes.append(old_mixed[j] * jnp.exp2(old[j] - peak) + nn(values, weights))

            ready = score(head_of(q_near, q_far, first))
            for j in range(4):
                following = score(head_of(q_near, q_far, first + j + 1)) if j < 3 else None
                weigh(j, *ready)
                ready = following
            for j in range(4):
                m_ref[first + j] = peaks[j]
                acc_ref[first + j] = mixes[j]
            return carry

        lax.fori_loop(0, 2, body, 0)

    def finish(a):
        def body(t, carry):
            first = a * GROUP + t * 4
            heads = pl.ds(first, 4)
            peak, mixed = m_ref[heads], acc_ref[heads]
            outs, sums, deltas = [], [], []
            for j in range(4):
                total = mixed[j, 128:129]
                result = (mixed[j, :128] / total).T
                sums.append(peak[j] + jnp.log(total) * LOG2E)
                product = result * head_of(do_near, do_far, first + j).astype(F32)
                high = product.astype(BF)
                low = (product - high.astype(F32)).astype(BF)
                halves = jnp.concatenate([high, low], axis=1)
                deltas.append(nt(jnp.ones((16, 256), BF), halves)[:1])
                outs.append(result.astype(BF))
            for j in range(4):
                h = first + j
                lse_ref[h] = sums[j]
                delta_ref[h] = deltas[j]
                columns = pl.ds(pl.multiple_of(h * 128, 128), 128)
                out_near[:, columns] = outs[j][:ROWS]
                out_far[:, columns] = outs[j][ROWS:]
            return carry

        lax.fori_loop(0, 2, body, 0)
        return send(
            out_far.at[:, a * 1024 : a * 1024 + 1024], out_ref.at[0, :, group_lanes(yl, a)], y_id
        )

    def gradients(a, slots):
        keys = jnp.concatenate(prompt_rows(slots, 0, a), axis=0)
        values = jnp.concatenate(prompt_rows(slots, 1, a), axis=0)
        heads = range(a * GROUP, a * GROUP + GROUP)
        queries = [head_of(q_near, q_far, h) for h in heads]
        cotangents = [head_of(do_near, do_far, h) for h in heads]
        all_probs, all_slopes = [], []
        for h, query, cotangent in zip(heads, queries, cotangents):
            probs = jnp.exp2(nt(keys, query) * SCORE_SCALE - lse_ref[h])
            slopes = probs * (nt(values, cotangent) - delta_ref[h])
            all_probs.append(probs.astype(BF))
            all_slopes.append(slopes.astype(BF))
        queries = jnp.concatenate(queries, axis=0)
        cotangents = jnp.concatenate(cotangents, axis=0)
        key_part = nn(jnp.concatenate(all_slopes, axis=1), queries) * SCALE
        value_part = nn(jnp.concatenate(all_probs, axis=1), cotangents)
        for n in range(len(slots)):
            gacc[n, 0] = key_part[n * 128 : n * 128 + 128].reshape(2, PROWS, 128)
            gacc[n, 1] = value_part[n * 128 : n * 128 + 128].reshape(2, PROWS, 128)

    def z_scatter(a, step):
        copies = []
        for way, peer in enumerate((z_right, z_left)):
            n = 0 if step == 0 else way
            for h in (way,) if step == 0 else (0, 1):
                part = gacc[n, h]
                if step > 1 or (step == 1 and h == way):
                    part = part + zs_in[a, way, step - 1, h].astype(F32)
                zs_out[a, way, step, h] = part.astype(BF)
            src, dst = zs_out.at[a, way, step], zs_in.at[a, way, step]
            if step == 0:
                src, dst = src.at[way], dst.at[way]
            copies.append(send(src, dst, peer))
        return copies

    def to_y_ring(a):
        for h in range(2):
            for n, where in enumerate((yl, other)):
                total = gacc[0, h, where]
                for way in range(2):
                    total = total + zs_in[a, way, 3, h, where].astype(F32)
                (share.at[a, 0, 0] if n == 0 else share_out.at[a])[h] = total.astype(BF)
        return [
            send(share_out.at[a], share.at[a, 0, 1], y_id),
            send(share.at[a, 0, 0], share.at[a, 1, 0], yh_id),
            send(share_out.at[a], share.at[a, 1, 1], diagonal_id),
        ]

    def to_core(a):
        return [send(share.at[a], core_in.at[a], core_id)]

    owners = []
    for source_core in (c, 1 - c):
        for source_half in (yh, 1 - yh):
            owners.append(owner_ref[prompt_ref[x * 4 + source_half * 2 + source_core]])

    def destined(a, target, h):
        total = jnp.zeros((2, PROWS, 128), F32)
        for n, owner in enumerate(owners):
            part = (share if n < 2 else core_in)[a, n % 2, :, h].astype(F32)
            total = total + jnp.where(owner == target * 4 + yh * 2 + c, part, 0.0)
        return total

    def x_scatter(a):
        copies = []
        for n, (distance, peer) in enumerate(((2, far_x_id), (1, x_right), (3, x_left))):
            for h in range(2):
                xs_out[a, n, h] = destined(a, (x + distance) % X, h).astype(BF)
            copies.append(send(xs_out.at[a, n], xs_in.at[a, n], peer))
        return copies

    def store(a):
        for h, ref in enumerate((gk_ref, gv_ref)):
            total = destined(a, x, h)
            for n in range(3):
                total = total + xs_in[a, n, h].astype(F32)
            ref[0, :, head_lanes(yl, a)] = total[0]
            ref[0, :, head_lanes(other, a)] = total[1]

    drained = []

    def drain():
        for copy in started[len(drained) :]:
            copy.wait_send()
            drained.append(copy)

    m_ref[...] = jnp.full(m_ref.shape, LOWEST, F32)
    acc_ref[...] = jnp.zeros(acc_ref.shape, F32)

    def pair(step):
        return [(z + step) % Z, (z + Z - step) % Z]

    opposite = [(z + 4) % Z]
    p, r = [None, None], [None, None]
    own, far = 0, 1

    def pass_on(step):
        for a in range(2):
            arrive(p[a])
            p[a] = prompt_gather(a, step)

    def pass_on_resp(which, step):
        arrive(r[which])
        r[which] = resp_gather(yl if which == own else other, step)

    def mine_at(slots):
        return [(i, yl) for i in slots]

    def theirs_at(slots):
        return [(i, other) for i in slots]

    present(own_resp)
    turn_values()
    r[own] = resp_gather(yl, 0)
    y_far = [send(far_block, resp.at[z, yl], y_id)]
    send_queries(1)
    arrive(x0)
    x1 = gather_step(lambda i: xbuf.at[i, c], x, X, 1, x_right, x_left)
    cores += [core_send((x + 1) % X), core_send((x + X - 1) % X)]
    present(own_prompt + [own_q, own_do])
    pass_on_resp(own, 1)
    arrive([y_q[0]])
    absorb(0, mine_at([z] + pair(1)), [])
    arrive(x1)
    cores += [core_send((x + 2) % X)]
    arrive(y_far)
    r[far] = resp_gather(other, 0)
    arrive(cores)
    theirs = owner_ref[prompt_ref[x * 4 + (1 - yh) * 2 + c]]
    mine = owner_ref[prompt_ref[dp]]

    def piece(owner, half, a):
        return xbuf[owner // 4, owner % 2, :, :, head_lanes(half, a)]

    ring = []
    for n, (owner, half, peer) in enumerate(
        ((mine, other, y_id), (theirs, yl, yh_id), (theirs, other, diagonal_id))
    ):
        for a in range(2):
            chosen_out[n, a] = piece(owner, half, a)
        ring.append(send(chosen_out.at[n], chosen_in.at[n], peer))
    pass_on_resp(own, 2)
    absorb(0, mine_at(pair(2)) + theirs_at([z]), [])
    arrive([y_q[1]])
    absorb(1, mine_at([z] + pair(1)), [])
    pass_on_resp(far, 1)
    arrive(ring)
    here = (mine // 2) % 2 == yh
    for a in range(2):
        for kv in range(2):
            prompt[a, z, kv, yl] = jnp.where(here, piece(mine, yl, a)[kv], chosen_in[1, a, kv])
            prompt[a, z, kv, other] = jnp.where(here, chosen_in[0, a, kv], chosen_in[2, a, kv])
        p[a] = prompt_gather(a, 0)
    pass_on_resp(own, 3)
    y_do = [
        send(do_ref.at[0, :, group_lanes(other, a)], do_far.at[:, a * 1024 : a * 1024 + 1024], y_id)
        for a in range(2)
    ]
    absorb(1, mine_at(pair(2)) + theirs_at([z]), [])
    absorb(0, mine_at(pair(3)) + theirs_at(pair(1)), [])
    pass_on(1)
    pass_on_resp(far, 2)
    absorb(1, mine_at(pair(3)) + theirs_at(pair(1)), [])
    arrive(r[own])
    pass_on(2)
    absorb(0, mine_at(opposite) + theirs_at(pair(2)), [])
    pass_on_resp(far, 3)
    absorb(1, mine_at(opposite) + theirs_at(pair(2)), [])
    pass_on(3)
    absorb(0, theirs_at(pair(3)), [z] + pair(1) + pair(2))
    drain()
    absorb(1, theirs_at(pair(3)), [z] + pair(1) + pair(2))
    arrive(r[far])
    arrive([y_do[0]])
    arrive(p[0])
    absorb(0, theirs_at(opposite), pair(3) + opposite)
    results = [finish(0)]
    gradients(0, opposite)
    s0 = z_scatter(0, 0)
    gradients(0, pair(3))
    arrive(s0)
    s0 = z_scatter(0, 1)
    arrive([y_do[1]])
    arrive(p[1])
    absorb(1, theirs_at(opposite), pair(3) + opposite)
    results += [finish(1)]
    own_result = fetch(out_near, out_ref.at[0, :, mine_q])
    gradients(1, opposite)
    s1 = z_scatter(1, 0)
    gradients(0, pair(2))
    arrive(s0)
    s0 = z_scatter(0, 2)
    gradients(1, pair(3))
    arrive(s1)
    s1 = z_scatter(1, 1)
    gradients(0, pair(1))
    arrive(s0)
    s0 = z_scatter(0, 3)
    gradients(1, pair(2))
    arrive(s1)
    s1 = z_scatter(1, 2)
    gradients(0, [z])
    arrive(s0)

    t0 = to_y_ring(0)
    gradients(1, pair(1))
    arrive(s1)
    s1 = z_scatter(1, 3)
    arrive(t0)
    t0 = to_core(0)
    gradients(1, [z])
    arrive(t0)
    t0 = x_scatter(0)
    arrive(s1)
    t1 = to_y_ring(1)
    drain()
    arrive(t1)
    t1 = to_core(1)
    arrive(t0)
    store(0)
    arrive(results)
    present([own_result])
    arrive(t1)
    t1 = x_scatter(1)
    drain()
    arrive(t1)
    store(1)


COPIES = 96
PIECES = 4


def copy_out(*refs):
    ins, outs, held = refs[:3], refs[3:6], refs[6:9]
    in_sem, out_sem = refs[9:]
    parts = [(0, slice(n * 1024, n * 1024 + 1024)) for n in range(PIECES)]
    parts += [(1, slice(0, 512)), (2, slice(0, 512))]

    def move(sources, targets, sem):
        return [
            pltpu.make_async_copy(sources[n].at[0, :, columns], targets[n].at[0, :, columns], sem.at[i])
            for i, (n, columns) in enumerate(parts)
        ]

    loads, stores = move(ins, held, in_sem), move(held, outs, out_sem)
    for copy in loads:
        copy.start()
    for load, save in zip(loads, stores):
        load.wait()
        save.start()
    for copy in stores:
        copy.wait()


def on_device(*arguments):
    block = (2, 2, PROWS, 128)
    vmem = pl.BlockSpec(memory_space=pltpu.VMEM)
    hbm = pl.BlockSpec(memory_space=pltpu.HBM)
    results = pl.pallas_call(
        kernel,
        out_shape=(
            jax.ShapeDtypeStruct((1, ROWS, 4096), BF),
            jax.ShapeDtypeStruct((1, PROWS, 512), F32),
            jax.ShapeDtypeStruct((1, PROWS, 512), F32),
        ),
        in_specs=[hbm] * 10,
        out_specs=(hbm, vmem, vmem),
        scratch_shapes=[
            pltpu.VMEM((ROWS, HALF_Q), BF),
            pltpu.VMEM((ROWS, HALF_Q), BF),
            pltpu.VMEM((ROWS, HALF_Q), BF),
            pltpu.VMEM((ROWS, HALF_Q), BF),
            pltpu.VMEM((ROWS, HALF_Q), BF),
            pltpu.VMEM((ROWS, HALF_Q), BF),
            pltpu.VMEM((Z, 2, 2, 2, 128, 128), BF),
            pltpu.VMEM((2, 2, 128, 128), BF),
            pltpu.VMEM((ROWS, 512), BF),
            pltpu.VMEM((X, 2, 2, PROWS, 512), BF),
            pltpu.VMEM((3, 2, 2, PROWS, 128), BF),
            pltpu.VMEM((3, 2, 2, PROWS, 128), BF),
            pltpu.VMEM((2, Z) + block, BF),
            pltpu.VMEM((128, 1024), BF),
            pltpu.VMEM((16, 1, 256), F32),
            pltpu.VMEM((16, 144, 256), F32),
            pltpu.VMEM((16, 1, 256), F32),
            pltpu.VMEM((16, 1, 256), F32),
            pltpu.VMEM((2,) + block, F32),
            pltpu.VMEM((2, 2, 4) + block, BF),
            pltpu.VMEM((2, 2, 4) + block, BF),
            pltpu.VMEM((2, 2, PROWS, 128), BF),
            pltpu.VMEM((2, 2) + block, BF),
            pltpu.VMEM((2, 2) + block, BF),
            pltpu.VMEM((2, 3) + block, BF),
            pltpu.VMEM((2, 3) + block, BF),
            pltpu.SMEM((16,), jnp.int32),
            pltpu.SMEM((16,), jnp.int32),
            pltpu.SMEM((16,), jnp.int32),
            pltpu.SMEM((32,), jnp.int32),
            pltpu.SemaphoreType.DMA((COPIES,)),
            pltpu.SemaphoreType.DMA((COPIES,)),
            pltpu.SemaphoreType.DMA((16,)),
        ],
        compiler_params=pltpu.CompilerParams(
            collective_id=0, has_side_effects=True, vmem_limit_bytes=60 * 1024 * 1024
        ),
        cost_estimate=pl.CostEstimate(
            flops=10_000_000_000, bytes_accessed=8 * 1024 * 1024, transcendentals=17_000_000
        ),
    )(*arguments)
    return pl.pallas_call(
        copy_out,
        out_shape=tuple(jax.ShapeDtypeStruct(r.shape, r.dtype) for r in results),
        in_specs=[pl.BlockSpec(memory_space=pl.ANY)] * 3,
        out_specs=(hbm,) * 3,
        scratch_shapes=[pltpu.VMEM(r.shape, r.dtype) for r in results]
        + [pltpu.SemaphoreType.DMA((PIECES + 2,))] * 2,
        compiler_params=pltpu.CompilerParams(vmem_limit_bytes=60 * 1024 * 1024),
    )(*results)


def solution(mesh):
    split = P("dp", "blk", None)
    return jax.shard_map(
        on_device,
        mesh=mesh,
        in_specs=(split,) * 6 + (P(),) * 4,
        out_specs=(split, split, split),
        check_vma=False,
    )
```

```python
import jax
import jax.numpy as jnp
from jax import lax
from jax.experimental import pallas as pl
from jax.experimental.pallas import tpu as pltpu
from jax.sharding import PartitionSpec as P

MESH = pl.DeviceIdType.MESH
HEAD_WIDTH = 128
SCALE = HEAD_WIDTH ** (-0.5)
LOG2E = 1.4426950408889634
SCORE_SCALE = SCALE * LOG2E
MASKED = -1e30
LOWEST = -1e20
BF = jnp.bfloat16
F32 = jnp.float32

X, YH, CORES, YL, Z = 4, 2, 2, 2, 8
GROUP = 8
ROWS = 128
PROWS = 64
HALF_KV = 256
HALF_Q = 2048


def nt(a, b):
    return lax.dot_general(a, b, (((1,), (1,)), ((), ())), preferred_element_type=F32)


def nn(a, b):
    return lax.dot_general(a, b, (((1,), (0,)), ((), ())), preferred_element_type=F32)


def tn(a, b):
    return lax.dot_general(a, b, (((0,), (0,)), ((), ())), preferred_element_type=F32)


def kernel(
    q_ref, rk_ref, rv_ref, pk_ref, pv_ref, do_ref, owner_hbm, prompt_hbm, length_hbm, half_hbm,
    out_ref, gk_ref, gv_ref,
    q_near, q_far, do_near, do_far, out_near, out_far,
    resp, far_block, values_in, xbuf, chosen_out, chosen_in, prompt, v_turned,
    m_ref, acc_ref, lse_ref, delta_ref, gacc,
    zs_out, zs_in, share_out, share, core_in, xs_out, xs_in,
    owner_ref, prompt_ref, length_ref, half_ref,
    send_sem, recv_sem, local_sem,
):
    dp = lax.axis_index("dp")
    blk = lax.axis_index("blk")
    x, yh, c = dp // 4, (dp // 2) % 2, dp % 2
    yl, z = blk // Z, blk % Z
    other = 1 - yl
    y_id = (dp, other * Z + z)
    z_right, z_left = (dp, yl * Z + (z + 1) % Z), (dp, yl * Z + (z + Z - 1) % Z)
    x_right = (((x + 1) % X) * 4 + yh * 2 + c, blk)
    x_left = (((x + X - 1) % X) * 4 + yh * 2 + c, blk)
    core_id = (x * 4 + yh * 2 + (1 - c), blk)
    yh_id = (x * 4 + (1 - yh) * 2 + c, blk)
    far_x_id = (((x + 2) % X) * 4 + yh * 2 + c, blk)
    diagonal_id = (x * 4 + (1 - yh) * 2 + c, other * Z + z)

    def lanes(which, width):
        return pl.ds(pl.multiple_of(which * width, width), width)

    def head_lanes(half, a):
        return pl.ds(pl.multiple_of(half * HALF_KV + a * 128, 128), 128)

    def group_lanes(half, a):
        return pl.ds(pl.multiple_of(half * HALF_Q + a * 1024, 1024), 1024)

    mine_kv, far_kv = lanes(yl, HALF_KV), lanes(other, HALF_KV)
    mine_q = lanes(yl, HALF_Q)

    fetched = []

    def fetch(src, dst):
        copy = pltpu.make_async_copy(src, dst, local_sem.at[len(fetched)])
        copy.start()
        fetched.append(copy)
        return copy

    def present(copies):
        for copy in copies:
            copy.wait()

    own_prompt = [
        fetch(ref.at[0], xbuf.at[x, c, kv]) for kv, ref in enumerate((pk_ref, pv_ref))
    ]
    own_resp = [fetch(rv_ref.at[0], values_in)]
    own_resp += [
        fetch(rk_ref.at[0, :, head_lanes(half, a)], to.at[0, a])
        for half, to in ((yl, resp.at[z, yl]), (other, far_block))
        for a in range(2)
    ]
    tables = [
        fetch(owner_hbm, owner_ref), fetch(prompt_hbm, prompt_ref),
        fetch(length_hbm, length_ref), fetch(half_hbm, half_ref),
    ]
    own_q = fetch(q_ref.at[0, :, mine_q], q_near)
    own_do = fetch(do_ref.at[0, :, mine_q], do_near)

    barrier = pltpu.get_barrier_semaphore()
    peers = (y_id, z_right, z_left, x_right, x_left, core_id, yh_id, diagonal_id, far_x_id)
    for peer in peers:
        pl.semaphore_signal(barrier, inc=1, device_id=peer, device_id_type=MESH)
    pl.semaphore_wait(barrier, len(peers))

    started = []

    def send(src, dst, peer, begin=True):
        index = len(started)
        copy = pltpu.make_async_remote_copy(
            src_ref=src, dst_ref=dst, send_sem=send_sem.at[index], recv_sem=recv_sem.at[index],
            device_id=peer, device_id_type=MESH,
        )
        if begin:
            copy.start()
        started.append(copy)
        return copy

    def arrive(copies):
        for copy in copies:
            copy.wait_recv()

    x0 = [
        send(ref.at[0], xbuf.at[x, c, kv], peer)
        for peer in (x_right, x_left)
        for kv, ref in enumerate((pk_ref, pv_ref))
    ]
    y_q = [None, None]

    def send_queries(a):
        near, far = q_ref.at[0, :, group_lanes(other, a)], q_far.at[:, a * 1024 : a * 1024 + 1024]
        y_q[a] = send(near, far, y_id)

    own_keys = [
        send(rk_ref.at[0, :, head_lanes(yl, a)], resp.at[z, yl, 0, a], peer)
        for peer in (z_right, z_left)
        for a in range(2)
    ]
    send_queries(0)
    cores = [
        send(ref.at[0], xbuf.at[x, c, kv], core_id) for kv, ref in enumerate((pk_ref, pv_ref))
    ]

    def gather_step(slot, pos, n, step, right, left, begin=True):
        copies = []
        for way, peer in enumerate((right, left)):
            at = slot((pos + n - step) % n if way == 0 else (pos + step) % n)
            at = at.at[way] if step == n // 2 - 1 else at
            copies.append(send(at, at, peer, begin))
        return copies

    def resp_gather(y, step, begin=True):
        return gather_step(lambda i: resp.at[i, y], z, Z, step, z_right, z_left, begin)

    def prompt_gather(a, step, begin=True):
        return gather_step(lambda i: prompt.at[a, i], z, Z, step, z_right, z_left, begin)

    def core_send(i):
        return send(xbuf.at[i, c], xbuf.at[i, c], core_id)

    def head_of(near, far, h):
        columns = pl.ds(pl.multiple_of(h * 128, 128), 128)
        return jnp.concatenate([near[:, columns], far[:, columns]], axis=0)

    def turn_values():
        for half, to in ((yl, resp.at[z, yl]), (other, far_block)):
            for a in range(2):
                to[1, a] = values_in[:, head_lanes(half, a)].T

    present(tables)
    lane = lax.broadcasted_iota(jnp.int32, (1, 2 * ROWS), 1)
    last = length_ref[dp] - 1
    limit = jnp.zeros((1, 2 * ROWS), jnp.int32)
    for part, holder in enumerate((blk, other * Z + z)):
        for e in range(2):
            block = part * 2 + e
            inside = (lane >= block * 64) & (lane < block * 64 + 64)
            limit = jnp.where(inside, half_ref[2 * holder + e] * 64 + lane - block * 64, limit)
    limit = jnp.minimum(limit, last)
    down = lax.broadcasted_iota(jnp.int32, (64, 2 * ROWS), 0)

    def prompt_rows(slots, kv, a):
        return [prompt[a, i, kv].reshape(2 * PROWS, 128) for i in slots]

    def absorb(a, resp_slots, prompt_slots, between=None):
        bounds = []
        for i, y in resp_slots:
            bounds += [limit - half_ref[2 * (y * Z + i) + e] * 64 for e in range(2)]
        bounds += [None] * (2 * len(prompt_slots))
        count = 64 * len(bounds)

        keys = [resp[i, y, 0, a] for i, y in resp_slots] + prompt_rows(prompt_slots, 0, a)
        keys = jnp.concatenate(keys, axis=0)
        for n, part in enumerate(prompt_rows(prompt_slots, 1, a)):
            v_turned[:, n * 128 : n * 128 + 128] = part.T

        def score(query):
            pieces, tops = [], []
            scores = nt(keys, query) * SCORE_SCALE
            for n, bound in enumerate(bounds):
                piece = scores[64 * n : 64 * n + 64]
                if bound is not None:
                    piece = jnp.where(down <= bound, piece, MASKED)
                tops.append(jnp.max(piece.reshape(8, 8, 2 * ROWS), axis=0))
                pieces.append(piece)
            while len(tops) > 1:
                tops = [
                    jnp.maximum(tops[i], tops[i + 1]) if i + 1 < len(tops) else tops[i]
                    for i in range(0, len(tops), 2)
                ]
            return jnp.concatenate(pieces, axis=0), jnp.max(tops[0], axis=0, keepdims=True)

        def body(t, carry):
            first = a * GROUP + t * 4
            heads = pl.ds(first, 4)
            values = [resp[i, y, 1, a] for i, y in resp_slots]
            if prompt_slots:
                values.append(v_turned[:, : 128 * len(prompt_slots)])
            values = jnp.concatenate(values, axis=1) if len(values) > 1 else values[0]
            values = jnp.concatenate([values, jnp.ones((16, count), BF)], axis=0)
            old, old_mixed = m_ref[heads], acc_ref[heads]
            peaks, mixes = [], []

            def weigh(j, scores, top):
                peak = jnp.maximum(old[j], top)
                weights = jnp.exp2(scores - peak).astype(BF)
                peaks.append(peak)
                mixes.append(old_mixed[j] * jnp.exp2(old[j] - peak) + nn(values, weights))

            ready = score(head_of(q_near, q_far, first))
            for j in range(4):
                following = score(head_of(q_near, q_far, first + j + 1)) if j < 3 else None
                weigh(j, *ready)
                ready = following
            for j in range(4):
                m_ref[first + j] = peaks[j]
                acc_ref[first + j] = mixes[j]
            if between is not None:
                pl.when(t == 0)(between)
            return carry

        lax.fori_loop(0, 2, body, 0)

    def finish(a):
        def body(t, carry):
            first = a * GROUP + t * 4
            heads = pl.ds(first, 4)
            peak, mixed = m_ref[heads], acc_ref[heads]
            outs, sums, deltas = [], [], []
            for j in range(4):
                total = mixed[j, 128:129]
                result = (mixed[j, :128] / total).T
                sums.append(peak[j] + jnp.log(total) * LOG2E)
                product = result * head_of(do_near, do_far, first + j).astype(F32)
                high = product.astype(BF)
                low = (product - high.astype(F32)).astype(BF)
                halves = jnp.concatenate([high, low], axis=1)
                deltas.append(nt(jnp.ones((16, 256), BF), halves)[:1])
                outs.append(result.astype(BF))
            for j in range(4):
                h = first + j
                lse_ref[h] = sums[j]
                delta_ref[h] = deltas[j]
                columns = pl.ds(pl.multiple_of(h * 128, 128), 128)
                out_near[:, columns] = outs[j][:ROWS]
                out_far[:, columns] = outs[j][ROWS:]
            return carry

        lax.fori_loop(0, 2, body, 0)
        return send(
            out_far.at[:, a * 1024 : a * 1024 + 1024], out_ref.at[0, :, group_lanes(yl, a)], y_id
        )

    def gradients(a, slots):
        keys = jnp.concatenate(prompt_rows(slots, 0, a), axis=0)
        values = jnp.concatenate(prompt_rows(slots, 1, a), axis=0)
        heads = range(a * GROUP, a * GROUP + GROUP)
        queries = [head_of(q_near, q_far, h) for h in heads]
        cotangents = [head_of(do_near, do_far, h) for h in heads]
        all_probs, all_slopes = [], []
        for h, query, cotangent in zip(heads, queries, cotangents):
            probs = jnp.exp2(nt(keys, query) * SCORE_SCALE - lse_ref[h])
            slopes = probs * (nt(values, cotangent) - delta_ref[h])
            all_probs.append(probs.astype(BF))
            all_slopes.append(slopes.astype(BF))
        queries = jnp.concatenate(queries, axis=0)
        cotangents = jnp.concatenate(cotangents, axis=0)
        key_part = nn(jnp.concatenate(all_slopes, axis=1), queries) * SCALE
        value_part = nn(jnp.concatenate(all_probs, axis=1), cotangents)
        for n in range(len(slots)):
            gacc[n, 0] = key_part[n * 128 : n * 128 + 128].reshape(2, PROWS, 128)
            gacc[n, 1] = value_part[n * 128 : n * 128 + 128].reshape(2, PROWS, 128)

    def z_scatter(a, step):
        copies = []
        for way, peer in enumerate((z_right, z_left)):
            n = 0 if step == 0 else way
            for h in (way,) if step == 0 else (0, 1):
                part = gacc[n, h]
                if step > 1 or (step == 1 and h == way):
                    part = part + zs_in[a, way, step - 1, h].astype(F32)
                zs_out[a, way, step, h] = part.astype(BF)
            src, dst = zs_out.at[a, way, step], zs_in.at[a, way, step]
            if step == 0:
                src, dst = src.at[way], dst.at[way]
            copies.append(send(src, dst, peer))
        return copies

    def to_y_ring(a):
        for h in range(2):
            for n, where in enumerate((yl, other)):
                total = gacc[0, h, where]
                for way in range(2):
                    total = total + zs_in[a, way, 3, h, where].astype(F32)
                (share.at[a, 0, 0] if n == 0 else share_out.at[a])[h] = total.astype(BF)
        return [
            send(share_out.at[a], share.at[a, 0, 1], y_id),
            send(share.at[a, 0, 0], share.at[a, 1, 0], yh_id),
            send(share_out.at[a], share.at[a, 1, 1], diagonal_id),
        ]

    def to_core(a):
        return [send(share.at[a], core_in.at[a], core_id)]

    owners = []
    for source_core in (c, 1 - c):
        for source_half in (yh, 1 - yh):
            owners.append(owner_ref[prompt_ref[x * 4 + source_half * 2 + source_core]])

    def destined(a, target, h):
        total = jnp.zeros((2, PROWS, 128), F32)
        for n, owner in enumerate(owners):
            part = (share if n < 2 else core_in)[a, n % 2, :, h].astype(F32)
            total = total + jnp.where(owner == target * 4 + yh * 2 + c, part, 0.0)
        return total

    def x_scatter(a):
        copies = []
        for n, (distance, peer) in enumerate(((2, far_x_id), (1, x_right), (3, x_left))):
            for h in range(2):
                xs_out[a, n, h] = destined(a, (x + distance) % X, h).astype(BF)
            copies.append(send(xs_out.at[a, n], xs_in.at[a, n], peer))
        return copies

    def store(a):
        for h, ref in enumerate((gk_ref, gv_ref)):
            total = destined(a, x, h)
            for n in range(3):
                total = total + xs_in[a, n, h].astype(F32)
            ref[0, :, head_lanes(yl, a)] = total[0]
            ref[0, :, head_lanes(other, a)] = total[1]

    drained = []

    def drain():
        for copy in started[len(drained) :]:
            copy.wait_send()
            drained.append(copy)

    m_ref[...] = jnp.full(m_ref.shape, LOWEST, F32)
    acc_ref[...] = jnp.zeros(acc_ref.shape, F32)

    def pair(step):
        return [(z + step) % Z, (z + Z - step) % Z]

    opposite = [(z + 4) % Z]
    p, r = [None, None], [None, None]
    own, far = 0, 1

    def exchange(held, which, following, now):
        previous, held[which] = held[which], following

        def act():
            arrive(previous)
            for copy in following:
                copy.start()

        if now:
            act()
        return act

    def pass_on(a, step, now=True):
        return exchange(p, a, prompt_gather(a, step, False), now)

    def pass_on_resp(which, step, now=True):
        return exchange(r, which, resp_gather(yl if which == own else other, step, False), now)

    def mine_at(slots):
        return [(i, yl) for i in slots]

    def theirs_at(slots):
        return [(i, other) for i in slots]

    present(own_resp)
    turn_values()
    r[own] = own_keys + [
        send(resp.at[z, yl, 1], resp.at[z, yl, 1], peer) for peer in (z_right, z_left)
    ]
    y_far = [send(far_block, resp.at[z, yl], y_id)]
    send_queries(1)
    arrive(x0)
    x1 = gather_step(lambda i: xbuf.at[i, c], x, X, 1, x_right, x_left)
    cores += [core_send((x + 1) % X), core_send((x + X - 1) % X)]
    present(own_prompt + [own_q, own_do])
    pass_on_resp(own, 1)
    arrive(x1)
    cores += [core_send((x + 2) % X)]
    arrive(y_far)
    r[far] = resp_gather(other, 0)
    arrive(cores)
    theirs = owner_ref[prompt_ref[x * 4 + (1 - yh) * 2 + c]]
    mine = owner_ref[prompt_ref[dp]]

    def piece(owner, half, a):
        return xbuf[owner // 4, owner % 2, :, :, head_lanes(half, a)]

    ring = []
    for n, (owner, half, peer) in enumerate(
        ((mine, other, y_id), (theirs, yl, yh_id), (theirs, other, diagonal_id))
    ):
        for a in range(2):
            chosen_out[n, a] = piece(owner, half, a)
        ring.append(send(chosen_out.at[n], chosen_in.at[n], peer))
    pass_on_resp(own, 2)
    arrive([y_q[0]])
    absorb(0, mine_at([z] + pair(1)), [])
    absorb(0, mine_at(pair(2)) + theirs_at([z]), [])
    pass_on_resp(far, 1)
    arrive(ring)
    here = (mine // 2) % 2 == yh
    for a in range(2):
        for kv in range(2):
            prompt[a, z, kv, yl] = jnp.where(here, piece(mine, yl, a)[kv], chosen_in[1, a, kv])
            prompt[a, z, kv, other] = jnp.where(here, chosen_in[0, a, kv], chosen_in[2, a, kv])
        p[a] = prompt_gather(a, 0)
    y_do = [
        send(do_ref.at[0, :, group_lanes(other, a)], do_far.at[:, a * 1024 : a * 1024 + 1024], y_id)
        for a in range(2)
    ]
    arrive([y_q[1]])
    absorb(1, mine_at([z] + pair(1)), [])
    pass_on_resp(own, 3)
    absorb(1, mine_at(pair(2)) + theirs_at([z]), [])
    pass_on(0, 1)
    pass_on(1, 1)
    absorb(0, mine_at(pair(3)) + theirs_at(pair(1)), [], pass_on_resp(far, 2, False))
    absorb(1, mine_at(pair(3)) + theirs_at(pair(1)), [], pass_on(0, 2, False))
    pass_on(1, 2)
    arrive(r[own])
    near = [z] + pair(1)
    absorb(0, mine_at(opposite) + theirs_at(pair(2)), near, pass_on_resp(far, 3, False))
    pass_on(0, 3)
    absorb(1, mine_at(opposite) + theirs_at(pair(2)), near, pass_on(1, 3, False))
    drain()
    arrive(r[far])
    absorb(0, theirs_at(pair(3) + opposite), pair(2))
    absorb(1, theirs_at(pair(3) + opposite), pair(2))
    arrive([y_do[0]])
    arrive(p[0])
    absorb(0, [], pair(3) + opposite)
    results = [finish(0)]
    gradients(0, opposite)
    s0 = z_scatter(0, 0)
    arrive([y_do[1]])
    arrive(p[1])
    absorb(1, [], pair(3) + opposite)
    results += [finish(1)]
    own_result = fetch(out_near, out_ref.at[0, :, mine_q])
    gradients(1, opposite)
    s1 = z_scatter(1, 0)
    gradients(0, pair(3))
    arrive(s0)
    s0 = z_scatter(0, 1)
    gradients(1, pair(3))
    arrive(s1)
    s1 = z_scatter(1, 1)
    gradients(0, pair(2))
    arrive(s0)
    s0 = z_scatter(0, 2)
    gradients(1, pair(2))
    arrive(s1)
    s1 = z_scatter(1, 2)
    gradients(0, pair(1))
    arrive(s0)
    s0 = z_scatter(0, 3)
    gradients(1, pair(1))
    arrive(s1)
    s1 = z_scatter(1, 3)
    gradients(0, [z])
    arrive(s0)

    t0 = to_y_ring(0)
    gradients(1, [z])
    arrive(t0)
    t0 = to_core(0)
    arrive(s1)
    t1 = to_y_ring(1)
    arrive(t0)
    t0 = x_scatter(0)
    drain()
    arrive(t1)
    t1 = to_core(1)
    arrive(t0)
    store(0)
    arrive(results)
    present([own_result])
    arrive(t1)
    t1 = x_scatter(1)
    drain()
    arrive(t1)
    store(1)


COPIES = 96
PIECES = 4


def copy_out(*refs):
    ins, outs, held = refs[:3], refs[3:6], refs[6:9]
    in_sem, out_sem = refs[9:]
    parts = [(0, slice(n * 1024, n * 1024 + 1024)) for n in range(PIECES)]
    parts += [(1, slice(0, 512)), (2, slice(0, 512))]

    def move(sources, targets, sem):
        return [
            pltpu.make_async_copy(sources[n].at[0, :, columns], targets[n].at[0, :, columns], sem.at[i])
            for i, (n, columns) in enumerate(parts)
        ]

    loads, stores = move(ins, held, in_sem), move(held, outs, out_sem)
    for copy in loads:
        copy.start()
    for load, save in zip(loads, stores):
        load.wait()
        save.start()
    for copy in stores:
        copy.wait()


def on_device(*arguments):
    block = (2, 2, PROWS, 128)
    vmem = pl.BlockSpec(memory_space=pltpu.VMEM)
    hbm = pl.BlockSpec(memory_space=pltpu.HBM)
    results = pl.pallas_call(
        kernel,
        out_shape=(
            jax.ShapeDtypeStruct((1, ROWS, 4096), BF),
            jax.ShapeDtypeStruct((1, PROWS, 512), F32),
            jax.ShapeDtypeStruct((1, PROWS, 512), F32),
        ),
        in_specs=[hbm] * 10,
        out_specs=(hbm, vmem, vmem),
        scratch_shapes=[
            pltpu.VMEM((ROWS, HALF_Q), BF),
            pltpu.VMEM((ROWS, HALF_Q), BF),
            pltpu.VMEM((ROWS, HALF_Q), BF),
            pltpu.VMEM((ROWS, HALF_Q), BF),
            pltpu.VMEM((ROWS, HALF_Q), BF),
            pltpu.VMEM((ROWS, HALF_Q), BF),
            pltpu.VMEM((Z, 2, 2, 2, 128, 128), BF),
            pltpu.VMEM((2, 2, 128, 128), BF),
            pltpu.VMEM((ROWS, 512), BF),
            pltpu.VMEM((X, 2, 2, PROWS, 512), BF),
            pltpu.VMEM((3, 2, 2, PROWS, 128), BF),
            pltpu.VMEM((3, 2, 2, PROWS, 128), BF),
            pltpu.VMEM((2, Z) + block, BF),
            pltpu.VMEM((128, 1024), BF),
            pltpu.VMEM((16, 1, 256), F32),
            pltpu.VMEM((16, 144, 256), F32),
            pltpu.VMEM((16, 1, 256), F32),
            pltpu.VMEM((16, 1, 256), F32),
            pltpu.VMEM((2,) + block, F32),
            pltpu.VMEM((2, 2, 4) + block, BF),
            pltpu.VMEM((2, 2, 4) + block, BF),
            pltpu.VMEM((2, 2, PROWS, 128), BF),
            pltpu.VMEM((2, 2) + block, BF),
            pltpu.VMEM((2, 2) + block, BF),
            pltpu.VMEM((2, 3) + block, BF),
            pltpu.VMEM((2, 3) + block, BF),
            pltpu.SMEM((16,), jnp.int32),
            pltpu.SMEM((16,), jnp.int32),
            pltpu.SMEM((16,), jnp.int32),
            pltpu.SMEM((32,), jnp.int32),
            pltpu.SemaphoreType.DMA((COPIES,)),
            pltpu.SemaphoreType.DMA((COPIES,)),
            pltpu.SemaphoreType.DMA((16,)),
        ],
        compiler_params=pltpu.CompilerParams(
            collective_id=0, has_side_effects=True, vmem_limit_bytes=60 * 1024 * 1024
        ),
        cost_estimate=pl.CostEstimate(
            flops=10_000_000_000, bytes_accessed=8 * 1024 * 1024, transcendentals=17_000_000
        ),
    )(*arguments)
    return pl.pallas_call(
        copy_out,
        out_shape=tuple(jax.ShapeDtypeStruct(r.shape, r.dtype) for r in results),
        in_specs=[pl.BlockSpec(memory_space=pl.ANY)] * 3,
        out_specs=(hbm,) * 3,
        scratch_shapes=[pltpu.VMEM(r.shape, r.dtype) for r in results]
        + [pltpu.SemaphoreType.DMA((PIECES + 2,))] * 2,
        compiler_params=pltpu.CompilerParams(vmem_limit_bytes=60 * 1024 * 1024),
    )(*results)


def solution(mesh):
    split = P("dp", "blk", None)
    return jax.shard_map(
        on_device,
        mesh=mesh,
        in_specs=(split,) * 6 + (P(),) * 4,
        out_specs=(split, split, split),
        check_vma=False,
    )
```

```python
import jax
import jax.numpy as jnp
from jax import lax
from jax.experimental import pallas as pl
from jax.experimental.pallas import tpu as pltpu
from jax.sharding import PartitionSpec as P

MESH = pl.DeviceIdType.MESH
HEAD_WIDTH = 128
SCALE = HEAD_WIDTH ** (-0.5)
LOG2E = 1.4426950408889634
SCORE_SCALE = SCALE * LOG2E
MASKED = -1e30
LOWEST = -1e20
BF = jnp.bfloat16
F32 = jnp.float32

X, YH, CORES, YL, Z = 4, 2, 2, 2, 8
GROUP = 8
ROWS = 128
PROWS = 64
HALF_KV = 256
HALF_Q = 2048


def nt(a, b):
    return lax.dot_general(a, b, (((1,), (1,)), ((), ())), preferred_element_type=F32)


def nn(a, b):
    return lax.dot_general(a, b, (((1,), (0,)), ((), ())), preferred_element_type=F32)


def tn(a, b):
    return lax.dot_general(a, b, (((0,), (0,)), ((), ())), preferred_element_type=F32)


def kernel(
    q_ref, rk_ref, rv_ref, pk_ref, pv_ref, do_ref, owner_hbm, prompt_hbm, length_hbm, half_hbm,
    out_ref, gk_ref, gv_ref,
    q_near, q_far, do_near, do_far, out_near, out_far,
    resp, far_block, values_in, xbuf, chosen_out, chosen_in, prompt, v_turned,
    m_ref, acc_ref, lse_ref, delta_ref, gacc,
    zs_out, zs_in, share_out, share, core_in, xs_out, xs_in,
    owner_ref, prompt_ref, length_ref, half_ref,
    send_sem, recv_sem, local_sem,
):
    dp = lax.axis_index("dp")
    blk = lax.axis_index("blk")
    x, yh, c = dp // 4, (dp // 2) % 2, dp % 2
    yl, z = blk // Z, blk % Z
    other = 1 - yl
    y_id = (dp, other * Z + z)
    z_right, z_left = (dp, yl * Z + (z + 1) % Z), (dp, yl * Z + (z + Z - 1) % Z)
    x_right = (((x + 1) % X) * 4 + yh * 2 + c, blk)
    x_left = (((x + X - 1) % X) * 4 + yh * 2 + c, blk)
    core_id = (x * 4 + yh * 2 + (1 - c), blk)
    yh_id = (x * 4 + (1 - yh) * 2 + c, blk)
    far_x_id = (((x + 2) % X) * 4 + yh * 2 + c, blk)
    diagonal_id = (x * 4 + (1 - yh) * 2 + c, other * Z + z)

    def lanes(which, width):
        return pl.ds(pl.multiple_of(which * width, width), width)

    def head_lanes(half, a):
        return pl.ds(pl.multiple_of(half * HALF_KV + a * 128, 128), 128)

    def group_lanes(half, a):
        return pl.ds(pl.multiple_of(half * HALF_Q + a * 1024, 1024), 1024)

    mine_kv, far_kv = lanes(yl, HALF_KV), lanes(other, HALF_KV)
    mine_q = lanes(yl, HALF_Q)

    fetched = []

    def fetch(src, dst):
        copy = pltpu.make_async_copy(src, dst, local_sem.at[len(fetched)])
        copy.start()
        fetched.append(copy)
        return copy

    def present(copies):
        for copy in copies:
            copy.wait()

    own_prompt = [
        fetch(ref.at[0], xbuf.at[x, c, kv]) for kv, ref in enumerate((pk_ref, pv_ref))
    ]
    own_resp = [fetch(rv_ref.at[0], values_in)]
    own_resp += [
        fetch(rk_ref.at[0, :, head_lanes(half, a)], to.at[0, a])
        for half, to in ((yl, resp.at[z, yl]), (other, far_block))
        for a in range(2)
    ]
    tables = [
        fetch(owner_hbm, owner_ref), fetch(prompt_hbm, prompt_ref),
        fetch(length_hbm, length_ref), fetch(half_hbm, half_ref),
    ]
    own_q = fetch(q_ref.at[0, :, mine_q], q_near)
    own_do = fetch(do_ref.at[0, :, mine_q], do_near)

    barrier = pltpu.get_barrier_semaphore()
    peers = (y_id, z_right, z_left, x_right, x_left, core_id, yh_id, diagonal_id, far_x_id)
    for peer in peers:
        pl.semaphore_signal(barrier, inc=1, device_id=peer, device_id_type=MESH)
    pl.semaphore_wait(barrier, len(peers))

    started = []

    def send(src, dst, peer, begin=True):
        index = len(started)
        copy = pltpu.make_async_remote_copy(
            src_ref=src, dst_ref=dst, send_sem=send_sem.at[index], recv_sem=recv_sem.at[index],
            device_id=peer, device_id_type=MESH,
        )
        if begin:
            copy.start()
        started.append(copy)
        return copy

    def arrive(copies):
        for copy in copies:
            copy.wait_recv()

    x0 = [
        send(ref.at[0], xbuf.at[x, c, kv], peer)
        for peer in (x_right, x_left)
        for kv, ref in enumerate((pk_ref, pv_ref))
    ]
    y_q = [None, None]

    def send_queries(a):
        near, far = q_ref.at[0, :, group_lanes(other, a)], q_far.at[:, a * 1024 : a * 1024 + 1024]
        y_q[a] = send(near, far, y_id)

    own_keys = [
        send(rk_ref.at[0, :, head_lanes(yl, a)], resp.at[z, yl, 0, a], peer)
        for peer in (z_right, z_left)
        for a in range(2)
    ]
    send_queries(0)
    cores = [
        send(ref.at[0], xbuf.at[x, c, kv], core_id) for kv, ref in enumerate((pk_ref, pv_ref))
    ]

    def gather_step(slot, pos, n, step, right, left, begin=True):
        copies = []
        for way, peer in enumerate((right, left)):
            at = slot((pos + n - step) % n if way == 0 else (pos + step) % n)
            at = at.at[way] if step == n // 2 - 1 else at
            copies.append(send(at, at, peer, begin))
        return copies

    def resp_gather(y, step, begin=True):
        return gather_step(lambda i: resp.at[i, y], z, Z, step, z_right, z_left, begin)

    def prompt_gather(a, step, begin=True):
        return gather_step(lambda i: prompt.at[a, i], z, Z, step, z_right, z_left, begin)

    def core_send(i):
        return send(xbuf.at[i, c], xbuf.at[i, c], core_id)

    def head_of(near, far, h):
        columns = pl.ds(pl.multiple_of(h * 128, 128), 128)
        return jnp.concatenate([near[:, columns], far[:, columns]], axis=0)

    def turn_values():
        for half, to in ((yl, resp.at[z, yl]), (other, far_block)):
            for a in range(2):
                to[1, a] = values_in[:, head_lanes(half, a)].T

    present(tables)
    lane = lax.broadcasted_iota(jnp.int32, (1, 2 * ROWS), 1)
    last = length_ref[dp] - 1
    limit = jnp.zeros((1, 2 * ROWS), jnp.int32)
    for part, holder in enumerate((blk, other * Z + z)):
        for e in range(2):
            block = part * 2 + e
            inside = (lane >= block * 64) & (lane < block * 64 + 64)
            limit = jnp.where(inside, half_ref[2 * holder + e] * 64 + lane - block * 64, limit)
    limit = jnp.minimum(limit, last)
    down = lax.broadcasted_iota(jnp.int32, (64, 2 * ROWS), 0)

    def prompt_rows(slots, kv, a):
        return [prompt[a, i, kv].reshape(2 * PROWS, 128) for i in slots]

    def absorb(a, resp_slots, prompt_slots, between=None):
        bounds = []
        for i, y in resp_slots:
            bounds += [limit - half_ref[2 * (y * Z + i) + e] * 64 for e in range(2)]
        bounds += [None] * (2 * len(prompt_slots))
        count = 64 * len(bounds)

        keys = [resp[i, y, 0, a] for i, y in resp_slots] + prompt_rows(prompt_slots, 0, a)
        keys = jnp.concatenate(keys, axis=0)
        for n, part in enumerate(prompt_rows(prompt_slots, 1, a)):
            v_turned[:, n * 128 : n * 128 + 128] = part.T

        def score(query):
            pieces, tops = [], []
            scores = nt(keys, query) * SCORE_SCALE
            for n, bound in enumerate(bounds):
                piece = scores[64 * n : 64 * n + 64]
                if bound is not None:
                    piece = jnp.where(down <= bound, piece, MASKED)
                tops.append(jnp.max(piece.reshape(8, 8, 2 * ROWS), axis=0))
                pieces.append(piece)
            while len(tops) > 1:
                tops = [
                    jnp.maximum(tops[i], tops[i + 1]) if i + 1 < len(tops) else tops[i]
                    for i in range(0, len(tops), 2)
                ]
            return jnp.concatenate(pieces, axis=0), jnp.max(tops[0], axis=0, keepdims=True)

        def body(t, carry):
            first = a * GROUP + t * 4
            heads = pl.ds(first, 4)
            values = [resp[i, y, 1, a] for i, y in resp_slots]
            if prompt_slots:
                values.append(v_turned[:, : 128 * len(prompt_slots)])
            values = jnp.concatenate(values, axis=1) if len(values) > 1 else values[0]
            values = jnp.concatenate([values, jnp.ones((16, count), BF)], axis=0)
            old, old_mixed = m_ref[heads], acc_ref[heads]
            peaks, mixes = [], []

            def weigh(j, scores, top):
                peak = jnp.maximum(old[j], top)
                weights = jnp.exp2(scores - peak).astype(BF)
                peaks.append(peak)
                mixes.append(old_mixed[j] * jnp.exp2(old[j] - peak) + nn(values, weights))

            ready = score(head_of(q_near, q_far, first))
            for j in range(4):
                following = score(head_of(q_near, q_far, first + j + 1)) if j < 3 else None
                weigh(j, *ready)
                ready = following
            for j in range(4):
                m_ref[first + j] = peaks[j]
                acc_ref[first + j] = mixes[j]
            if between is not None:
                pl.when(t == 0)(between)
            return carry

        lax.fori_loop(0, 2, body, 0)

    def finish(a):
        def body(t, carry):
            first = a * GROUP + t * 4
            heads = pl.ds(first, 4)
            peak, mixed = m_ref[heads], acc_ref[heads]
            outs, sums, deltas = [], [], []
            for j in range(4):
                total = mixed[j, 128:129]
                result = (mixed[j, :128] / total).T
                sums.append(peak[j] + jnp.log(total) * LOG2E)
                product = result * head_of(do_near, do_far, first + j).astype(F32)
                high = product.astype(BF)
                low = (product - high.astype(F32)).astype(BF)
                halves = jnp.concatenate([high, low], axis=1)
                deltas.append(nt(jnp.ones((16, 256), BF), halves)[:1])
                outs.append(result.astype(BF))
            for j in range(4):
                h = first + j
                lse_ref[h] = sums[j]
                delta_ref[h] = deltas[j]
                columns = pl.ds(pl.multiple_of(h * 128, 128), 128)
                out_near[:, columns] = outs[j][:ROWS]
                out_far[:, columns] = outs[j][ROWS:]
            return carry

        lax.fori_loop(0, 2, body, 0)
        return send(
            out_far.at[:, a * 1024 : a * 1024 + 1024], out_ref.at[0, :, group_lanes(yl, a)], y_id
        )

    def gradients(a, slots):
        keys = jnp.concatenate(prompt_rows(slots, 0, a), axis=0)
        values = jnp.concatenate(prompt_rows(slots, 1, a), axis=0)
        heads = range(a * GROUP, a * GROUP + GROUP)
        queries = [head_of(q_near, q_far, h) for h in heads]
        cotangents = [head_of(do_near, do_far, h) for h in heads]
        all_probs, all_slopes = [], []
        for h, query, cotangent in zip(heads, queries, cotangents):
            probs = jnp.exp2(nt(keys, query) * SCORE_SCALE - lse_ref[h])
            slopes = probs * (nt(values, cotangent) - delta_ref[h])
            all_probs.append(probs.astype(BF))
            all_slopes.append(slopes.astype(BF))
        queries = jnp.concatenate(queries, axis=0)
        cotangents = jnp.concatenate(cotangents, axis=0)
        key_part = nn(jnp.concatenate(all_slopes, axis=1), queries) * SCALE
        value_part = nn(jnp.concatenate(all_probs, axis=1), cotangents)
        for n in range(len(slots)):
            gacc[n, 0] = key_part[n * 128 : n * 128 + 128].reshape(2, PROWS, 128)
            gacc[n, 1] = value_part[n * 128 : n * 128 + 128].reshape(2, PROWS, 128)

    def z_scatter(a, step):
        copies = []
        for way, peer in enumerate((z_right, z_left)):
            n = 0 if step == 0 else way
            for h in (way,) if step == 0 else (0, 1):
                part = gacc[n, h]
                if step > 1 or (step == 1 and h == way):
                    part = part + zs_in[a, way, step - 1, h].astype(F32)
                zs_out[a, way, step, h] = part.astype(BF)
            src, dst = zs_out.at[a, way, step], zs_in.at[a, way, step]
            if step == 0:
                src, dst = src.at[way], dst.at[way]
            copies.append(send(src, dst, peer))
        return copies

    def to_y_ring(a):
        for h in range(2):
            for n, where in enumerate((yl, other)):
                total = gacc[0, h, where]
                for way in range(2):
                    total = total + zs_in[a, way, 3, h, where].astype(F32)
                (share.at[a, 0, 0] if n == 0 else share_out.at[a])[h] = total.astype(BF)
        return [
            send(share_out.at[a], share.at[a, 0, 1], y_id),
            send(share.at[a, 0, 0], share.at[a, 1, 0], yh_id),
            send(share_out.at[a], share.at[a, 1, 1], diagonal_id),
        ]

    def to_core(a):
        return [send(share.at[a], core_in.at[a], core_id)]

    owners = []
    for source_core in (c, 1 - c):
        for source_half in (yh, 1 - yh):
            owners.append(owner_ref[prompt_ref[x * 4 + source_half * 2 + source_core]])

    def destined(a, target, h):
        total = jnp.zeros((2, PROWS, 128), F32)
        for n, owner in enumerate(owners):
            part = (share if n < 2 else core_in)[a, n % 2, :, h].astype(F32)
            total = total + jnp.where(owner == target * 4 + yh * 2 + c, part, 0.0)
        return total

    def x_scatter(a):
        copies = []
        for n, (distance, peer) in enumerate(((2, far_x_id), (1, x_right), (3, x_left))):
            for h in range(2):
                xs_out[a, n, h] = destined(a, (x + distance) % X, h).astype(BF)
            copies.append(send(xs_out.at[a, n], xs_in.at[a, n], peer))
        return copies

    def store(a):
        for h, ref in enumerate((gk_ref, gv_ref)):
            total = destined(a, x, h)
            for n in range(3):
                total = total + xs_in[a, n, h].astype(F32)
            ref[0, :, head_lanes(yl, a)] = total[0]
            ref[0, :, head_lanes(other, a)] = total[1]

    drained = []

    def drain(but=0):
        for copy in started[len(drained) : len(started) - but]:
            copy.wait_send()
            drained.append(copy)

    m_ref[...] = jnp.full(m_ref.shape, LOWEST, F32)
    acc_ref[...] = jnp.zeros(acc_ref.shape, F32)

    def pair(step):
        return [(z + step) % Z, (z + Z - step) % Z]

    opposite = [(z + 4) % Z]
    p, r = [None, None], [None, None]
    own, far = 0, 1

    def exchange(held, which, following, now):
        previous, held[which] = held[which], following

        def act():
            arrive(previous)
            for copy in following:
                copy.start()

        if now:
            act()
        return act

    def pass_on(a, step, now=True):
        return exchange(p, a, prompt_gather(a, step, False), now)

    def pass_on_resp(which, step, now=True):
        return exchange(r, which, resp_gather(yl if which == own else other, step, False), now)

    def mine_at(slots):
        return [(i, yl) for i in slots]

    def theirs_at(slots):
        return [(i, other) for i in slots]

    present(own_resp)
    turn_values()
    r[own] = own_keys + [
        send(resp.at[z, yl, 1], resp.at[z, yl, 1], peer) for peer in (z_right, z_left)
    ]
    y_far = [send(far_block, resp.at[z, yl], y_id)]
    send_queries(1)
    arrive(x0)
    x1 = gather_step(lambda i: xbuf.at[i, c], x, X, 1, x_right, x_left)
    cores += [core_send((x + 1) % X), core_send((x + X - 1) % X)]
    present(own_prompt + [own_q, own_do])
    pass_on_resp(own, 1)
    arrive([y_q[0]])
    last_core = [send(xbuf.at[(x + 2) % X, c], xbuf.at[(x + 2) % X, c], core_id, False)]
    cores += last_core

    def feed_core():
        arrive(x1)
        last_core[0].start()

    absorb(0, mine_at([z] + pair(1)), [], feed_core)
    arrive(y_far)
    r[far] = resp_gather(other, 0)
    arrive(cores)
    theirs = owner_ref[prompt_ref[x * 4 + (1 - yh) * 2 + c]]
    mine = owner_ref[prompt_ref[dp]]

    def piece(owner, half, a):
        return xbuf[owner // 4, owner % 2, :, :, head_lanes(half, a)]

    ring = []
    for n, (owner, half, peer) in enumerate(
        ((mine, other, y_id), (theirs, yl, yh_id), (theirs, other, diagonal_id))
    ):
        for a in range(2):
            chosen_out[n, a] = piece(owner, half, a)
        ring.append(send(chosen_out.at[n], chosen_in.at[n], peer))
    pass_on_resp(own, 2)
    absorb(0, mine_at(pair(2)) + theirs_at([z]), [])
    pass_on_resp(far, 1)
    arrive(ring)
    here = (mine // 2) % 2 == yh
    for a in range(2):
        for kv in range(2):
            prompt[a, z, kv, yl] = jnp.where(here, piece(mine, yl, a)[kv], chosen_in[1, a, kv])
            prompt[a, z, kv, other] = jnp.where(here, chosen_in[0, a, kv], chosen_in[2, a, kv])
        p[a] = prompt_gather(a, 0, a == 0)
    y_do = [
        send(do_ref.at[0, :, group_lanes(other, a)], do_far.at[:, a * 1024 : a * 1024 + 1024], y_id)
        for a in range(2)
    ]
    arrive([y_q[1]])
    absorb(1, mine_at([z] + pair(1)), [])
    pass_on_resp(own, 3)
    absorb(1, mine_at(pair(2)) + theirs_at([z]), [])
    pass_on(0, 1)
    for copy in p[1]:
        copy.start()
    absorb(0, mine_at(pair(3)) + theirs_at(pair(1)), [], pass_on_resp(far, 2, False))
    pass_on(0, 2)
    pass_on(1, 1)
    absorb(1, mine_at(pair(3)) + theirs_at(pair(1)), [])
    arrive(r[own])
    near = [z] + pair(1)
    absorb(0, mine_at(opposite) + theirs_at(pair(2)), near, pass_on_resp(far, 3, False))
    pass_on(0, 3)
    pass_on(1, 2)
    absorb(1, mine_at(opposite) + theirs_at(pair(2)), near)
    drain()
    arrive(r[far])
    absorb(0, theirs_at(pair(3) + opposite), pair(2), pass_on(1, 3, False))
    arrive([y_do[0]])
    arrive(p[0])
    absorb(0, [], pair(3) + opposite)
    results = [finish(0)]
    gradients(0, opposite)
    s0 = z_scatter(0, 0)
    absorb(1, theirs_at(pair(3) + opposite), pair(2))
    gradients(0, pair(3))
    arrive(s0)
    s0 = z_scatter(0, 1)
    arrive([y_do[1]])
    arrive(p[1])
    absorb(1, [], pair(3) + opposite)
    results += [finish(1)]
    own_result = fetch(out_near, out_ref.at[0, :, mine_q])
    gradients(1, opposite)
    s1 = z_scatter(1, 0)
    gradients(0, pair(2))
    arrive(s0)
    s0 = z_scatter(0, 2)
    gradients(1, pair(3))
    arrive(s1)
    s1 = z_scatter(1, 1)
    gradients(0, pair(1))
    arrive(s0)
    s0 = z_scatter(0, 3)
    gradients(1, pair(2))
    arrive(s1)
    s1 = z_scatter(1, 2)
    gradients(0, [z])
    arrive(s0)

    t0 = to_y_ring(0)
    gradients(1, pair(1))
    arrive(s1)
    s1 = z_scatter(1, 3)
    arrive(t0)
    t0 = to_core(0)
    gradients(1, [z])
    arrive(t0)
    t0 = x_scatter(0)
    arrive(s1)
    t1 = to_y_ring(1)
    drain(6)
    arrive(t1)
    t1 = to_core(1)
    arrive(t1)
    t1 = x_scatter(1)
    arrive(t0)
    store(0)
    arrive(results)
    present([own_result])
    drain()
    arrive(t1)
    store(1)


COPIES = 96
PIECES = 4


def copy_out(*refs):
    ins, outs, held = refs[:3], refs[3:6], refs[6:9]
    in_sem, out_sem = refs[9:]
    parts = [(0, slice(n * 1024, n * 1024 + 1024)) for n in range(PIECES)]
    parts += [(1, slice(0, 512)), (2, slice(0, 512))]

    def move(sources, targets, sem):
        return [
            pltpu.make_async_copy(sources[n].at[0, :, columns], targets[n].at[0, :, columns], sem.at[i])
            for i, (n, columns) in enumerate(parts)
        ]

    loads, stores = move(ins, held, in_sem), move(held, outs, out_sem)
    for copy in loads:
        copy.start()
    for load, save in zip(loads, stores):
        load.wait()
        save.start()
    for copy in stores:
        copy.wait()


def on_device(*arguments):
    block = (2, 2, PROWS, 128)
    vmem = pl.BlockSpec(memory_space=pltpu.VMEM)
    hbm = pl.BlockSpec(memory_space=pltpu.HBM)
    results = pl.pallas_call(
        kernel,
        out_shape=(
            jax.ShapeDtypeStruct((1, ROWS, 4096), BF),
            jax.ShapeDtypeStruct((1, PROWS, 512), F32),
            jax.ShapeDtypeStruct((1, PROWS, 512), F32),
        ),
        in_specs=[hbm] * 10,
        out_specs=(hbm, vmem, vmem),
        scratch_shapes=[
            pltpu.VMEM((ROWS, HALF_Q), BF),
            pltpu.VMEM((ROWS, HALF_Q), BF),
            pltpu.VMEM((ROWS, HALF_Q), BF),
            pltpu.VMEM((ROWS, HALF_Q), BF),
            pltpu.VMEM((ROWS, HALF_Q), BF),
            pltpu.VMEM((ROWS, HALF_Q), BF),
            pltpu.VMEM((Z, 2, 2, 2, 128, 128), BF),
            pltpu.VMEM((2, 2, 128, 128), BF),
            pltpu.VMEM((ROWS, 512), BF),
            pltpu.VMEM((X, 2, 2, PROWS, 512), BF),
            pltpu.VMEM((3, 2, 2, PROWS, 128), BF),
            pltpu.VMEM((3, 2, 2, PROWS, 128), BF),
            pltpu.VMEM((2, Z) + block, BF),
            pltpu.VMEM((128, 1024), BF),
            pltpu.VMEM((16, 1, 256), F32),
            pltpu.VMEM((16, 144, 256), F32),
            pltpu.VMEM((16, 1, 256), F32),
            pltpu.VMEM((16, 1, 256), F32),
            pltpu.VMEM((2,) + block, F32),
            pltpu.VMEM((2, 2, 4) + block, BF),
            pltpu.VMEM((2, 2, 4) + block, BF),
            pltpu.VMEM((2, 2, PROWS, 128), BF),
            pltpu.VMEM((2, 2) + block, BF),
            pltpu.VMEM((2, 2) + block, BF),
            pltpu.VMEM((2, 3) + block, BF),
            pltpu.VMEM((2, 3) + block, BF),
            pltpu.SMEM((16,), jnp.int32),
            pltpu.SMEM((16,), jnp.int32),
            pltpu.SMEM((16,), jnp.int32),
            pltpu.SMEM((32,), jnp.int32),
            pltpu.SemaphoreType.DMA((COPIES,)),
            pltpu.SemaphoreType.DMA((COPIES,)),
            pltpu.SemaphoreType.DMA((16,)),
        ],
        compiler_params=pltpu.CompilerParams(
            collective_id=0, has_side_effects=True, vmem_limit_bytes=60 * 1024 * 1024
        ),
        cost_estimate=pl.CostEstimate(
            flops=10_000_000_000, bytes_accessed=8 * 1024 * 1024, transcendentals=17_000_000
        ),
    )(*arguments)
    return pl.pallas_call(
        copy_out,
        out_shape=tuple(jax.ShapeDtypeStruct(r.shape, r.dtype) for r in results),
        in_specs=[pl.BlockSpec(memory_space=pl.ANY)] * 3,
        out_specs=(hbm,) * 3,
        scratch_shapes=[pltpu.VMEM(r.shape, r.dtype) for r in results]
        + [pltpu.SemaphoreType.DMA((PIECES + 2,))] * 2,
        compiler_params=pltpu.CompilerParams(vmem_limit_bytes=60 * 1024 * 1024),
    )(*results)


def solution(mesh):
    split = P("dp", "blk", None)
    return jax.shard_map(
        on_device,
        mesh=mesh,
        in_specs=(split,) * 6 + (P(),) * 4,
        out_specs=(split, split, split),
        check_vma=False,
    )
```

```python
import jax
import jax.numpy as jnp
from jax import lax
from jax.experimental import pallas as pl
from jax.experimental.pallas import tpu as pltpu
from jax.sharding import PartitionSpec as P

MESH = pl.DeviceIdType.MESH
HEAD_WIDTH = 128
SCALE = HEAD_WIDTH ** (-0.5)
LOG2E = 1.4426950408889634
SCORE_SCALE = SCALE * LOG2E
MASKED = -1e30
LOWEST = -1e20
BF = jnp.bfloat16
F32 = jnp.float32

X, YH, CORES, YL, Z = 4, 2, 2, 2, 8
GROUP = 8
ROWS = 128
PROWS = 64
HALF_KV = 256
HALF_Q = 2048


def nt(a, b):
    return lax.dot_general(a, b, (((1,), (1,)), ((), ())), preferred_element_type=F32)


def nn(a, b):
    return lax.dot_general(a, b, (((1,), (0,)), ((), ())), preferred_element_type=F32)


def tn(a, b):
    return lax.dot_general(a, b, (((0,), (0,)), ((), ())), preferred_element_type=F32)


def kernel(
    q_ref, rk_ref, rv_ref, pk_ref, pv_ref, do_ref, owner_hbm, prompt_hbm, length_hbm, half_hbm,
    out_ref, gk_ref, gv_ref,
    q_near, q_far, do_near, do_far, out_near, out_far, q_turned, do_turned,
    resp, far_block, values_in, xbuf, chosen_out, chosen_in, prompt, v_turned,
    m_ref, acc_ref, lse_ref, delta_ref, gacc,
    zs_out, zs_in, share_out, share, core_in, xs_out, xs_in,
    owner_ref, prompt_ref, length_ref, half_ref,
    send_sem, recv_sem, local_sem,
):
    dp = lax.axis_index("dp")
    blk = lax.axis_index("blk")
    x, yh, c = dp // 4, (dp // 2) % 2, dp % 2
    yl, z = blk // Z, blk % Z
    other = 1 - yl
    y_id = (dp, other * Z + z)
    z_right, z_left = (dp, yl * Z + (z + 1) % Z), (dp, yl * Z + (z + Z - 1) % Z)
    x_right = (((x + 1) % X) * 4 + yh * 2 + c, blk)
    x_left = (((x + X - 1) % X) * 4 + yh * 2 + c, blk)
    core_id = (x * 4 + yh * 2 + (1 - c), blk)
    yh_id = (x * 4 + (1 - yh) * 2 + c, blk)
    far_x_id = (((x + 2) % X) * 4 + yh * 2 + c, blk)
    diagonal_id = (x * 4 + (1 - yh) * 2 + c, other * Z + z)

    def lanes(which, width):
        return pl.ds(pl.multiple_of(which * width, width), width)

    def head_lanes(half, a):
        return pl.ds(pl.multiple_of(half * HALF_KV + a * 128, 128), 128)

    def group_lanes(half, a):
        return pl.ds(pl.multiple_of(half * HALF_Q + a * 1024, 1024), 1024)

    mine_kv, far_kv = lanes(yl, HALF_KV), lanes(other, HALF_KV)
    mine_q = lanes(yl, HALF_Q)

    fetched = []

    def fetch(src, dst):
        copy = pltpu.make_async_copy(src, dst, local_sem.at[len(fetched)])
        copy.start()
        fetched.append(copy)
        return copy

    def present(copies):
        for copy in copies:
            copy.wait()

    own_prompt = [
        fetch(ref.at[0], xbuf.at[x, c, kv]) for kv, ref in enumerate((pk_ref, pv_ref))
    ]
    own_resp = [fetch(rv_ref.at[0], values_in)]
    own_resp += [
        fetch(rk_ref.at[0, :, head_lanes(half, a)], to.at[0, a])
        for half, to in ((yl, resp.at[z, yl]), (other, far_block))
        for a in range(2)
    ]
    tables = [
        fetch(owner_hbm, owner_ref), fetch(prompt_hbm, prompt_ref),
        fetch(length_hbm, length_ref), fetch(half_hbm, half_ref),
    ]
    own_q = fetch(q_ref.at[0, :, mine_q], q_near)
    own_do = fetch(do_ref.at[0, :, mine_q], do_near)

    barrier = pltpu.get_barrier_semaphore()
    peers = (y_id, z_right, z_left, x_right, x_left, core_id, yh_id, diagonal_id, far_x_id)
    for peer in peers:
        pl.semaphore_signal(barrier, inc=1, device_id=peer, device_id_type=MESH)
    pl.semaphore_wait(barrier, len(peers))

    started = []

    def send(src, dst, peer, begin=True):
        index = len(started)
        copy = pltpu.make_async_remote_copy(
            src_ref=src, dst_ref=dst, send_sem=send_sem.at[index], recv_sem=recv_sem.at[index],
            device_id=peer, device_id_type=MESH,
        )
        if begin:
            copy.start()
        started.append(copy)
        return copy

    def arrive(copies):
        for copy in copies:
            copy.wait_recv()

    x0 = [
        send(ref.at[0], xbuf.at[x, c, kv], peer)
        for peer in (x_right, x_left)
        for kv, ref in enumerate((pk_ref, pv_ref))
    ]
    y_q = [None, None]

    def send_queries(a):
        near, far = q_ref.at[0, :, group_lanes(other, a)], q_far.at[:, a * 1024 : a * 1024 + 1024]
        y_q[a] = send(near, far, y_id)

    own_keys = [
        send(rk_ref.at[0, :, head_lanes(yl, a)], resp.at[z, yl, 0, a], peer)
        for peer in (z_right, z_left)
        for a in range(2)
    ]
    send_queries(0)
    cores = [
        send(ref.at[0], xbuf.at[x, c, kv], core_id) for kv, ref in enumerate((pk_ref, pv_ref))
    ]

    def gather_step(slot, pos, n, step, right, left, begin=True):
        copies = []
        for way, peer in enumerate((right, left)):
            at = slot((pos + n - step) % n if way == 0 else (pos + step) % n)
            at = at.at[way] if step == n // 2 - 1 else at
            copies.append(send(at, at, peer, begin))
        return copies

    def resp_gather(y, step, begin=True):
        return gather_step(lambda i: resp.at[i, y], z, Z, step, z_right, z_left, begin)

    def prompt_gather(a, step, begin=True):
        return gather_step(lambda i: prompt.at[a, i], z, Z, step, z_right, z_left, begin)

    def core_send(i):
        return send(xbuf.at[i, c], xbuf.at[i, c], core_id)

    def head_of(near, far, h):
        columns = pl.ds(pl.multiple_of(h * 128, 128), 128)
        return jnp.concatenate([near[:, columns], far[:, columns]], axis=0)

    def prepare(source, part, a, turned):
        def body(g, carry):
            h = a * GROUP + g
            tile = source[:, pl.ds(pl.multiple_of(h * 128, 128), 128)]
            turned[h, :, part * ROWS : (part + 1) * ROWS] = tile.T
            return carry

        lax.fori_loop(0, GROUP, body, 0, unroll=4)

    def turn_values():
        for half, to in ((yl, resp.at[z, yl]), (other, far_block)):
            for a in range(2):
                to[1, a] = values_in[:, head_lanes(half, a)].T

    present(tables)
    lane = lax.broadcasted_iota(jnp.int32, (1, 2 * ROWS), 1)
    last = length_ref[dp] - 1
    limit = jnp.zeros((1, 2 * ROWS), jnp.int32)
    for part, holder in enumerate((blk, other * Z + z)):
        for e in range(2):
            block = part * 2 + e
            inside = (lane >= block * 64) & (lane < block * 64 + 64)
            limit = jnp.where(inside, half_ref[2 * holder + e] * 64 + lane - block * 64, limit)
    limit = jnp.minimum(limit, last)
    down = lax.broadcasted_iota(jnp.int32, (64, 2 * ROWS), 0)

    def prompt_rows(slots, kv, a):
        return [prompt[a, i, kv].reshape(2 * PROWS, 128) for i in slots]

    def absorb(a, resp_slots, prompt_slots, between=None):
        bounds = []
        for i, y in resp_slots:
            bounds += [limit - half_ref[2 * (y * Z + i) + e] * 64 for e in range(2)]
        bounds += [None] * (2 * len(prompt_slots))
        count = 64 * len(bounds)

        keys = [resp[i, y, 0, a] for i, y in resp_slots] + prompt_rows(prompt_slots, 0, a)
        keys = jnp.concatenate(keys, axis=0)
        for n, part in enumerate(prompt_rows(prompt_slots, 1, a)):
            v_turned[:, n * 128 : n * 128 + 128] = part.T

        def score(query):
            pieces, tops = [], []
            scores = nn(keys, query) * SCORE_SCALE
            for n, bound in enumerate(bounds):
                piece = scores[64 * n : 64 * n + 64]
                if bound is not None:
                    piece = jnp.where(down <= bound, piece, MASKED)
                tops.append(jnp.max(piece.reshape(8, 8, 2 * ROWS), axis=0))
                pieces.append(piece)
            while len(tops) > 1:
                tops = [
                    jnp.maximum(tops[i], tops[i + 1]) if i + 1 < len(tops) else tops[i]
                    for i in range(0, len(tops), 2)
                ]
            return jnp.concatenate(pieces, axis=0), jnp.max(tops[0], axis=0, keepdims=True)

        def body(t, carry):
            first = a * GROUP + t * 4
            heads = pl.ds(first, 4)
            values = [resp[i, y, 1, a] for i, y in resp_slots]
            if prompt_slots:
                values.append(v_turned[:, : 128 * len(prompt_slots)])
            values = jnp.concatenate(values, axis=1) if len(values) > 1 else values[0]
            values = jnp.concatenate([values, jnp.ones((16, count), BF)], axis=0)
            old, old_mixed = m_ref[heads], acc_ref[heads]
            peaks, mixes = [], []

            def weigh(j, scores, top):
                peak = jnp.maximum(old[j], top)
                weights = jnp.exp2(scores - peak).astype(BF)
                peaks.append(peak)
                mixes.append(old_mixed[j] * jnp.exp2(old[j] - peak) + nn(values, weights))

            ready = score(q_turned[first])
            for j in range(4):
                following = score(q_turned[first + j + 1]) if j < 3 else None
                weigh(j, *ready)
                ready = following
            for j in range(4):
                m_ref[first + j] = peaks[j]
                acc_ref[first + j] = mixes[j]
            if between is not None:
                pl.when(t == 0)(between)
            return carry

        lax.fori_loop(0, 2, body, 0)

    def finish(a):
        def body(t, carry):
            first = a * GROUP + t * 4
            heads = pl.ds(first, 4)
            peak, mixed = m_ref[heads], acc_ref[heads]
            outs, logs, deltas = [], [], []
            for j in range(4):
                total = mixed[j, 128:129]
                result = mixed[j, :128] / total
                logs.append(peak[j] + jnp.log(total) * LOG2E)
                cotangent = do_turned[first + j].astype(F32)
                deltas.append(jnp.sum(cotangent * result, axis=0, keepdims=True))
                outs.append(result.T.astype(BF))
            for j in range(4):
                h = first + j
                lse_ref[h] = logs[j]
                delta_ref[h] = deltas[j]
                columns = pl.ds(pl.multiple_of(h * 128, 128), 128)
                out_near[:, columns] = outs[j][:ROWS]
                out_far[:, columns] = outs[j][ROWS:]
            return carry

        lax.fori_loop(0, 2, body, 0)
        return send(
            out_far.at[:, a * 1024 : a * 1024 + 1024], out_ref.at[0, :, group_lanes(yl, a)], y_id
        )

    def gradients(a, slots):
        keys = jnp.concatenate(prompt_rows(slots, 0, a), axis=0)
        values = jnp.concatenate(prompt_rows(slots, 1, a), axis=0)
        heads = range(a * GROUP, a * GROUP + GROUP)
        queries = [head_of(q_near, q_far, h) for h in heads]
        cotangents = [head_of(do_near, do_far, h) for h in heads]
        all_probs, all_slopes = [], []
        for h in heads:
            probs = jnp.exp2(nn(keys, q_turned[h]) * SCORE_SCALE - lse_ref[h])
            slopes = probs * (nn(values, do_turned[h]) - delta_ref[h])
            all_probs.append(probs.astype(BF))
            all_slopes.append(slopes.astype(BF))
        queries = jnp.concatenate(queries, axis=0)
        cotangents = jnp.concatenate(cotangents, axis=0)
        key_part = nn(jnp.concatenate(all_slopes, axis=1), queries) * SCALE
        value_part = nn(jnp.concatenate(all_probs, axis=1), cotangents)
        for n in range(len(slots)):
            gacc[n, 0] = key_part[n * 128 : n * 128 + 128].reshape(2, PROWS, 128)
            gacc[n, 1] = value_part[n * 128 : n * 128 + 128].reshape(2, PROWS, 128)

    def z_scatter(a, step):
        copies = []
        for way, peer in enumerate((z_right, z_left)):
            n = 0 if step == 0 else way
            for h in (way,) if step == 0 else (0, 1):
                part = gacc[n, h]
                if step > 1 or (step == 1 and h == way):
                    part = part + zs_in[a, way, step - 1, h].astype(F32)
                zs_out[a, way, step, h] = part.astype(BF)
            src, dst = zs_out.at[a, way, step], zs_in.at[a, way, step]
            if step == 0:
                src, dst = src.at[way], dst.at[way]
            copies.append(send(src, dst, peer))
        return copies

    def to_y_ring(a):
        for h in range(2):
            for n, where in enumerate((yl, other)):
                total = gacc[0, h, where]
                for way in range(2):
                    total = total + zs_in[a, way, 3, h, where].astype(F32)
                (share.at[a, 0, 0] if n == 0 else share_out.at[a])[h] = total.astype(BF)
        return [
            send(share_out.at[a], share.at[a, 0, 1], y_id),
            send(share.at[a, 0, 0], share.at[a, 1, 0], yh_id),
            send(share_out.at[a], share.at[a, 1, 1], diagonal_id),
        ]

    def to_core(a):
        return [send(share.at[a], core_in.at[a], core_id)]

    owners = []
    for source_core in (c, 1 - c):
        for source_half in (yh, 1 - yh):
            owners.append(owner_ref[prompt_ref[x * 4 + source_half * 2 + source_core]])

    def destined(a, target, h):
        total = jnp.zeros((2, PROWS, 128), F32)
        for n, owner in enumerate(owners):
            part = (share if n < 2 else core_in)[a, n % 2, :, h].astype(F32)
            total = total + jnp.where(owner == target * 4 + yh * 2 + c, part, 0.0)
        return total

    def x_scatter(a):
        copies = []
        for n, (distance, peer) in enumerate(((2, far_x_id), (1, x_right), (3, x_left))):
            for h in range(2):
                xs_out[a, n, h] = destined(a, (x + distance) % X, h).astype(BF)
            copies.append(send(xs_out.at[a, n], xs_in.at[a, n], peer))
        return copies

    def store(a):
        for h, ref in enumerate((gk_ref, gv_ref)):
            total = destined(a, x, h)
            for n in range(3):
                total = total + xs_in[a, n, h].astype(F32)
            ref[0, :, head_lanes(yl, a)] = total[0]
            ref[0, :, head_lanes(other, a)] = total[1]

    drained = []

    def drain(but=0):
        for copy in started[len(drained) : len(started) - but]:
            copy.wait_send()
            drained.append(copy)

    m_ref[...] = jnp.full(m_ref.shape, LOWEST, F32)
    acc_ref[...] = jnp.zeros(acc_ref.shape, F32)

    def pair(step):
        return [(z + step) % Z, (z + Z - step) % Z]

    opposite = [(z + 4) % Z]
    p, r = [None, None], [None, None]
    own, far = 0, 1

    def exchange(held, which, following, now):
        previous, held[which] = held[which], following

        def act():
            arrive(previous)
            for copy in following:
                copy.start()

        if now:
            act()
        return act

    def pass_on(a, step, now=True):
        return exchange(p, a, prompt_gather(a, step, False), now)

    def pass_on_resp(which, step, now=True):
        return exchange(r, which, resp_gather(yl if which == own else other, step, False), now)

    def mine_at(slots):
        return [(i, yl) for i in slots]

    def theirs_at(slots):
        return [(i, other) for i in slots]

    present(own_resp)
    turn_values()
    r[own] = own_keys + [
        send(resp.at[z, yl, 1], resp.at[z, yl, 1], peer) for peer in (z_right, z_left)
    ]
    y_far = [send(far_block, resp.at[z, yl], y_id)]
    send_queries(1)
    present([own_q, own_do])
    for a in range(2):
        prepare(q_near, 0, a, q_turned)
    arrive(x0)
    x1 = gather_step(lambda i: xbuf.at[i, c], x, X, 1, x_right, x_left)
    cores += [core_send((x + 1) % X), core_send((x + X - 1) % X)]
    present(own_prompt)
    pass_on_resp(own, 1)
    arrive([y_q[0]])
    prepare(q_far, 1, 0, q_turned)
    last_core = [send(xbuf.at[(x + 2) % X, c], xbuf.at[(x + 2) % X, c], core_id, False)]
    cores += last_core

    def feed_core():
        arrive(x1)
        last_core[0].start()

    absorb(0, mine_at([z] + pair(1)), [], feed_core)
    arrive(y_far)
    r[far] = resp_gather(other, 0)
    for a in range(2):
        prepare(do_near, 0, a, do_turned)
    arrive(cores)
    theirs = owner_ref[prompt_ref[x * 4 + (1 - yh) * 2 + c]]
    mine = owner_ref[prompt_ref[dp]]

    def piece(owner, half, a):
        return xbuf[owner // 4, owner % 2, :, :, head_lanes(half, a)]

    ring = []
    for n, (owner, half, peer) in enumerate(
        ((mine, other, y_id), (theirs, yl, yh_id), (theirs, other, diagonal_id))
    ):
        for a in range(2):
            chosen_out[n, a] = piece(owner, half, a)
        ring.append(send(chosen_out.at[n], chosen_in.at[n], peer))
    pass_on_resp(own, 2)
    absorb(0, mine_at(pair(2)) + theirs_at([z]), [])
    pass_on_resp(far, 1)
    arrive(ring)
    here = (mine // 2) % 2 == yh
    for a in range(2):
        for kv in range(2):
            prompt[a, z, kv, yl] = jnp.where(here, piece(mine, yl, a)[kv], chosen_in[1, a, kv])
            prompt[a, z, kv, other] = jnp.where(here, chosen_in[0, a, kv], chosen_in[2, a, kv])
        p[a] = prompt_gather(a, 0, a == 0)
    y_do = [
        send(do_ref.at[0, :, group_lanes(other, a)], do_far.at[:, a * 1024 : a * 1024 + 1024], y_id)
        for a in range(2)
    ]
    arrive([y_q[1]])
    prepare(q_far, 1, 1, q_turned)
    absorb(1, mine_at([z] + pair(1)), [])
    pass_on_resp(own, 3)
    absorb(1, mine_at(pair(2)) + theirs_at([z]), [])
    pass_on(0, 1)
    for copy in p[1]:
        copy.start()
    absorb(0, mine_at(pair(3)) + theirs_at(pair(1)), [], pass_on_resp(far, 2, False))
    pass_on(0, 2)
    pass_on(1, 1)
    absorb(1, mine_at(pair(3)) + theirs_at(pair(1)), [])
    arrive(r[own])
    near = [z] + pair(1)
    absorb(0, mine_at(opposite) + theirs_at(pair(2)), near, pass_on_resp(far, 3, False))
    pass_on(0, 3)
    pass_on(1, 2)
    absorb(1, mine_at(opposite) + theirs_at(pair(2)), near)
    drain()
    arrive(r[far])
    absorb(0, theirs_at(pair(3) + opposite), pair(2), pass_on(1, 3, False))
    arrive([y_do[0]])
    prepare(do_far, 1, 0, do_turned)
    arrive(p[0])
    absorb(0, [], pair(3) + opposite)
    results = [finish(0)]
    gradients(0, opposite)
    s0 = z_scatter(0, 0)
    absorb(1, theirs_at(pair(3) + opposite), pair(2))
    gradients(0, pair(3))
    arrive(s0)
    s0 = z_scatter(0, 1)
    arrive([y_do[1]])
    prepare(do_far, 1, 1, do_turned)
    arrive(p[1])
    absorb(1, [], pair(3) + opposite)
    results += [finish(1)]
    own_result = fetch(out_near, out_ref.at[0, :, mine_q])
    gradients(1, opposite)
    s1 = z_scatter(1, 0)
    gradients(0, pair(2))
    arrive(s0)
    s0 = z_scatter(0, 2)
    gradients(1, pair(3))
    arrive(s1)
    s1 = z_scatter(1, 1)
    gradients(0, pair(1))
    arrive(s0)
    s0 = z_scatter(0, 3)
    gradients(1, pair(2))
    arrive(s1)
    s1 = z_scatter(1, 2)
    gradients(0, [z])
    arrive(s0)

    t0 = to_y_ring(0)
    gradients(1, pair(1))
    arrive(s1)
    s1 = z_scatter(1, 3)
    arrive(t0)
    t0 = to_core(0)
    gradients(1, [z])
    arrive(t0)
    t0 = x_scatter(0)
    arrive(s1)
    t1 = to_y_ring(1)
    drain(6)
    arrive(t1)
    t1 = to_core(1)
    arrive(t1)
    t1 = x_scatter(1)
    arrive(t0)
    store(0)
    arrive(results)
    present([own_result])
    drain()
    arrive(t1)
    store(1)


COPIES = 96
PIECES = 4


def copy_out(*refs):
    ins, outs, held = refs[:3], refs[3:6], refs[6:9]
    in_sem, out_sem = refs[9:]
    parts = [(0, slice(n * 1024, n * 1024 + 1024)) for n in range(PIECES)]
    parts += [(1, slice(0, 512)), (2, slice(0, 512))]

    def move(sources, targets, sem):
        return [
            pltpu.make_async_copy(sources[n].at[0, :, columns], targets[n].at[0, :, columns], sem.at[i])
            for i, (n, columns) in enumerate(parts)
        ]

    loads, stores = move(ins, held, in_sem), move(held, outs, out_sem)
    for copy in loads:
        copy.start()
    for load, save in zip(loads, stores):
        load.wait()
        save.start()
    for copy in stores:
        copy.wait()


def on_device(*arguments):
    block = (2, 2, PROWS, 128)
    vmem = pl.BlockSpec(memory_space=pltpu.VMEM)
    hbm = pl.BlockSpec(memory_space=pltpu.HBM)
    results = pl.pallas_call(
        kernel,
        out_shape=(
            jax.ShapeDtypeStruct((1, ROWS, 4096), BF),
            jax.ShapeDtypeStruct((1, PROWS, 512), F32),
            jax.ShapeDtypeStruct((1, PROWS, 512), F32),
        ),
        in_specs=[hbm] * 10,
        out_specs=(hbm, vmem, vmem),
        scratch_shapes=[
            pltpu.VMEM((ROWS, HALF_Q), BF),
            pltpu.VMEM((ROWS, HALF_Q), BF),
            pltpu.VMEM((ROWS, HALF_Q), BF),
            pltpu.VMEM((ROWS, HALF_Q), BF),
            pltpu.VMEM((ROWS, HALF_Q), BF),
            pltpu.VMEM((ROWS, HALF_Q), BF),
            pltpu.VMEM((16, 128, 256), BF),
            pltpu.VMEM((16, 128, 256), BF),
            pltpu.VMEM((Z, 2, 2, 2, 128, 128), BF),
            pltpu.VMEM((2, 2, 128, 128), BF),
            pltpu.VMEM((ROWS, 512), BF),
            pltpu.VMEM((X, 2, 2, PROWS, 512), BF),
            pltpu.VMEM((3, 2, 2, PROWS, 128), BF),
            pltpu.VMEM((3, 2, 2, PROWS, 128), BF),
            pltpu.VMEM((2, Z) + block, BF),
            pltpu.VMEM((128, 1024), BF),
            pltpu.VMEM((16, 1, 256), F32),
            pltpu.VMEM((16, 144, 256), F32),
            pltpu.VMEM((16, 1, 256), F32),
            pltpu.VMEM((16, 1, 256), F32),
            pltpu.VMEM((2,) + block, F32),
            pltpu.VMEM((2, 2, 4) + block, BF),
            pltpu.VMEM((2, 2, 4) + block, BF),
            pltpu.VMEM((2, 2, PROWS, 128), BF),
            pltpu.VMEM((2, 2) + block, BF),
            pltpu.VMEM((2, 2) + block, BF),
            pltpu.VMEM((2, 3) + block, BF),
            pltpu.VMEM((2, 3) + block, BF),
            pltpu.SMEM((16,), jnp.int32),
            pltpu.SMEM((16,), jnp.int32),
            pltpu.SMEM((16,), jnp.int32),
            pltpu.SMEM((32,), jnp.int32),
            pltpu.SemaphoreType.DMA((COPIES,)),
            pltpu.SemaphoreType.DMA((COPIES,)),
            pltpu.SemaphoreType.DMA((16,)),
        ],
        compiler_params=pltpu.CompilerParams(
            collective_id=0, has_side_effects=True, vmem_limit_bytes=60 * 1024 * 1024
        ),
        cost_estimate=pl.CostEstimate(
            flops=10_000_000_000, bytes_accessed=8 * 1024 * 1024, transcendentals=17_000_000
        ),
    )(*arguments)
    return pl.pallas_call(
        copy_out,
        out_shape=tuple(jax.ShapeDtypeStruct(r.shape, r.dtype) for r in results),
        in_specs=[pl.BlockSpec(memory_space=pl.ANY)] * 3,
        out_specs=(hbm,) * 3,
        scratch_shapes=[pltpu.VMEM(r.shape, r.dtype) for r in results]
        + [pltpu.SemaphoreType.DMA((PIECES + 2,))] * 2,
        compiler_params=pltpu.CompilerParams(vmem_limit_bytes=60 * 1024 * 1024),
    )(*results)


def solution(mesh):
    split = P("dp", "blk", None)
    return jax.shard_map(
        on_device,
        mesh=mesh,
        in_specs=(split,) * 6 + (P(),) * 4,
        out_specs=(split, split, split),
        check_vma=False,
    )
```

```python
import jax
import jax.numpy as jnp
from jax import lax
from jax.experimental import pallas as pl
from jax.experimental.pallas import tpu as pltpu
from jax.sharding import PartitionSpec as P

MESH = pl.DeviceIdType.MESH
HEAD_WIDTH = 128
SCALE = HEAD_WIDTH ** (-0.5)
LOG2E = 1.4426950408889634
SCORE_SCALE = SCALE * LOG2E
MASKED = -1e30
LOWEST = -1e20
BF = jnp.bfloat16
F32 = jnp.float32

X, YH, CORES, YL, Z = 4, 2, 2, 2, 8
GROUP = 8
ROWS = 128
PROWS = 64
HALF_KV = 256
HALF_Q = 2048


def nt(a, b):
    return lax.dot_general(a, b, (((1,), (1,)), ((), ())), preferred_element_type=F32)


def nn(a, b):
    return lax.dot_general(a, b, (((1,), (0,)), ((), ())), preferred_element_type=F32)


def tn(a, b):
    return lax.dot_general(a, b, (((0,), (0,)), ((), ())), preferred_element_type=F32)


def kernel(
    q_ref, rk_ref, rv_ref, pk_ref, pv_ref, do_ref, owner_hbm, prompt_hbm, length_hbm, half_hbm,
    out_ref, gk_ref, gv_ref,
    q_near, q_far, do_near, do_far, out_near, out_far, q_turned, do_turned,
    resp, far_block, values_in, xbuf, chosen_out, chosen_in, prompt, v_turned,
    m_ref, acc_ref, lse_ref, delta_ref, gacc,
    zs_out, zs_in, share_out, share, core_in, xs_out, xs_in,
    owner_ref, prompt_ref, length_ref, half_ref,
    send_sem, recv_sem, local_sem,
):
    dp = lax.axis_index("dp")
    blk = lax.axis_index("blk")
    x, yh, c = dp // 4, (dp // 2) % 2, dp % 2
    yl, z = blk // Z, blk % Z
    other = 1 - yl
    y_id = (dp, other * Z + z)
    z_right, z_left = (dp, yl * Z + (z + 1) % Z), (dp, yl * Z + (z + Z - 1) % Z)
    z_right2, z_left2 = (dp, yl * Z + (z + 2) % Z), (dp, yl * Z + (z + Z - 2) % Z)
    x_right = (((x + 1) % X) * 4 + yh * 2 + c, blk)
    x_left = (((x + X - 1) % X) * 4 + yh * 2 + c, blk)
    core_id = (x * 4 + yh * 2 + (1 - c), blk)
    yh_id = (x * 4 + (1 - yh) * 2 + c, blk)
    far_x_id = (((x + 2) % X) * 4 + yh * 2 + c, blk)
    diagonal_id = (x * 4 + (1 - yh) * 2 + c, other * Z + z)

    def lanes(which, width):
        return pl.ds(pl.multiple_of(which * width, width), width)

    def head_lanes(half, a):
        return pl.ds(pl.multiple_of(half * HALF_KV + a * 128, 128), 128)

    def group_lanes(half, a):
        return pl.ds(pl.multiple_of(half * HALF_Q + a * 1024, 1024), 1024)

    mine_kv, far_kv = lanes(yl, HALF_KV), lanes(other, HALF_KV)
    mine_q = lanes(yl, HALF_Q)

    fetched = []

    def fetch(src, dst):
        copy = pltpu.make_async_copy(src, dst, local_sem.at[len(fetched)])
        copy.start()
        fetched.append(copy)
        return copy

    def present(copies):
        for copy in copies:
            copy.wait()

    own_prompt = [
        fetch(ref.at[0], xbuf.at[x, c, kv]) for kv, ref in enumerate((pk_ref, pv_ref))
    ]
    own_resp = [fetch(rv_ref.at[0], values_in)]
    own_resp += [
        fetch(rk_ref.at[0, :, head_lanes(half, a)], to.at[0, a])
        for half, to in ((yl, resp.at[z, yl]), (other, far_block))
        for a in range(2)
    ]
    tables = [
        fetch(owner_hbm, owner_ref), fetch(prompt_hbm, prompt_ref),
        fetch(length_hbm, length_ref), fetch(half_hbm, half_ref),
    ]
    own_q = fetch(q_ref.at[0, :, mine_q], q_near)
    own_do = fetch(do_ref.at[0, :, mine_q], do_near)

    barrier = pltpu.get_barrier_semaphore()
    peers = (y_id, z_right, z_left, x_right, x_left, core_id, yh_id, diagonal_id, far_x_id, z_right2, z_left2)
    for peer in peers:
        pl.semaphore_signal(barrier, inc=1, device_id=peer, device_id_type=MESH)
    pl.semaphore_wait(barrier, len(peers))

    started = []

    def send(src, dst, peer, begin=True):
        index = len(started)
        copy = pltpu.make_async_remote_copy(
            src_ref=src, dst_ref=dst, send_sem=send_sem.at[index], recv_sem=recv_sem.at[index],
            device_id=peer, device_id_type=MESH,
        )
        if begin:
            copy.start()
        started.append(copy)
        return copy

    def arrive(copies):
        for copy in copies:
            copy.wait_recv()

    x0 = [
        send(ref.at[0], xbuf.at[x, c, kv], peer)
        for peer in (x_right, x_left)
        for kv, ref in enumerate((pk_ref, pv_ref))
    ]
    y_q = [None, None]

    def send_queries(a):
        near, far = q_ref.at[0, :, group_lanes(other, a)], q_far.at[:, a * 1024 : a * 1024 + 1024]
        y_q[a] = send(near, far, y_id)

    own_keys = [
        send(rk_ref.at[0, :, head_lanes(yl, a)], resp.at[z, yl, 0, a], peer)
        for peer in (z_right, z_left)
        for a in range(2)
    ]
    send_queries(0)
    cores = [
        send(ref.at[0], xbuf.at[x, c, kv], core_id) for kv, ref in enumerate((pk_ref, pv_ref))
    ]

    def gather_step(slot, pos, n, step, right, left, begin=True):
        copies = []
        for way, peer in enumerate((right, left)):
            at = slot((pos + n - step) % n if way == 0 else (pos + step) % n)
            at = at.at[way] if step == n // 2 - 1 else at
            copies.append(send(at, at, peer, begin))
        return copies

    def resp_gather(y, step, begin=True):
        return gather_step(lambda i: resp.at[i, y], z, Z, step, z_right, z_left, begin)

    def prompt_first(a):
        at = prompt.at[a, z]
        return [send(at, at, peer) for peer in (z_right2, z_left2, z_right, z_left)]

    def prompt_second(a, begin):
        copies = []
        for way, (distance, near, far) in enumerate(
            ((Z - 2, z_right, z_right2), (2, z_left, z_left2))
        ):
            at = prompt.at[a, (z + distance) % Z]
            copies += [send(at.at[way], at.at[way], far, begin), send(at, at, near, begin)]
        return copies

    def core_send(i):
        return send(xbuf.at[i, c], xbuf.at[i, c], core_id)

    def head_of(near, far, h):
        columns = pl.ds(pl.multiple_of(h * 128, 128), 128)
        return jnp.concatenate([near[:, columns], far[:, columns]], axis=0)

    def prepare(source, part, a, turned):
        def body(g, carry):
            h = a * GROUP + g
            tile = source[:, pl.ds(pl.multiple_of(h * 128, 128), 128)]
            turned[h, :, part * ROWS : (part + 1) * ROWS] = tile.T
            return carry

        lax.fori_loop(0, GROUP, body, 0, unroll=4)

    def turn_values():
        for half, to in ((yl, resp.at[z, yl]), (other, far_block)):
            for a in range(2):
                to[1, a] = values_in[:, head_lanes(half, a)].T

    present(tables)
    lane = lax.broadcasted_iota(jnp.int32, (1, 2 * ROWS), 1)
    last = length_ref[dp] - 1
    limit = jnp.zeros((1, 2 * ROWS), jnp.int32)
    for part, holder in enumerate((blk, other * Z + z)):
        for e in range(2):
            block = part * 2 + e
            inside = (lane >= block * 64) & (lane < block * 64 + 64)
            limit = jnp.where(inside, half_ref[2 * holder + e] * 64 + lane - block * 64, limit)
    limit = jnp.minimum(limit, last)
    down = lax.broadcasted_iota(jnp.int32, (64, 2 * ROWS), 0)

    def prompt_rows(slots, kv, a):
        return [prompt[a, i, kv].reshape(2 * PROWS, 128) for i in slots]

    def absorb(a, resp_slots, prompt_slots, between=None):
        bounds = []
        for i, y in resp_slots:
            bounds += [limit - half_ref[2 * (y * Z + i) + e] * 64 for e in range(2)]
        bounds += [None] * (2 * len(prompt_slots))
        count = 64 * len(bounds)

        keys = [resp[i, y, 0, a] for i, y in resp_slots] + prompt_rows(prompt_slots, 0, a)
        keys = jnp.concatenate(keys, axis=0)
        for n, part in enumerate(prompt_rows(prompt_slots, 1, a)):
            v_turned[:, n * 128 : n * 128 + 128] = part.T

        def score(query):
            pieces, tops = [], []
            scores = nn(keys, query) * SCORE_SCALE
            for n, bound in enumerate(bounds):
                piece = scores[64 * n : 64 * n + 64]
                if bound is not None:
                    piece = jnp.where(down <= bound, piece, MASKED)
                tops.append(jnp.max(piece.reshape(8, 8, 2 * ROWS), axis=0))
                pieces.append(piece)
            while len(tops) > 1:
                tops = [
                    jnp.maximum(tops[i], tops[i + 1]) if i + 1 < len(tops) else tops[i]
                    for i in range(0, len(tops), 2)
                ]
            return jnp.concatenate(pieces, axis=0), jnp.max(tops[0], axis=0, keepdims=True)

        def body(t, carry):
            first = a * GROUP + t * 4
            heads = pl.ds(first, 4)
            values = [resp[i, y, 1, a] for i, y in resp_slots]
            if prompt_slots:
                values.append(v_turned[:, : 128 * len(prompt_slots)])
            values = jnp.concatenate(values, axis=1) if len(values) > 1 else values[0]
            values = jnp.concatenate([values, jnp.ones((16, count), BF)], axis=0)
            old, old_mixed = m_ref[heads], acc_ref[heads]
            peaks, mixes = [], []

            def weigh(j, scores, top):
                peak = jnp.maximum(old[j], top)
                weights = jnp.exp2(scores - peak).astype(BF)
                peaks.append(peak)
                mixes.append(old_mixed[j] * jnp.exp2(old[j] - peak) + nn(values, weights))

            ready = score(q_turned[first])
            for j in range(4):
                following = score(q_turned[first + j + 1]) if j < 3 else None
                weigh(j, *ready)
                ready = following
            for j in range(4):
                m_ref[first + j] = peaks[j]
                acc_ref[first + j] = mixes[j]
            if between is not None:
                pl.when(t == 0)(between)
            return carry

        lax.fori_loop(0, 2, body, 0)

    def finish(a):
        def body(t, carry):
            first = a * GROUP + t * 4
            heads = pl.ds(first, 4)
            peak, mixed = m_ref[heads], acc_ref[heads]
            outs, logs, deltas = [], [], []
            for j in range(4):
                total = mixed[j, 128:129]
                result = mixed[j, :128] / total
                logs.append(peak[j] + jnp.log(total) * LOG2E)
                cotangent = do_turned[first + j].astype(F32)
                deltas.append(jnp.sum(cotangent * result, axis=0, keepdims=True))
                outs.append(result.T.astype(BF))
            for j in range(4):
                h = first + j
                lse_ref[h] = logs[j]
                delta_ref[h] = deltas[j]
                columns = pl.ds(pl.multiple_of(h * 128, 128), 128)
                out_near[:, columns] = outs[j][:ROWS]
                out_far[:, columns] = outs[j][ROWS:]
            return carry

        lax.fori_loop(0, 2, body, 0)
        return send(
            out_far.at[:, a * 1024 : a * 1024 + 1024], out_ref.at[0, :, group_lanes(yl, a)], y_id
        )

    def gradients(a, slots, place=0):
        keys = jnp.concatenate(prompt_rows(slots, 0, a), axis=0)
        values = jnp.concatenate(prompt_rows(slots, 1, a), axis=0)
        heads = range(a * GROUP, a * GROUP + GROUP)
        queries = [head_of(q_near, q_far, h) for h in heads]
        cotangents = [head_of(do_near, do_far, h) for h in heads]
        all_probs, all_slopes = [], []
        for h in heads:
            probs = jnp.exp2(nn(keys, q_turned[h]) * SCORE_SCALE - lse_ref[h])
            slopes = probs * (nn(values, do_turned[h]) - delta_ref[h])
            all_probs.append(probs.astype(BF))
            all_slopes.append(slopes.astype(BF))
        queries = jnp.concatenate(queries, axis=0)
        cotangents = jnp.concatenate(cotangents, axis=0)
        key_part = nn(jnp.concatenate(all_slopes, axis=1), queries) * SCALE
        value_part = nn(jnp.concatenate(all_probs, axis=1), cotangents)
        for n in range(len(slots)):
            gacc[place + n, 0] = key_part[n * 128 : n * 128 + 128].reshape(2, PROWS, 128)
            gacc[place + n, 1] = value_part[n * 128 : n * 128 + 128].reshape(2, PROWS, 128)

    def z_first(a):
        copies = []
        for way, (near, far) in enumerate(((z_right, z_right2), (z_left, z_left2))):
            zs_out[a, way, 1, way] = gacc[0, way].astype(BF)
            copies.append(send(zs_out.at[a, way, 1, way], zs_in.at[a, way, 1, way], far))
            for h in range(2):
                zs_out[a, way, 0, h] = gacc[1 + way, h].astype(BF)
            copies.append(send(zs_out.at[a, way, 0], zs_in.at[a, way, 0], near))
        return copies

    def z_second(a):
        copies = []
        for way, (near, far) in enumerate(((z_right, z_right2), (z_left, z_left2))):
            for h in range(2):
                part = gacc[3 + way, h] + zs_in[a, way, 0, h].astype(F32)
                if h == way:
                    part = part + zs_in[a, way, 1, h].astype(F32)
                zs_out[a, way, 2, h] = part.astype(BF)
                zs_out[a, way, 3, h] = gacc[5 + way, h].astype(BF)
            copies.append(send(zs_out.at[a, way, 2], zs_in.at[a, way, 2], far))
            copies.append(send(zs_out.at[a, way, 3], zs_in.at[a, way, 3], near))
        return copies

    def to_y_ring(a):
        for h in range(2):
            for n, where in enumerate((yl, other)):
                total = gacc[0, h, where]
                for way in range(2):
                    total = total + zs_in[a, way, 2, h, where].astype(F32)
                    total = total + zs_in[a, way, 3, h, where].astype(F32)
                (share.at[a, 0, 0] if n == 0 else share_out.at[a])[h] = total.astype(BF)
        return [
            send(share_out.at[a], share.at[a, 0, 1], y_id),
            send(share.at[a, 0, 0], share.at[a, 1, 0], yh_id),
            send(share_out.at[a], share.at[a, 1, 1], diagonal_id),
        ]

    def to_core(a):
        return [send(share.at[a], core_in.at[a], core_id)]

    owners = []
    for source_core in (c, 1 - c):
        for source_half in (yh, 1 - yh):
            owners.append(owner_ref[prompt_ref[x * 4 + source_half * 2 + source_core]])

    def destined(a, target, h):
        total = jnp.zeros((2, PROWS, 128), F32)
        for n, owner in enumerate(owners):
            part = (share if n < 2 else core_in)[a, n % 2, :, h].astype(F32)
            total = total + jnp.where(owner == target * 4 + yh * 2 + c, part, 0.0)
        return total

    def x_scatter(a):
        copies = []
        for n, (distance, peer) in enumerate(((2, far_x_id), (1, x_right), (3, x_left))):
            for h in range(2):
                xs_out[a, n, h] = destined(a, (x + distance) % X, h).astype(BF)
            copies.append(send(xs_out.at[a, n], xs_in.at[a, n], peer))
        return copies

    def store(a):
        for h, ref in enumerate((gk_ref, gv_ref)):
            total = destined(a, x, h)
            for n in range(3):
                total = total + xs_in[a, n, h].astype(F32)
            ref[0, :, head_lanes(yl, a)] = total[0]
            ref[0, :, head_lanes(other, a)] = total[1]

    drained = []

    def drain(but=0):
        for copy in started[len(drained) : len(started) - but]:
            copy.wait_send()
            drained.append(copy)

    m_ref[...] = jnp.full(m_ref.shape, LOWEST, F32)
    acc_ref[...] = jnp.zeros(acc_ref.shape, F32)

    def pair(step):
        return [(z + step) % Z, (z + Z - step) % Z]

    opposite = [(z + 4) % Z]
    p, r = [None, None], [None, None]
    own, far = 0, 1

    def exchange(held, which, following, now):
        previous, held[which] = held[which], following

        def act():
            arrive(previous)
            for copy in following:
                copy.start()

        if now:
            act()
        return act

    def pass_on(a, now=True):
        return exchange(p, a, prompt_second(a, False), now)

    def pass_on_resp(which, step, now=True):
        return exchange(r, which, resp_gather(yl if which == own else other, step, False), now)

    def mine_at(slots):
        return [(i, yl) for i in slots]

    def theirs_at(slots):
        return [(i, other) for i in slots]

    present(own_resp)
    turn_values()
    r[own] = own_keys + [
        send(resp.at[z, yl, 1], resp.at[z, yl, 1], peer) for peer in (z_right, z_left)
    ]
    y_far = [send(far_block, resp.at[z, yl], y_id)]
    send_queries(1)
    present([own_q, own_do])
    for a in range(2):
        prepare(q_near, 0, a, q_turned)
    arrive(x0)
    x1 = gather_step(lambda i: xbuf.at[i, c], x, X, 1, x_right, x_left)
    cores += [core_send((x + 1) % X), core_send((x + X - 1) % X)]
    present(own_prompt)
    pass_on_resp(own, 1)
    arrive([y_q[0]])
    prepare(q_far, 1, 0, q_turned)
    last_core = [send(xbuf.at[(x + 2) % X, c], xbuf.at[(x + 2) % X, c], core_id, False)]
    cores += last_core

    def feed_core():
        arrive(x1)
        last_core[0].start()

    absorb(0, mine_at([z] + pair(1)), [], feed_core)
    arrive(y_far)
    r[far] = resp_gather(other, 0)
    for a in range(2):
        prepare(do_near, 0, a, do_turned)
    arrive(cores)
    theirs = owner_ref[prompt_ref[x * 4 + (1 - yh) * 2 + c]]
    mine = owner_ref[prompt_ref[dp]]

    def piece(owner, half, a):
        return xbuf[owner // 4, owner % 2, :, :, head_lanes(half, a)]

    ring = []
    for n, (owner, half, peer) in enumerate(
        ((mine, other, y_id), (theirs, yl, yh_id), (theirs, other, diagonal_id))
    ):
        for a in range(2):
            chosen_out[n, a] = piece(owner, half, a)
        ring.append(send(chosen_out.at[n], chosen_in.at[n], peer))
    pass_on_resp(own, 2)
    absorb(0, mine_at(pair(2)) + theirs_at([z]), [])
    pass_on_resp(far, 1)
    arrive(ring)
    here = (mine // 2) % 2 == yh
    for a in range(2):
        for kv in range(2):
            prompt[a, z, kv, yl] = jnp.where(here, piece(mine, yl, a)[kv], chosen_in[1, a, kv])
            prompt[a, z, kv, other] = jnp.where(here, chosen_in[0, a, kv], chosen_in[2, a, kv])
        p[a] = prompt_first(a)
    y_do = [
        send(do_ref.at[0, :, group_lanes(other, a)], do_far.at[:, a * 1024 : a * 1024 + 1024], y_id)
        for a in range(2)
    ]
    arrive([y_q[1]])
    prepare(q_far, 1, 1, q_turned)
    absorb(1, mine_at([z] + pair(1)), [])
    pass_on_resp(own, 3)
    absorb(1, mine_at(pair(2)) + theirs_at([z]), [])
    absorb(0, mine_at(pair(3)) + theirs_at(pair(1)), [], pass_on_resp(far, 2, False))
    pass_on(0)
    absorb(1, mine_at(pair(3)) + theirs_at(pair(1)), [], pass_on(1, False))
    arrive(r[own])
    near = [z] + pair(1) + pair(2)
    absorb(0, mine_at(opposite) + theirs_at(pair(2)), near, pass_on_resp(far, 3, False))
    absorb(1, mine_at(opposite) + theirs_at(pair(2)), near)
    drain()
    arrive(r[far])
    arrive([y_do[0]])
    prepare(do_far, 1, 0, do_turned)
    arrive(p[0])
    absorb(0, theirs_at(pair(3) + opposite), pair(3) + opposite)
    results = [finish(0)]
    gradients(0, opposite + pair(3))
    s0 = z_first(0)
    arrive([y_do[1]])
    prepare(do_far, 1, 1, do_turned)
    arrive(p[1])
    absorb(1, theirs_at(pair(3) + opposite), pair(3) + opposite)
    results += [finish(1)]
    own_result = fetch(out_near, out_ref.at[0, :, mine_q])
    gradients(1, opposite + pair(3))
    s1 = z_first(1)
    gradients(0, pair(2) + pair(1), 3)
    arrive(s0)
    s0 = z_second(0)
    gradients(1, pair(2) + pair(1), 3)
    arrive(s1)
    s1 = z_second(1)
    gradients(0, [z])
    arrive(s0)

    t0 = to_y_ring(0)
    gradients(1, [z])
    arrive(t0)
    t0 = to_core(0)
    arrive(s1)
    t1 = to_y_ring(1)
    arrive(t0)
    t0 = x_scatter(0)
    drain(6)
    arrive(t1)
    t1 = to_core(1)
    arrive(t1)
    t1 = x_scatter(1)
    arrive(t0)
    store(0)
    arrive(results)
    present([own_result])
    drain()
    arrive(t1)
    store(1)


COPIES = 96
PIECES = 4


def copy_out(*refs):
    ins, outs, held = refs[:3], refs[3:6], refs[6:9]
    in_sem, out_sem = refs[9:]
    parts = [(0, slice(n * 1024, n * 1024 + 1024)) for n in range(PIECES)]
    parts += [(1, slice(0, 512)), (2, slice(0, 512))]

    def move(sources, targets, sem):
        return [
            pltpu.make_async_copy(sources[n].at[0, :, columns], targets[n].at[0, :, columns], sem.at[i])
            for i, (n, columns) in enumerate(parts)
        ]

    loads, stores = move(ins, held, in_sem), move(held, outs, out_sem)
    for copy in loads:
        copy.start()
    for load, save in zip(loads, stores):
        load.wait()
        save.start()
    for copy in stores:
        copy.wait()


def on_device(*arguments):
    block = (2, 2, PROWS, 128)
    vmem = pl.BlockSpec(memory_space=pltpu.VMEM)
    hbm = pl.BlockSpec(memory_space=pltpu.HBM)
    results = pl.pallas_call(
        kernel,
        out_shape=(
            jax.ShapeDtypeStruct((1, ROWS, 4096), BF),
            jax.ShapeDtypeStruct((1, PROWS, 512), F32),
            jax.ShapeDtypeStruct((1, PROWS, 512), F32),
        ),
        in_specs=[hbm] * 10,
        out_specs=(hbm, vmem, vmem),
        scratch_shapes=[
            pltpu.VMEM((ROWS, HALF_Q), BF),
            pltpu.VMEM((ROWS, HALF_Q), BF),
            pltpu.VMEM((ROWS, HALF_Q), BF),
            pltpu.VMEM((ROWS, HALF_Q), BF),
            pltpu.VMEM((ROWS, HALF_Q), BF),
            pltpu.VMEM((ROWS, HALF_Q), BF),
            pltpu.VMEM((16, 128, 256), BF),
            pltpu.VMEM((16, 128, 256), BF),
            pltpu.VMEM((Z, 2, 2, 2, 128, 128), BF),
            pltpu.VMEM((2, 2, 128, 128), BF),
            pltpu.VMEM((ROWS, 512), BF),
            pltpu.VMEM((X, 2, 2, PROWS, 512), BF),
            pltpu.VMEM((3, 2, 2, PROWS, 128), BF),
            pltpu.VMEM((3, 2, 2, PROWS, 128), BF),
            pltpu.VMEM((2, Z) + block, BF),
            pltpu.VMEM((128, 1024), BF),
            pltpu.VMEM((16, 1, 256), F32),
            pltpu.VMEM((16, 144, 256), F32),
            pltpu.VMEM((16, 1, 256), F32),
            pltpu.VMEM((16, 1, 256), F32),
            pltpu.VMEM((7,) + block, F32),
            pltpu.VMEM((2, 2, 4) + block, BF),
            pltpu.VMEM((2, 2, 4) + block, BF),
            pltpu.VMEM((2, 2, PROWS, 128), BF),
            pltpu.VMEM((2, 2) + block, BF),
            pltpu.VMEM((2, 2) + block, BF),
            pltpu.VMEM((2, 3) + block, BF),
            pltpu.VMEM((2, 3) + block, BF),
            pltpu.SMEM((16,), jnp.int32),
            pltpu.SMEM((16,), jnp.int32),
            pltpu.SMEM((16,), jnp.int32),
            pltpu.SMEM((32,), jnp.int32),
            pltpu.SemaphoreType.DMA((COPIES,)),
            pltpu.SemaphoreType.DMA((COPIES,)),
            pltpu.SemaphoreType.DMA((16,)),
        ],
        compiler_params=pltpu.CompilerParams(
            collective_id=0, has_side_effects=True, vmem_limit_bytes=60 * 1024 * 1024
        ),
        cost_estimate=pl.CostEstimate(
            flops=10_000_000_000, bytes_accessed=8 * 1024 * 1024, transcendentals=17_000_000
        ),
    )(*arguments)
    return pl.pallas_call(
        copy_out,
        out_shape=tuple(jax.ShapeDtypeStruct(r.shape, r.dtype) for r in results),
        in_specs=[pl.BlockSpec(memory_space=pl.ANY)] * 3,
        out_specs=(hbm,) * 3,
        scratch_shapes=[pltpu.VMEM(r.shape, r.dtype) for r in results]
        + [pltpu.SemaphoreType.DMA((PIECES + 2,))] * 2,
        compiler_params=pltpu.CompilerParams(vmem_limit_bytes=60 * 1024 * 1024),
    )(*results)


def solution(mesh):
    split = P("dp", "blk", None)
    return jax.shard_map(
        on_device,
        mesh=mesh,
        in_specs=(split,) * 6 + (P(),) * 4,
        out_specs=(split, split, split),
        check_vma=False,
    )
```

```python
import jax
import jax.numpy as jnp
from jax import lax
from jax.experimental import pallas as pl
from jax.experimental.pallas import tpu as pltpu
from jax.sharding import PartitionSpec as P

MESH = pl.DeviceIdType.MESH
HEAD_WIDTH = 128
SCALE = HEAD_WIDTH ** (-0.5)
LOG2E = 1.4426950408889634
SCORE_SCALE = SCALE * LOG2E
MASKED = -1e30
LOWEST = -1e20
BF = jnp.bfloat16
F32 = jnp.float32

X, YH, CORES, YL, Z = 4, 2, 2, 2, 8
GROUP = 8
ROWS = 128
PROWS = 64
HALF_KV = 256
HALF_Q = 2048


def nt(a, b):
    return lax.dot_general(a, b, (((1,), (1,)), ((), ())), preferred_element_type=F32)


def nn(a, b):
    return lax.dot_general(a, b, (((1,), (0,)), ((), ())), preferred_element_type=F32)


def tn(a, b):
    return lax.dot_general(a, b, (((0,), (0,)), ((), ())), preferred_element_type=F32)


def kernel(
    q_ref, rk_ref, rv_ref, pk_ref, pv_ref, do_ref, owner_hbm, prompt_hbm, length_hbm, half_hbm,
    out_ref, gk_ref, gv_ref,
    q_near, q_far, do_near, do_far, out_near, out_far, q_turned, do_turned,
    resp, far_block, values_in, xbuf, chosen_out, chosen_in, prompt, v_turned,
    m_ref, acc_ref, lse_ref, delta_ref, gacc,
    zs_out, zs_in, share_out, share, core_in, xs_out, xs_in,
    owner_ref, prompt_ref, length_ref, half_ref,
    send_sem, recv_sem, local_sem,
):
    dp = lax.axis_index("dp")
    blk = lax.axis_index("blk")
    x, yh, c = dp // 4, (dp // 2) % 2, dp % 2
    yl, z = blk // Z, blk % Z
    other = 1 - yl
    y_id = (dp, other * Z + z)
    z_right, z_left = (dp, yl * Z + (z + 1) % Z), (dp, yl * Z + (z + Z - 1) % Z)
    z_right2, z_left2 = (dp, yl * Z + (z + 2) % Z), (dp, yl * Z + (z + Z - 2) % Z)
    x_right = (((x + 1) % X) * 4 + yh * 2 + c, blk)
    x_left = (((x + X - 1) % X) * 4 + yh * 2 + c, blk)
    core_id = (x * 4 + yh * 2 + (1 - c), blk)
    yh_id = (x * 4 + (1 - yh) * 2 + c, blk)
    far_x_id = (((x + 2) % X) * 4 + yh * 2 + c, blk)
    diagonal_id = (x * 4 + (1 - yh) * 2 + c, other * Z + z)

    def lanes(which, width):
        return pl.ds(pl.multiple_of(which * width, width), width)

    def head_lanes(half, a):
        return pl.ds(pl.multiple_of(half * HALF_KV + a * 128, 128), 128)

    def group_lanes(half, a):
        return pl.ds(pl.multiple_of(half * HALF_Q + a * 1024, 1024), 1024)

    mine_kv, far_kv = lanes(yl, HALF_KV), lanes(other, HALF_KV)
    mine_q = lanes(yl, HALF_Q)

    fetched = []

    def fetch(src, dst):
        copy = pltpu.make_async_copy(src, dst, local_sem.at[len(fetched)])
        copy.start()
        fetched.append(copy)
        return copy

    def present(copies):
        for copy in copies:
            copy.wait()

    own_prompt = [
        fetch(ref.at[0], xbuf.at[x, c, kv]) for kv, ref in enumerate((pk_ref, pv_ref))
    ]
    own_resp = [fetch(rv_ref.at[0], values_in)]
    own_resp += [
        fetch(rk_ref.at[0, :, head_lanes(half, a)], to.at[0, a])
        for half, to in ((yl, resp.at[z, yl]), (other, far_block))
        for a in range(2)
    ]
    tables = [
        fetch(owner_hbm, owner_ref), fetch(prompt_hbm, prompt_ref),
        fetch(length_hbm, length_ref), fetch(half_hbm, half_ref),
    ]
    own_q = fetch(q_ref.at[0, :, mine_q], q_near)
    own_do = fetch(do_ref.at[0, :, mine_q], do_near)

    barrier = pltpu.get_barrier_semaphore()
    peers = (y_id, z_right, z_left, x_right, x_left, core_id, yh_id, diagonal_id, far_x_id, z_right2, z_left2)
    for peer in peers:
        pl.semaphore_signal(barrier, inc=1, device_id=peer, device_id_type=MESH)
    pl.semaphore_wait(barrier, len(peers))

    started = []

    def send(src, dst, peer, begin=True):
        index = len(started)
        copy = pltpu.make_async_remote_copy(
            src_ref=src, dst_ref=dst, send_sem=send_sem.at[index], recv_sem=recv_sem.at[index],
            device_id=peer, device_id_type=MESH,
        )
        if begin:
            copy.start()
        started.append(copy)
        return copy

    def arrive(copies):
        for copy in copies:
            copy.wait_recv()

    x0 = [
        send(ref.at[0], xbuf.at[x, c, kv], peer)
        for peer in (x_right, x_left)
        for kv, ref in enumerate((pk_ref, pv_ref))
    ]
    y_q = [None, None]

    def send_queries(a):
        near, far = q_ref.at[0, :, group_lanes(other, a)], q_far.at[:, a * 1024 : a * 1024 + 1024]
        y_q[a] = send(near, far, y_id)

    own_keys = [
        send(rk_ref.at[0, :, head_lanes(yl, a)], resp.at[z, yl, 0, a], peer)
        for peer in (z_right, z_left)
        for a in range(2)
    ]
    send_queries(0)
    cores = [
        send(ref.at[0], xbuf.at[x, c, kv], core_id) for kv, ref in enumerate((pk_ref, pv_ref))
    ]

    def gather_step(slot, pos, n, step, right, left, begin=True):
        copies = []
        for way, peer in enumerate((right, left)):
            at = slot((pos + n - step) % n if way == 0 else (pos + step) % n)
            at = at.at[way] if step == n // 2 - 1 else at
            copies.append(send(at, at, peer, begin))
        return copies

    def resp_gather(y, step, begin=True):
        return gather_step(lambda i: resp.at[i, y], z, Z, step, z_right, z_left, begin)

    def prompt_gather(a, step, begin=True):
        return gather_step(lambda i: prompt.at[a, i], z, Z, step, z_right, z_left, begin)

    def core_send(i):
        return send(xbuf.at[i, c], xbuf.at[i, c], core_id)

    def head_of(near, far, h):
        columns = pl.ds(pl.multiple_of(h * 128, 128), 128)
        return jnp.concatenate([near[:, columns], far[:, columns]], axis=0)

    def prepare(source, part, a, turned):
        def body(g, carry):
            h = a * GROUP + g
            tile = source[:, pl.ds(pl.multiple_of(h * 128, 128), 128)]
            turned[h, :, part * ROWS : (part + 1) * ROWS] = tile.T
            return carry

        lax.fori_loop(0, GROUP, body, 0, unroll=4)

    def turn_values():
        for half, to in ((yl, resp.at[z, yl]), (other, far_block)):
            for a in range(2):
                to[1, a] = values_in[:, head_lanes(half, a)].T

    present(tables)
    lane = lax.broadcasted_iota(jnp.int32, (1, 2 * ROWS), 1)
    last = length_ref[dp] - 1
    limit = jnp.zeros((1, 2 * ROWS), jnp.int32)
    for part, holder in enumerate((blk, other * Z + z)):
        for e in range(2):
            block = part * 2 + e
            inside = (lane >= block * 64) & (lane < block * 64 + 64)
            limit = jnp.where(inside, half_ref[2 * holder + e] * 64 + lane - block * 64, limit)
    limit = jnp.minimum(limit, last)
    down = lax.broadcasted_iota(jnp.int32, (64, 2 * ROWS), 0)

    def prompt_rows(slots, kv, a):
        return [prompt[a, i, kv].reshape(2 * PROWS, 128) for i in slots]

    def absorb(a, resp_slots, prompt_slots, between=None):
        bounds = []
        for i, y in resp_slots:
            bounds += [limit - half_ref[2 * (y * Z + i) + e] * 64 for e in range(2)]
        bounds += [None] * (2 * len(prompt_slots))
        count = 64 * len(bounds)

        keys = [resp[i, y, 0, a] for i, y in resp_slots] + prompt_rows(prompt_slots, 0, a)
        keys = jnp.concatenate(keys, axis=0)
        for n, part in enumerate(prompt_rows(prompt_slots, 1, a)):
            v_turned[:, n * 128 : n * 128 + 128] = part.T

        def score(query):
            pieces, tops = [], []
            scores = nn(keys, query) * SCORE_SCALE
            for n, bound in enumerate(bounds):
                piece = scores[64 * n : 64 * n + 64]
                if bound is not None:
                    piece = jnp.where(down <= bound, piece, MASKED)
                tops.append(jnp.max(piece.reshape(8, 8, 2 * ROWS), axis=0))
                pieces.append(piece)
            while len(tops) > 1:
                tops = [
                    jnp.maximum(tops[i], tops[i + 1]) if i + 1 < len(tops) else tops[i]
                    for i in range(0, len(tops), 2)
                ]
            return jnp.concatenate(pieces, axis=0), jnp.max(tops[0], axis=0, keepdims=True)

        def body(t, carry):
            first = a * GROUP + t * 4
            heads = pl.ds(first, 4)
            values = [resp[i, y, 1, a] for i, y in resp_slots]
            if prompt_slots:
                values.append(v_turned[:, : 128 * len(prompt_slots)])
            values = jnp.concatenate(values, axis=1) if len(values) > 1 else values[0]
            values = jnp.concatenate([values, jnp.ones((16, count), BF)], axis=0)
            old, old_mixed = m_ref[heads], acc_ref[heads]
            peaks, mixes = [], []

            def weigh(j, scores, top):
                peak = jnp.maximum(old[j], top)
                weights = jnp.exp2(scores - peak).astype(BF)
                peaks.append(peak)
                mixes.append(old_mixed[j] * jnp.exp2(old[j] - peak) + nn(values, weights))

            ready = score(q_turned[first])
            for j in range(4):
                following = score(q_turned[first + j + 1]) if j < 3 else None
                weigh(j, *ready)
                ready = following
            for j in range(4):
                m_ref[first + j] = peaks[j]
                acc_ref[first + j] = mixes[j]
            if between is not None:
                pl.when(t == 0)(between)
            return carry

        lax.fori_loop(0, 2, body, 0)

    def finish(a):
        def body(t, carry):
            first = a * GROUP + t * 4
            heads = pl.ds(first, 4)
            peak, mixed = m_ref[heads], acc_ref[heads]
            outs, logs, deltas = [], [], []
            for j in range(4):
                total = mixed[j, 128:129]
                result = mixed[j, :128] / total
                logs.append(peak[j] + jnp.log(total) * LOG2E)
                cotangent = do_turned[first + j].astype(F32)
                deltas.append(jnp.sum(cotangent * result, axis=0, keepdims=True))
                outs.append(result.T.astype(BF))
            for j in range(4):
                h = first + j
                lse_ref[h] = logs[j]
                delta_ref[h] = deltas[j]
                columns = pl.ds(pl.multiple_of(h * 128, 128), 128)
                out_near[:, columns] = outs[j][:ROWS]
                out_far[:, columns] = outs[j][ROWS:]
            return carry

        lax.fori_loop(0, 2, body, 0)
        return send(
            out_far.at[:, a * 1024 : a * 1024 + 1024], out_ref.at[0, :, group_lanes(yl, a)], y_id
        )

    def gradients(a, slots, place=0):
        keys = jnp.concatenate(prompt_rows(slots, 0, a), axis=0)
        values = jnp.concatenate(prompt_rows(slots, 1, a), axis=0)
        heads = range(a * GROUP, a * GROUP + GROUP)
        queries = [head_of(q_near, q_far, h) for h in heads]
        cotangents = [head_of(do_near, do_far, h) for h in heads]
        all_probs, all_slopes = [], []
        for h in heads:
            probs = jnp.exp2(nn(keys, q_turned[h]) * SCORE_SCALE - lse_ref[h])
            slopes = probs * (nn(values, do_turned[h]) - delta_ref[h])
            all_probs.append(probs.astype(BF))
            all_slopes.append(slopes.astype(BF))
        queries = jnp.concatenate(queries, axis=0)
        cotangents = jnp.concatenate(cotangents, axis=0)
        key_part = nn(jnp.concatenate(all_slopes, axis=1), queries) * SCALE
        value_part = nn(jnp.concatenate(all_probs, axis=1), cotangents)
        for n in range(len(slots)):
            gacc[place + n, 0] = key_part[n * 128 : n * 128 + 128].reshape(2, PROWS, 128)
            gacc[place + n, 1] = value_part[n * 128 : n * 128 + 128].reshape(2, PROWS, 128)

    def z_first(a):
        copies = []
        for way, (near, far) in enumerate(((z_right, z_right2), (z_left, z_left2))):
            zs_out[a, way, 1, way] = gacc[0, way].astype(BF)
            copies.append(send(zs_out.at[a, way, 1, way], zs_in.at[a, way, 1, way], far))
            for h in range(2):
                zs_out[a, way, 0, h] = gacc[1 + way, h].astype(BF)
            copies.append(send(zs_out.at[a, way, 0], zs_in.at[a, way, 0], near))
        return copies

    def z_second(a):
        copies = []
        for way, (near, far) in enumerate(((z_right, z_right2), (z_left, z_left2))):
            for h in range(2):
                part = gacc[3 + way, h] + zs_in[a, way, 0, h].astype(F32)
                if h == way:
                    part = part + zs_in[a, way, 1, h].astype(F32)
                zs_out[a, way, 2, h] = part.astype(BF)
                zs_out[a, way, 3, h] = gacc[5 + way, h].astype(BF)
            copies.append(send(zs_out.at[a, way, 2], zs_in.at[a, way, 2], far))
            copies.append(send(zs_out.at[a, way, 3], zs_in.at[a, way, 3], near))
        return copies

    def to_y_ring(a):
        for h in range(2):
            for n, where in enumerate((yl, other)):
                total = gacc[0, h, where]
                for way in range(2):
                    total = total + zs_in[a, way, 2, h, where].astype(F32)
                    total = total + zs_in[a, way, 3, h, where].astype(F32)
                (share.at[a, 0, 0] if n == 0 else share_out.at[a])[h] = total.astype(BF)
        return [
            send(share_out.at[a], share.at[a, 0, 1], y_id),
            send(share.at[a, 0, 0], share.at[a, 1, 0], yh_id),
            send(share_out.at[a], share.at[a, 1, 1], diagonal_id),
        ]

    def to_core(a):
        return [send(share.at[a], core_in.at[a], core_id)]

    owners = []
    for source_core in (c, 1 - c):
        for source_half in (yh, 1 - yh):
            owners.append(owner_ref[prompt_ref[x * 4 + source_half * 2 + source_core]])

    def destined(a, target, h):
        total = jnp.zeros((2, PROWS, 128), F32)
        for n, owner in enumerate(owners):
            part = (share if n < 2 else core_in)[a, n % 2, :, h].astype(F32)
            total = total + jnp.where(owner == target * 4 + yh * 2 + c, part, 0.0)
        return total

    def x_scatter(a):
        copies = []
        for n, (distance, peer) in enumerate(((2, far_x_id), (1, x_right), (3, x_left))):
            for h in range(2):
                xs_out[a, n, h] = destined(a, (x + distance) % X, h).astype(BF)
            copies.append(send(xs_out.at[a, n], xs_in.at[a, n], peer))
        return copies

    def store(a):
        for h, ref in enumerate((gk_ref, gv_ref)):
            total = destined(a, x, h)
            for n in range(3):
                total = total + xs_in[a, n, h].astype(F32)
            ref[0, :, head_lanes(yl, a)] = total[0]
            ref[0, :, head_lanes(other, a)] = total[1]

    drained = []

    def drain(but=0):
        for copy in started[len(drained) : len(started) - but]:
            copy.wait_send()
            drained.append(copy)

    m_ref[...] = jnp.full(m_ref.shape, LOWEST, F32)
    acc_ref[...] = jnp.zeros(acc_ref.shape, F32)

    def pair(step):
        return [(z + step) % Z, (z + Z - step) % Z]

    opposite = [(z + 4) % Z]
    p, r = [None, None], [None, None]
    own, far = 0, 1

    def exchange(held, which, following, now):
        previous, held[which] = held[which], following

        def act():
            arrive(previous)
            for copy in following:
                copy.start()

        if now:
            act()
        return act

    def pass_on(a, step, now=True):
        return exchange(p, a, prompt_gather(a, step, False), now)

    def pass_on_resp(which, step, now=True):
        return exchange(r, which, resp_gather(yl if which == own else other, step, False), now)

    def mine_at(slots):
        return [(i, yl) for i in slots]

    def theirs_at(slots):
        return [(i, other) for i in slots]

    present(own_resp)
    turn_values()
    r[own] = own_keys + [
        send(resp.at[z, yl, 1], resp.at[z, yl, 1], peer) for peer in (z_right, z_left)
    ]
    y_far = [send(far_block, resp.at[z, yl], y_id)]
    send_queries(1)
    present([own_q, own_do])
    for a in range(2):
        prepare(q_near, 0, a, q_turned)
    arrive(x0)
    x1 = gather_step(lambda i: xbuf.at[i, c], x, X, 1, x_right, x_left)
    cores += [core_send((x + 1) % X), core_send((x + X - 1) % X)]
    present(own_prompt)
    pass_on_resp(own, 1)
    arrive([y_q[0]])
    prepare(q_far, 1, 0, q_turned)
    last_core = [send(xbuf.at[(x + 2) % X, c], xbuf.at[(x + 2) % X, c], core_id, False)]
    cores += last_core

    def feed_core():
        arrive(x1)
        last_core[0].start()

    absorb(0, mine_at([z] + pair(1)), [], feed_core)
    arrive(y_far)
    r[far] = resp_gather(other, 0)
    for a in range(2):
        prepare(do_near, 0, a, do_turned)
    arrive(cores)
    theirs = owner_ref[prompt_ref[x * 4 + (1 - yh) * 2 + c]]
    mine = owner_ref[prompt_ref[dp]]

    def piece(owner, half, a):
        return xbuf[owner // 4, owner % 2, :, :, head_lanes(half, a)]

    ring = []
    for n, (owner, half, peer) in enumerate(
        ((mine, other, y_id), (theirs, yl, yh_id), (theirs, other, diagonal_id))
    ):
        for a in range(2):
            chosen_out[n, a] = piece(owner, half, a)
        ring.append(send(chosen_out.at[n], chosen_in.at[n], peer))
    pass_on_resp(own, 2)
    absorb(0, mine_at(pair(2)) + theirs_at([z]), [])
    pass_on_resp(far, 1)
    arrive(ring)
    here = (mine // 2) % 2 == yh
    for a in range(2):
        for kv in range(2):
            prompt[a, z, kv, yl] = jnp.where(here, piece(mine, yl, a)[kv], chosen_in[1, a, kv])
            prompt[a, z, kv, other] = jnp.where(here, chosen_in[0, a, kv], chosen_in[2, a, kv])
        p[a] = prompt_gather(a, 0, a == 0)
    y_do = [
        send(do_ref.at[0, :, group_lanes(other, a)], do_far.at[:, a * 1024 : a * 1024 + 1024], y_id)
        for a in range(2)
    ]
    arrive([y_q[1]])
    prepare(q_far, 1, 1, q_turned)
    absorb(1, mine_at([z] + pair(1)), [])
    pass_on_resp(own, 3)
    absorb(1, mine_at(pair(2)) + theirs_at([z]), [])
    pass_on(0, 1)
    for copy in p[1]:
        copy.start()
    absorb(0, mine_at(pair(3)) + theirs_at(pair(1)), [], pass_on_resp(far, 2, False))
    pass_on(0, 2)
    pass_on(1, 1)
    absorb(1, mine_at(pair(3)) + theirs_at(pair(1)), [])
    arrive(r[own])
    near = [z] + pair(1)
    absorb(0, mine_at(opposite) + theirs_at(pair(2)), near, pass_on_resp(far, 3, False))
    pass_on(0, 3)
    pass_on(1, 2)
    absorb(1, mine_at(opposite) + theirs_at(pair(2)), near)
    drain()
    arrive(r[far])
    absorb(0, theirs_at(pair(3) + opposite), pair(2), pass_on(1, 3, False))
    arrive([y_do[0]])
    prepare(do_far, 1, 0, do_turned)
    arrive(p[0])
    absorb(0, [], pair(3) + opposite)
    results = [finish(0)]
    gradients(0, opposite + pair(3))
    s0 = z_first(0)
    absorb(1, theirs_at(pair(3) + opposite), pair(2))
    arrive([y_do[1]])
    prepare(do_far, 1, 1, do_turned)
    arrive(p[1])
    absorb(1, [], pair(3) + opposite)
    results += [finish(1)]
    own_result = fetch(out_near, out_ref.at[0, :, mine_q])
    gradients(1, opposite + pair(3))
    s1 = z_first(1)
    gradients(0, pair(2) + pair(1), 3)
    arrive(s0)
    s0 = z_second(0)
    gradients(1, pair(2) + pair(1), 3)
    arrive(s1)
    s1 = z_second(1)
    gradients(0, [z])
    arrive(s0)

    t0 = to_y_ring(0)
    gradients(1, [z])
    arrive(t0)
    t0 = to_core(0)
    arrive(s1)
    t1 = to_y_ring(1)
    arrive(t0)
    t0 = x_scatter(0)
    drain(6)
    arrive(t1)
    t1 = to_core(1)
    arrive(t1)
    t1 = x_scatter(1)
    arrive(t0)
    store(0)
    arrive(results)
    present([own_result])
    drain()
    arrive(t1)
    store(1)


COPIES = 96
PIECES = 4


def copy_out(*refs):
    ins, outs, held = refs[:3], refs[3:6], refs[6:9]
    in_sem, out_sem = refs[9:]
    parts = [(0, slice(n * 1024, n * 1024 + 1024)) for n in range(PIECES)]
    parts += [(1, slice(0, 512)), (2, slice(0, 512))]

    def move(sources, targets, sem):
        return [
            pltpu.make_async_copy(sources[n].at[0, :, columns], targets[n].at[0, :, columns], sem.at[i])
            for i, (n, columns) in enumerate(parts)
        ]

    loads, stores = move(ins, held, in_sem), move(held, outs, out_sem)
    for copy in loads:
        copy.start()
    for load, save in zip(loads, stores):
        load.wait()
        save.start()
    for copy in stores:
        copy.wait()


def on_device(*arguments):
    block = (2, 2, PROWS, 128)
    vmem = pl.BlockSpec(memory_space=pltpu.VMEM)
    hbm = pl.BlockSpec(memory_space=pltpu.HBM)
    results = pl.pallas_call(
        kernel,
        out_shape=(
            jax.ShapeDtypeStruct((1, ROWS, 4096), BF),
            jax.ShapeDtypeStruct((1, PROWS, 512), F32),
            jax.ShapeDtypeStruct((1, PROWS, 512), F32),
        ),
        in_specs=[hbm] * 10,
        out_specs=(hbm, vmem, vmem),
        scratch_shapes=[
            pltpu.VMEM((ROWS, HALF_Q), BF),
            pltpu.VMEM((ROWS, HALF_Q), BF),
            pltpu.VMEM((ROWS, HALF_Q), BF),
            pltpu.VMEM((ROWS, HALF_Q), BF),
            pltpu.VMEM((ROWS, HALF_Q), BF),
            pltpu.VMEM((ROWS, HALF_Q), BF),
            pltpu.VMEM((16, 128, 256), BF),
            pltpu.VMEM((16, 128, 256), BF),
            pltpu.VMEM((Z, 2, 2, 2, 128, 128), BF),
            pltpu.VMEM((2, 2, 128, 128), BF),
            pltpu.VMEM((ROWS, 512), BF),
            pltpu.VMEM((X, 2, 2, PROWS, 512), BF),
            pltpu.VMEM((3, 2, 2, PROWS, 128), BF),
            pltpu.VMEM((3, 2, 2, PROWS, 128), BF),
            pltpu.VMEM((2, Z) + block, BF),
            pltpu.VMEM((128, 1024), BF),
            pltpu.VMEM((16, 1, 256), F32),
            pltpu.VMEM((16, 144, 256), F32),
            pltpu.VMEM((16, 1, 256), F32),
            pltpu.VMEM((16, 1, 256), F32),
            pltpu.VMEM((7,) + block, F32),
            pltpu.VMEM((2, 2, 4) + block, BF),
            pltpu.VMEM((2, 2, 4) + block, BF),
            pltpu.VMEM((2, 2, PROWS, 128), BF),
            pltpu.VMEM((2, 2) + block, BF),
            pltpu.VMEM((2, 2) + block, BF),
            pltpu.VMEM((2, 3) + block, BF),
            pltpu.VMEM((2, 3) + block, BF),
            pltpu.SMEM((16,), jnp.int32),
            pltpu.SMEM((16,), jnp.int32),
            pltpu.SMEM((16,), jnp.int32),
            pltpu.SMEM((32,), jnp.int32),
            pltpu.SemaphoreType.DMA((COPIES,)),
            pltpu.SemaphoreType.DMA((COPIES,)),
            pltpu.SemaphoreType.DMA((16,)),
        ],
        compiler_params=pltpu.CompilerParams(
            collective_id=0, has_side_effects=True, vmem_limit_bytes=60 * 1024 * 1024
        ),
        cost_estimate=pl.CostEstimate(
            flops=10_000_000_000, bytes_accessed=8 * 1024 * 1024, transcendentals=17_000_000
        ),
    )(*arguments)
    return pl.pallas_call(
        copy_out,
        out_shape=tuple(jax.ShapeDtypeStruct(r.shape, r.dtype) for r in results),
        in_specs=[pl.BlockSpec(memory_space=pl.ANY)] * 3,
        out_specs=(hbm,) * 3,
        scratch_shapes=[pltpu.VMEM(r.shape, r.dtype) for r in results]
        + [pltpu.SemaphoreType.DMA((PIECES + 2,))] * 2,
        compiler_params=pltpu.CompilerParams(vmem_limit_bytes=60 * 1024 * 1024),
    )(*results)


def solution(mesh):
    split = P("dp", "blk", None)
    return jax.shard_map(
        on_device,
        mesh=mesh,
        in_specs=(split,) * 6 + (P(),) * 4,
        out_specs=(split, split, split),
        check_vma=False,
    )
```
